32 devices in a mesh: dp: 4 (over y, core), blk: 8 (over z, x).
Axes of the slice: x: 2, y: 2, z: 4, core: 2. Of those that a mesh axis runs over, the one named last changes fastest.
Arguments:
- counts: int32 [8, 512, 1024], P('dp', 'blk'), may hold values from 0 to 15
- coords: int32 [2, 8, 512], P(None, 'dp', 'blk'), may hold values from 0 to 1023
- segment_ids: int32 [8, 512], P('dp', 'blk'), may hold values from 0 to 511, as said below
- logit_grad: bfloat16 [8, 512, 1024], P('dp', 'blk'), may hold values from -5 to 5
- enc_weight: bfloat16 [1024, 1024], P('blk'), may hold values from -0.09375 to 0.09375
- qkv_weight: bfloat16 [1024, 3072], P('blk'), may hold values from -0.1875 to 0.1875
- out_weight: bfloat16 [1024, 1024], P('blk'), may hold values from -0.75 to 0.75
- up_weight: bfloat16 [1024, 4096], P('blk'), may hold values from -0.1875 to 0.1875
- down_weight: bfloat16 [4096, 1024], P('blk'), may hold values from -0.09375 to 0.09375
- dec_weight: bfloat16 [1024, 1024], P('blk'), may hold values from -0.1875 to 0.1875
- dec_bias: bfloat16 [1024], P('blk'), may hold values from -4 to 4
- norm1_gain: bfloat16 [1024], P('blk'), may hold values from 0.5 to 1.5
- norm1_shift: bfloat16 [1024], P('blk'), may hold values from -3 to 3
- norm2_gain: bfloat16 [1024], P('blk'), may hold values from 0.5 to 1.5
- norm2_shift: bfloat16 [1024], P('blk'), may hold values from -3 to 3
Outputs:
- logits: bfloat16 [8, 512, 1024], P('dp', 'blk')
- input_grad: bfloat16 [8, 512, 1024], P('dp', 'blk')
- grad_enc_weight: float32 [1024, 1024], P('blk')
- grad_qkv_weight: float32 [1024, 3072], P('blk')
- grad_out_weight: float32 [1024, 1024], P('blk')
- grad_up_weight: float32 [1024, 4096], P('blk')
- grad_down_weight: float32 [4096, 1024], P('blk')
- grad_dec_weight: float32 [1024, 1024], P('blk')
- grad_dec_bias: float32 [1024], P('blk')
- grad_norm1_gain: float32 [1024], P('blk')
- grad_norm1_shift: float32 [1024], P('blk')
- grad_norm2_gain: float32 [1024], P('blk')
- grad_norm2_shift: float32 [1024], P('blk')
The draws below stay inside these ranges and needn't reach their ends.
Inputs may be any that keep to these rules, and one draw needn't show every extreme that they name: `segment_ids`: Non-decreasing along each sequence; in each group of 2 sequences on one index of dp, one sequence is a single segment, and in every other sequence the last cell is a segment of its own with id 512 - 1.
All inputs are finite; a program needn't handle non-finite values.
Results may differ from the reference program's by a relative error of at most 0.02.
Values may be sent and summed in bfloat16 or wider, within the bound.
No kernel may reach another device: no remote copies, remote signals or barrier semaphores. Data moves between devices by JAX's collectives and lax.ppermute only.
A program may use at most 448 MiB of HBM per device.

```python
import math
import jax
import jax.numpy as jnp
from jax import lax

D = 1024
FF = 4096
HEADS = 16
HEAD_DIM = 64
SEQS = 2
GENES = 1024
LEN = 512
SEQ_ALL = 8


def draw_segment_ids(key, part):
    key = jax.random.fold_in(key, 11)
    key_rate, key_ticks, key_pick = jax.random.split(key, 3)
    shifts = jax.random.randint(key_rate, (SEQ_ALL, 1), 3, 13)
    tick_values = jax.random.randint(key_ticks, (SEQ_ALL, LEN), 0, 1 << 20)
    position = jnp.arange(LEN, dtype=jnp.int32)[None, :]
    starts = (jnp.right_shift(tick_values, 20 - shifts) == 0) & (position > 0) & (position < LEN - 1)
    labels = jnp.cumsum(starts.astype(jnp.int32), axis=1).astype(jnp.int32)
    labels = jnp.where(position == LEN - 1, LEN - 1, labels).astype(jnp.int32)
    chosen = jax.random.randint(key_pick, (SEQ_ALL // SEQS, 1), 0, SEQS)
    seq_numbers = jnp.arange(SEQ_ALL, dtype=jnp.int32).reshape(SEQ_ALL // SEQS, SEQS) % SEQS
    single = (seq_numbers == chosen).reshape(SEQ_ALL, 1)
    return jnp.where(single, 0, labels).astype(jnp.int32)


def touch_ends(values, rng, smallest, high):
    place = [jax.random.randint(jax.random.fold_in(rng, axis), (), 0, length) for axis, length in enumerate(values.shape)]
    main_axis = values.shape.index(max(values.shape))
    beside = place[:main_axis] + [(place[main_axis] + 1) % values.shape[main_axis]] + place[main_axis + 1:]
    return values.at[tuple(place)].set(smallest).at[tuple(beside)].set(high)


def shard_levels(own_key, dims, pieces, smallest, high):
    factor_of, own = 1.0, jax.random.fold_in(own_key, 6)
    for axis_at, parts in pieces:
        steps = jnp.exp(jax.random.uniform(jax.random.fold_in(own, axis_at), (parts,), jnp.float32, smallest / len(pieces), high / len(pieces)))
        factor_of = factor_of * jnp.repeat(steps, dims[axis_at] // parts).reshape([-1 if axis == axis_at else 1 for axis in range(len(dims))])
    return factor_of


def scatter_about(rng, shape, deviation, limit, pieces=(), kind=jnp.bfloat16):
    values = deviation * jax.random.normal(rng, shape, jnp.float32)
    if pieces:
        values = values * shard_levels(rng, shape, pieces, -0.22, 0.18)
    return jnp.clip(values, -limit, limit).astype(kind)


def setup_inputs(seed: int = 0) -> dict:
    keys = jax.random.split(jax.random.key(seed), 16)
    counts = touch_ends(jax.random.randint(keys[0], (SEQ_ALL, LEN, GENES), 0, 16), jax.random.fold_in(keys[0], 1), 0, 15).astype(jnp.int32)
    coords = touch_ends(jax.random.randint(keys[1], (2, SEQ_ALL, LEN), 0, 1024), jax.random.fold_in(keys[1], 1), 0, 1023).astype(jnp.int32)
    segment_ids = draw_segment_ids(jax.random.fold_in(keys[15], 71), 0)
    logit_grad = scatter_about(keys[3], (SEQ_ALL, LEN, GENES), 0.35, 5.0, ((0, 4), (1, 8)))
    enc_weight = scatter_about(keys[4], (GENES, D), (4 * GENES) ** -0.5, 0.09375, ((0, 8),))
    qkv_weight = scatter_about(keys[5], (D, 3 * D), D ** -0.5, 0.1875, ((0, 8),))
    out_weight = scatter_about(keys[6], (D, D), (D // 16) ** -0.5, 0.75, ((0, 8),))
    up_weight = scatter_about(keys[7], (D, FF), D ** -0.5, 0.1875, ((0, 8),))
    down_weight = scatter_about(keys[8], (FF, D), FF ** -0.5, 0.09375, ((0, 8),))
    dec_weight = scatter_about(keys[9], (D, GENES), D ** -0.5, 0.1875, ((0, 8),))
    dec_bias = scatter_about(keys[10], (GENES,), 1.0, 4.0, ((0, 8),))
    norm1_gain = jnp.clip(1.0 + 0.1 * jax.random.normal(keys[11], (D,), jnp.float32), 0.5, 1.5).astype(jnp.bfloat16)
    norm1_shift = scatter_about(keys[12], (D,), 0.5, 3.0, ((0, 8),))
    norm2_gain = jnp.clip(1.0 + 0.1 * jax.random.normal(keys[13], (D,), jnp.float32), 0.5, 1.5).astype(jnp.bfloat16)
    norm2_shift = scatter_about(keys[14], (D,), 0.5, 3.0, ((0, 8),))
    return dict(counts=counts, coords=coords, segment_ids=segment_ids, logit_grad=logit_grad, enc_weight=enc_weight, qkv_weight=qkv_weight, out_weight=out_weight, up_weight=up_weight, down_weight=down_weight, dec_weight=dec_weight, dec_bias=dec_bias, norm1_gain=norm1_gain, norm1_shift=norm1_shift, norm2_gain=norm2_gain, norm2_shift=norm2_shift)


@jax.custom_vjp
def low(v):
    return lax.optimization_barrier(v.astype(jnp.bfloat16)).astype(jnp.float32)

@jax.custom_vjp
def low_back(v):
    return v

def low_keep(v):
    return (low(v), None)

def low_pass(kept, grad):
    return (grad,)

def back_keep(v):
    return (v, None)

def back_low(kept, grad):
    return (low(grad),)
low.defvjp(low_keep, low_pass)
low_back.defvjp(back_keep, back_low)
NEGATIVE = -1e+30
EPSILON = 1e-05

def matmul(left, right):
    return jnp.dot(left, right, precision=lax.Precision.HIGHEST, preferred_element_type=jnp.float32)

def layer_norm(inputs, gain_vec, shift_vec):
    centre = inputs - lax.optimization_barrier(jnp.mean(inputs, axis=-1, keepdims=True))
    spread = lax.optimization_barrier(jnp.mean(centre * centre, axis=-1, keepdims=True))
    return centre * lax.rsqrt(spread + EPSILON) * gain_vec + shift_vec

def sinusoids(coords):
    quarter = D // 4
    frequency = jnp.exp(jnp.arange(quarter, dtype=jnp.float32) * (-math.log(10000.0) / quarter))
    first_angle = coords[0].astype(jnp.float32)[..., None] * frequency
    second_angle = coords[1].astype(jnp.float32)[..., None] * frequency
    return jnp.concatenate([jnp.sin(first_angle), jnp.cos(first_angle), jnp.sin(second_angle), jnp.cos(second_angle)], axis=-1)

def attend_sequence(queries, key_rows, values, seg_row):
    length = queries.shape[0]
    block = math.gcd(length, 512)
    scaling = HEAD_DIM ** (-0.5)
    query_blocks = queries.reshape(length // block, block, HEADS, HEAD_DIM)
    seg_blocks = seg_row.reshape(length // block, block)

    def one_block(packed):
        query_part, seg_part = packed
        scores = low_back(jnp.einsum('qhe,khe->hqk', query_part, key_rows, precision=lax.Precision.HIGHEST) * scaling)
        allowed = seg_part[None, :, None] == seg_row[None, None, :]
        scores = jnp.where(allowed, scores, NEGATIVE)
        probs = low(jax.nn.softmax(scores, axis=-1))
        output = jnp.einsum('hqk,khe->qhe', probs, values, precision=lax.Precision.HIGHEST)
        return low_back(low(output))
    result = lax.map(jax.checkpoint(one_block), (query_blocks, seg_blocks))
    return result.reshape(length, HEADS, HEAD_DIM)

def reference(counts, coords, segment_ids, logit_grad, enc_weight, qkv_weight, out_weight, up_weight, down_weight, dec_weight, dec_bias, norm1_gain, norm1_shift, norm2_gain, norm2_shift):
    express = low(jnp.log1p(counts.astype(jnp.float32))).reshape(SEQ_ALL * LEN, GENES)
    embed = sinusoids(coords).reshape(SEQ_ALL * LEN, D)
    weights_in = [enc_weight, qkv_weight, out_weight, up_weight, down_weight, dec_weight, dec_bias, norm1_gain, norm1_shift, norm2_gain, norm2_shift]
    weights_in = [entry.astype(jnp.float32) for entry in weights_in]

    def forward(express_in, w_enc, w_qkv, w_out, w_up, w_down, w_dec, b_dec, gain_one, shift_one, gain_two, shift_two):
        hidden0 = low_back(matmul(express_in, w_enc)) + embed
        normed1 = low(layer_norm(hidden0, gain_one, shift_one))
        qkv = low_back(low(matmul(normed1, w_qkv)))
        queries = qkv[:, :D].reshape(SEQ_ALL, LEN, HEADS, HEAD_DIM)
        key_rows = qkv[:, D:2 * D].reshape(SEQ_ALL, LEN, HEADS, HEAD_DIM)
        values = qkv[:, 2 * D:].reshape(SEQ_ALL, LEN, HEADS, HEAD_DIM)
        context = lax.map(lambda packed: attend_sequence(*packed), (queries, key_rows, values, segment_ids))
        context = context.reshape(SEQ_ALL * LEN, D)
        hidden1 = hidden0 + low_back(matmul(context, w_out))
        normed2 = low(layer_norm(hidden1, gain_two, shift_two))
        up_value = low_back(matmul(normed2, w_up))
        active = low(jax.nn.gelu(up_value))
        hidden2 = hidden1 + low_back(matmul(active, w_down))
        output = matmul(low(hidden2), w_dec) + b_dec
        return output.reshape(SEQ_ALL, LEN, GENES)
    outputs, pullback = jax.vjp(forward, express, *weights_in)
    grads = pullback(logit_grad.astype(jnp.float32))
    input_grad = grads[0].reshape(SEQ_ALL, LEN, GENES).astype(jnp.bfloat16)
    return (outputs.astype(jnp.bfloat16), input_grad, grads[1], grads[2], grads[3], grads[4], grads[5], grads[6], grads[7], grads[8], grads[9], grads[10], grads[11])
```

```python
import functools
import math

import jax
import jax.numpy as jnp
from jax import lax
from jax.experimental import pallas as pl
from jax.experimental.pallas import tpu as pltpu
from jax.sharding import Mesh
from jax.sharding import PartitionSpec as P

HEADS = 16


NEGATIVE = -1e30
EPSILON = 1e-05


def layer_norm(inputs, gain_vec, shift_vec):
    centre = inputs - jnp.mean(inputs, axis=-1, keepdims=True)
    spread = jnp.mean(centre * centre, axis=-1, keepdims=True)
    return centre * lax.rsqrt(spread + EPSILON) * gain_vec + shift_vec


def sinusoids(coords, width):
    quarter = width // 4
    frequency = jnp.exp(jnp.arange(quarter, dtype=jnp.float32) * (-math.log(10000.0) / quarter))
    first_angle = coords[0].astype(jnp.float32)[..., None] * frequency
    second_angle = coords[1].astype(jnp.float32)[..., None] * frequency
    return jnp.concatenate(
        [jnp.sin(first_angle), jnp.cos(first_angle), jnp.sin(second_angle), jnp.cos(second_angle)],
        axis=-1,
    )


def inner(left, right):
    return lax.dot_general(
        left, right, (((0,), (0,)), ((), ())), preferred_element_type=jnp.float32
    )


def times_t(left, right):
    return lax.dot_general(
        left, right, (((1,), (1,)), ((), ())), preferred_element_type=jnp.float32
    )


def spread_plan(
    counts,
    coords,
    segment_ids,
    logit_grad,
    enc_weight,
    qkv_weight,
    out_weight,
    up_weight,
    down_weight,
    dec_weight,
    dec_bias,
    norm1_gain,
    norm1_shift,
    norm2_gain,
    norm2_shift,
):
    gathered = (
        lax.all_gather(enc_weight, "blk", axis=0, tiled=True),
        lax.all_gather(qkv_weight, "blk", axis=0, tiled=True),
        lax.all_gather(out_weight, "blk", axis=0, tiled=True),
        lax.all_gather(up_weight, "blk", axis=0, tiled=True),
        lax.all_gather(down_weight, "blk", axis=0, tiled=True),
        lax.all_gather(dec_weight, "blk", axis=0, tiled=True),
        lax.all_gather(dec_bias, "blk", axis=0, tiled=True),
        lax.all_gather(norm1_gain, "blk", axis=0, tiled=True),
        lax.all_gather(norm1_shift, "blk", axis=0, tiled=True),
        lax.all_gather(norm2_gain, "blk", axis=0, tiled=True),
        lax.all_gather(norm2_shift, "blk", axis=0, tiled=True),
    )
    w_enc, w_qkv, w_out, w_up, w_down, w_dec, b_dec, gain_one, shift_one, gain_two, shift_two = (
        gathered
    )
    seg_all = lax.all_gather(segment_ids, "blk", axis=1, tiled=True)
    seq_count, cell_count, gene_count = counts.shape
    width = w_enc.shape[1]
    head_count = HEADS
    head_size = width // head_count
    scaling = head_size ** (-0.5)
    row_count = seq_count * cell_count
    express = (
        jnp.log1p(counts.astype(jnp.float32)).astype(jnp.bfloat16).reshape(row_count, gene_count)
    )
    embed = sinusoids(coords, width).reshape(row_count, width)
    hidden0 = jnp.dot(express, w_enc, preferred_element_type=jnp.float32) + embed
    gain_one32 = gain_one.astype(jnp.float32)
    shift_one32 = shift_one.astype(jnp.float32)
    gain_two32 = gain_two.astype(jnp.float32)
    shift_two32 = shift_two.astype(jnp.float32)
    normed1 = layer_norm(hidden0, gain_one32, shift_one32).astype(jnp.bfloat16)
    qkv = jnp.dot(normed1, w_qkv, preferred_element_type=jnp.float32).astype(jnp.bfloat16)
    queries = qkv[:, :width].reshape(seq_count, cell_count, head_count, head_size)
    key_rows = qkv[:, width : 2 * width].reshape(seq_count, cell_count, head_count, head_size)
    values = qkv[:, 2 * width :].reshape(seq_count, cell_count, head_count, head_size)

    def masked_scores(query_part, key_part, seg_query, seg_key):
        scores = (
            jnp.einsum("sqhe,skhe->shqk", query_part, key_part, preferred_element_type=jnp.float32)
            * scaling
        )
        return jnp.where(seg_query[:, None, :, None] == seg_key[:, None, None, :], scores, NEGATIVE)

    start_max = jnp.full((seq_count, head_count, cell_count), NEGATIVE, jnp.float32)
    piece = (
        lax.all_gather(key_rows, "blk", axis=1, tiled=True),
        lax.all_gather(values, "blk", axis=1, tiled=True),
    )
    seg_part = seg_all
    incoming = (piece[0], piece[1], seg_part)
    running_max = start_max
    key_part, value_part, context_seg_part = incoming
    query_part = queries
    scores = masked_scores(query_part, key_part, segment_ids, context_seg_part)
    newest = jnp.maximum(running_max, jnp.max(scores, axis=-1))
    expo = jnp.exp(scores - newest[..., None])
    running_sum = jnp.sum(expo, axis=-1)
    update = jnp.einsum(
        "shqk,skhe->sqhe", expo.astype(jnp.bfloat16), value_part, preferred_element_type=jnp.float32
    )
    weighted = update
    running_max, running_sum, weighted = (newest, running_sum, weighted)
    context32 = weighted / jnp.transpose(running_sum, (0, 2, 1))[..., None]
    logsum = jnp.transpose(running_max + jnp.log(running_sum), (0, 2, 1))
    context = context32.astype(jnp.bfloat16).reshape(row_count, width)
    hidden1 = hidden0 + jnp.dot(context, w_out, preferred_element_type=jnp.float32)
    normed2 = layer_norm(hidden1, gain_two32, shift_two32).astype(jnp.bfloat16)
    up_value = jnp.dot(normed2, w_up, preferred_element_type=jnp.float32)
    active = jax.nn.gelu(up_value).astype(jnp.bfloat16)
    hidden2 = hidden1 + jnp.dot(active, w_down, preferred_element_type=jnp.float32)
    hidden2_low = hidden2.astype(jnp.bfloat16)
    logits = (
        jnp.dot(hidden2_low, w_dec, preferred_element_type=jnp.float32) + b_dec.astype(jnp.float32)
    ).astype(jnp.bfloat16)
    cotangent = logit_grad.reshape(row_count, gene_count)
    grad_dec = inner(hidden2_low, cotangent)
    grad_bias = jnp.sum(cotangent.astype(jnp.float32), axis=0)
    grad_h2 = times_t(cotangent, w_dec)
    grad_down = grad_h2.astype(jnp.bfloat16)
    grad_w_down = inner(active, grad_down)
    grad_active = times_t(grad_down, w_down)
    gelu_pull = jax.vjp(jax.nn.gelu, up_value)[1]
    grad_up = gelu_pull(grad_active)[0].astype(jnp.bfloat16)
    grad_w_up = inner(normed2, grad_up)
    grad_normed2 = times_t(grad_up, w_up)
    norm_pull_two = jax.vjp(layer_norm, hidden1, gain_two32, shift_two32)[1]
    part_two, grad_gain_two, grad_shift_two = norm_pull_two(grad_normed2)
    grad_h1 = grad_h2 + part_two
    grad_attn = grad_h1.astype(jnp.bfloat16)
    grad_w_out = inner(context, grad_attn)
    grad_context = (
        times_t(grad_attn, w_out)
        .astype(jnp.bfloat16)
        .reshape(seq_count, cell_count, head_count, head_size)
    )
    delta = jnp.sum(grad_context.astype(jnp.float32) * context32, axis=-1)
    logsum_all, delta_all = (
        lax.all_gather(logsum, "blk", axis=1, tiled=True),
        lax.all_gather(delta, "blk", axis=1, tiled=True),
    )
    seg_part = seg_all
    query_seg_part = seg_part
    query_part = queries
    gradout_part = grad_context
    logsum_part = logsum
    delta_part = delta
    scores = masked_scores(query_part, key_part, segment_ids, query_seg_part)
    probs = jnp.exp(scores - jnp.transpose(logsum_part, (0, 2, 1))[..., None])
    dprob = jnp.einsum(
        "sqhe,skhe->shqk", gradout_part, value_part, preferred_element_type=jnp.float32
    )
    dscore = (probs * (dprob - jnp.transpose(delta_part, (0, 2, 1))[..., None])).astype(
        jnp.bfloat16
    )
    grad_queries = (
        jnp.einsum("shqk,skhe->sqhe", dscore, key_part, preferred_element_type=jnp.float32)
        * scaling
    )
    piece = (
        lax.all_gather(queries, "blk", axis=1, tiled=True),
        lax.all_gather(grad_context, "blk", axis=1, tiled=True),
    )
    seg_part = seg_all
    logsum_part = logsum_all
    delta_part = delta_all
    incoming = (piece[0], piece[1], logsum_part, delta_part, seg_part)
    query_part, gradout_part, key_logsum_part, key_delta_part, key_seg_part = incoming
    key_part = key_rows
    scores = masked_scores(query_part, key_part, key_seg_part, segment_ids)
    probs = jnp.exp(scores - jnp.transpose(key_logsum_part, (0, 2, 1))[..., None])
    grad_values = jnp.einsum(
        "shqk,sqhe->skhe",
        probs.astype(jnp.bfloat16),
        gradout_part,
        preferred_element_type=jnp.float32,
    )
    dprob = jnp.einsum("sqhe,skhe->shqk", gradout_part, values, preferred_element_type=jnp.float32)
    dscore = (probs * (dprob - jnp.transpose(key_delta_part, (0, 2, 1))[..., None])).astype(
        jnp.bfloat16
    )
    grad_keys = (
        jnp.einsum("shqk,sqhe->skhe", dscore, query_part, preferred_element_type=jnp.float32)
        * scaling
    )
    grad_keys, grad_values = (grad_keys, grad_values)
    grad_qkv = jnp.concatenate(
        [
            grad_queries.reshape(row_count, width),
            grad_keys.reshape(row_count, width),
            grad_values.reshape(row_count, width),
        ],
        axis=1,
    ).astype(jnp.bfloat16)
    grad_w_qkv = inner(normed1, grad_qkv)
    grad_normed1 = times_t(grad_qkv, w_qkv)
    norm_pull_one = jax.vjp(layer_norm, hidden0, gain_one32, shift_one32)[1]
    part_one, grad_gain_one, grad_shift_one = norm_pull_one(grad_normed1)
    grad_h0 = (grad_h1 + part_one).astype(jnp.bfloat16)
    input_grad = (
        times_t(grad_h0, w_enc).astype(jnp.bfloat16).reshape(seq_count, cell_count, gene_count)
    )
    enc_share = lax.psum_scatter(inner(express, grad_h0), "blk", scatter_dimension=0, tiled=True)
    shares = (
        lax.psum_scatter(grad_w_qkv, "blk", scatter_dimension=0, tiled=True),
        lax.psum_scatter(grad_w_out, "blk", scatter_dimension=0, tiled=True),
        lax.psum_scatter(grad_w_up, "blk", scatter_dimension=0, tiled=True),
        lax.psum_scatter(grad_w_down, "blk", scatter_dimension=0, tiled=True),
        lax.psum_scatter(grad_dec, "blk", scatter_dimension=0, tiled=True),
        lax.psum_scatter(grad_bias, "blk", scatter_dimension=0, tiled=True),
        lax.psum_scatter(grad_gain_one, "blk", scatter_dimension=0, tiled=True),
        lax.psum_scatter(grad_shift_one, "blk", scatter_dimension=0, tiled=True),
        lax.psum_scatter(grad_gain_two, "blk", scatter_dimension=0, tiled=True),
        lax.psum_scatter(grad_shift_two, "blk", scatter_dimension=0, tiled=True),
    )
    summed = (
        lax.psum(enc_share.astype(jnp.bfloat16), "dp").astype(jnp.float32),
        lax.psum(shares[0].astype(jnp.bfloat16), "dp").astype(jnp.float32),
        lax.psum(shares[1].astype(jnp.bfloat16), "dp").astype(jnp.float32),
        lax.psum(shares[2].astype(jnp.bfloat16), "dp").astype(jnp.float32),
        lax.psum(shares[3].astype(jnp.bfloat16), "dp").astype(jnp.float32),
        lax.psum(shares[4].astype(jnp.bfloat16), "dp").astype(jnp.float32),
        lax.psum(shares[5].astype(jnp.bfloat16), "dp").astype(jnp.float32),
        lax.psum(shares[6].astype(jnp.bfloat16), "dp").astype(jnp.float32),
        lax.psum(shares[7].astype(jnp.bfloat16), "dp").astype(jnp.float32),
        lax.psum(shares[8].astype(jnp.bfloat16), "dp").astype(jnp.float32),
        lax.psum(shares[9].astype(jnp.bfloat16), "dp").astype(jnp.float32),
    )
    return (
        logits.reshape(seq_count, cell_count, gene_count),
        input_grad,
        summed[0],
        summed[1],
        summed[2],
        summed[3],
        summed[4],
        summed[5],
        summed[6],
        summed[7],
        summed[8],
        summed[9],
        summed[10],
    )


AXES = ("y", "core", "z", "x")
SPLIT = 64


class Place:
    def __init__(self, sizes):
        self.sizes = sizes
        self.y, self.core, self.z, self.x = (lax.axis_index(name) for name in AXES)

    def send(self, value, move):
        ny, nc, nz, nx = self.sizes

        def flat(place):
            y, c, z, x = place
            return ((y * nc + c) * nz + z) * nx + x

        everywhere = [
            (y, c, z, x) for y in range(ny) for c in range(nc) for z in range(nz) for x in range(nx)
        ]
        return lax.ppermute(value, AXES, [(flat(p), flat(move(*p))) for p in everywhere])

    def swap_core(self, value):
        return self.send(value, lambda y, c, z, x: (y, 1 - c, z, x))

    def swap_x(self, value):
        return self.send(value, lambda y, c, z, x: (y, c, z, 1 - x))

    def swap_y(self, value):
        return self.send(value, lambda y, c, z, x: (1 - y, c, z, x))

    def shift_z(self, value, step):
        nz = self.sizes[2]
        return self.send(value, lambda y, c, z, x: (y, c, (z + step) % nz, x))

    def to_group(self, value):
        low = self.z % 2 == 0
        first = self.send(
            jnp.where(low, value[0], value[1]), lambda y, c, z, x: (y, z // 2, 2 * c + z % 2, x)
        )
        second = self.send(
            jnp.where(low, value[1], value[0]),
            lambda y, c, z, x: (y, z // 2, 2 * c + 1 - z % 2, x),
        )
        return first, second

    def from_group(self, value):
        first, second = self.to_group_raw(value)
        low = self.z % 2 == 0
        return jnp.stack([jnp.where(low, first, second), jnp.where(low, second, first)])

    def to_group_raw(self, value):
        first = self.send(value[0], lambda y, c, z, x: (y, z // 2, 2 * c + z % 2, x))
        second = self.send(value[1], lambda y, c, z, x: (y, z // 2, 2 * c + 1 - z % 2, x))
        return first, second

    def whole_group(self, value):
        half = jnp.concatenate([value, self.swap_x(value)], axis=0)
        return jnp.concatenate([half, self.swap_core(half)], axis=0)

    def sum_group(self, part):
        half = part.shape[0] // 2
        low = part.astype(jnp.bfloat16)
        mine = (part[:half] + self.swap_core(low[half:]).astype(jnp.float32)).astype(jnp.bfloat16)
        other = self.swap_x(mine)
        quarter = half // 2
        other = jnp.concatenate([other[quarter:], other[:quarter]], axis=0)
        return mine.astype(jnp.float32) + other.astype(jnp.float32)


def in_order(index, mine, other):
    return jnp.where(index == 0, jnp.stack([mine, other]), jnp.stack([other, mine]))


def lay_out(pieces, out_shape, copies):
    count = len(copies(0, 0, 0, 0))

    def kernel(*refs):
        sources, target, sems = refs[:-2], refs[-2], refs[-1]
        place = tuple(lax.axis_index(name) for name in AXES)
        started = []
        for number, (piece, rows, columns, row, column) in enumerate(copies(*place)):
            size = rows[1] - rows[0]
            width = columns[1] - columns[0]
            copy = pltpu.make_async_copy(
                sources[piece].at[rows[0] : rows[1], columns[0] : columns[1]],
                target.at[pl.ds(pl.multiple_of(row, 16), size), column : column + width],
                sems.at[number],
            )
            copy.start()
            started.append(copy)
        for copy in started:
            copy.wait()

    size = math.prod(out_shape) * 2
    return pl.pallas_call(
        kernel,
        out_shape=jax.ShapeDtypeStruct(out_shape, jnp.bfloat16),
        in_specs=[pl.BlockSpec(memory_space=pl.ANY)] * len(pieces),
        out_specs=pl.BlockSpec(memory_space=pl.ANY),
        scratch_shapes=[pltpu.SemaphoreType.DMA((count,))],
        cost_estimate=pl.CostEstimate(flops=0, bytes_accessed=2 * size, transcendentals=0),
    )(*pieces)


def dot(left, right):
    return jnp.dot(left, right, preferred_element_type=jnp.float32)


def soft(queries, keys, allowed, scaling):
    scores = times_t(queries, keys) * scaling
    scores = jnp.where(allowed, scores, NEGATIVE)
    expo = jnp.exp(scores - jnp.max(scores, axis=-1, keepdims=True))
    return expo / jnp.sum(expo, axis=-1, keepdims=True)


def attend_kernel(heads, size, qkv_ref, column_ref, row_ref, out_ref):
    width = heads * size
    allowed = column_ref[...] == row_ref[...]
    for head in range(heads):
        at = head * size
        queries = qkv_ref[:, at : at + size]
        keys = qkv_ref[:, width + at : width + at + size]
        values = qkv_ref[:, 2 * width + at : 2 * width + at + size]
        probs = soft(queries, keys, allowed, size**-0.5)
        out_ref[:, at : at + size] = dot(probs.astype(jnp.bfloat16), values).astype(jnp.bfloat16)


def attend_back_kernel(heads, size, qkv_ref, grad_ref, column_ref, row_ref, out_ref):
    width = heads * size
    allowed = column_ref[...] == row_ref[...]
    for head in range(heads):
        at = head * size
        queries = qkv_ref[:, at : at + size]
        keys = qkv_ref[:, width + at : width + at + size]
        values = qkv_ref[:, 2 * width + at : 2 * width + at + size]
        grad = grad_ref[:, at : at + size]
        probs = soft(queries, keys, allowed, size**-0.5)
        dprob = times_t(grad, values)
        weighted = probs * dprob
        delta = jnp.sum(weighted, axis=-1, keepdims=True)
        dscore = (weighted - probs * delta).astype(jnp.bfloat16)
        grad_queries = dot(dscore, keys) * size**-0.5
        grad_keys = inner(dscore, queries) * size**-0.5
        grad_values = inner(probs.astype(jnp.bfloat16), grad)
        out_ref[:, at : at + size] = grad_queries.astype(jnp.bfloat16)
        out_ref[:, width + at : width + at + size] = grad_keys.astype(jnp.bfloat16)
        out_ref[:, 2 * width + at : 2 * width + at + size] = grad_values.astype(jnp.bfloat16)


def in_vmem(kernel, out_shape, flops, transcendentals, *operands):
    whole = pl.BlockSpec(memory_space=pltpu.VMEM)
    return pl.pallas_call(
        kernel,
        out_shape=jax.ShapeDtypeStruct(out_shape, jnp.bfloat16),
        in_specs=[whole] * len(operands),
        out_specs=whole,
        compiler_params=pltpu.CompilerParams(vmem_limit_bytes=40 * 1024 * 1024),
        cost_estimate=pl.CostEstimate(
            flops=flops, bytes_accessed=4 * math.prod(out_shape), transcendentals=transcendentals
        ),
    )(*operands)


def sinusoids_of_whole(coords, width):
    quarter = width // 4
    frequency = jnp.exp(jnp.arange(quarter, dtype=jnp.float32) * (-math.log(10000.0) / quarter))
    number = jnp.arange(32, dtype=jnp.float32)[:, None]
    far, near = 32.0 * number * frequency, number * frequency
    far = jnp.concatenate([jnp.sin(far), jnp.cos(far)], axis=1)
    near = jnp.concatenate([jnp.sin(near), jnp.cos(near)], axis=1)
    parts = []
    for coord in coords:
        whole = coord.astype(jnp.int32)
        pick_far = (whole // 32 == jnp.arange(32)[None, :]).astype(jnp.float32)
        pick_near = (whole % 32 == jnp.arange(32)[None, :]).astype(jnp.float32)
        at_far = jnp.dot(pick_far, far, precision=lax.Precision.HIGHEST)
        at_near = jnp.dot(pick_near, near, precision=lax.Precision.HIGHEST)
        sin_far, cos_far = at_far[:, :quarter], at_far[:, quarter:]
        sin_near, cos_near = at_near[:, :quarter], at_near[:, quarter:]
        parts.append(sin_far * cos_near + cos_far * sin_near)
        parts.append(cos_far * cos_near - sin_far * sin_near)
    return jnp.concatenate(parts, axis=1)


def normalise(inputs):
    centre = inputs - jnp.mean(inputs, axis=-1, keepdims=True)
    factor = lax.rsqrt(jnp.mean(centre * centre, axis=-1, keepdims=True) + EPSILON)
    return centre * factor, factor


def normalise_back(grad, normal, factor, gain):
    scaled = grad * gain
    inside = (
        scaled
        - jnp.mean(scaled, axis=-1, keepdims=True)
        - normal * jnp.mean(scaled * normal, axis=-1, keepdims=True)
    )
    return factor * inside, jnp.stack([jnp.sum(grad * normal, axis=0), jnp.sum(grad, axis=0)])


def wide(rows):
    count, width = rows.shape
    return rows.reshape(count, 4, width // 4).transpose(1, 0, 2).reshape(4 * count, width // 4)


def grouped_plan(
    sizes,
    counts,
    coords,
    segment_ids,
    logit_grad,
    enc_weight,
    qkv_weight,
    out_weight,
    up_weight,
    down_weight,
    dec_weight,
    dec_bias,
    norm1_gain,
    norm1_shift,
    norm2_gain,
    norm2_shift,
):
    place = Place(sizes)
    nz = sizes[2]
    seqs, cells, genes = counts.shape
    width = enc_weight.shape[1]
    block = enc_weight.shape[0]
    head = width // HEADS
    heads = HEADS // 4
    slice_width = width // 4
    own_rows = seqs * cells
    rows = 4 * own_rows
    ff = up_weight.shape[1]
    ff_slice = ff // 4
    bf16, f32 = jnp.bfloat16, jnp.float32

    def pick(value, axis, index):
        return lax.dynamic_index_in_dim(value, index, axis, keepdims=False)

    express = jnp.log1p(counts.astype(f32)).astype(bf16)
    whole = jnp.stack([coords[0], coords[1], segment_ids], axis=-1)
    beside = jnp.concatenate([whole // SPLIT, whole % SPLIT], axis=-1).astype(bf16)
    beside = jnp.pad(beside, ((0, 0), (0, 0), (0, 122)))
    cell_rows = jnp.concatenate([express, beside], axis=-1)
    first, second = place.to_group(cell_rows)
    cell_rows = place.whole_group(jnp.concatenate([first, second], axis=0))
    express = cell_rows[:, :genes]
    beside = cell_rows[:, genes:].astype(f32)
    beside = beside[:, :3] * SPLIT + beside[:, 3:6]
    segment = beside[:, 2:3]
    segment_row = segment.reshape(1, rows)
    embed = sinusoids_of_whole((beside[:, 0:1], beside[:, 1:2]), width)

    vectors = jnp.stack([dec_bias, norm1_gain, norm1_shift, norm2_gain, norm2_shift]).reshape(1, 5 * block)
    vectors = jnp.pad(vectors, ((0, 15), (0, width - 5 * block)))
    half = block // 2
    tall = half + 16
    enc_own = jnp.concatenate([pick(enc_weight.reshape(2, half, width), 0, place.core), vectors], axis=0)
    enc_z = jnp.concatenate([enc_own] + [place.shift_z(enc_own, k) for k in range(1, nz)], axis=0)
    enc_zx = jnp.concatenate([enc_z, place.swap_x(enc_z)], axis=0)
    enc_far = place.swap_core(enc_zx)

    def enc_copies(y, core, z, x):
        return [
            (dc, ((dx * nz + k) * tall, (dx * nz + k) * tall + half), (0, width),
             (2 * ((z - k) % nz) + (x ^ dx)) * block + (core ^ dc) * half, 0)
            for dc in range(2) for dx in range(2) for k in range(nz)
        ]

    def vector_copies(y, core, z, x):
        return [
            (0, ((dx * nz + k) * tall + half, (dx * nz + k + 1) * tall), (0, width),
             (2 * ((z - k) % nz) + (x ^ dx)) * 16, 0)
            for dx in range(2) for k in range(nz)
        ]

    w_enc = lay_out((enc_zx, enc_far), (genes, width), enc_copies)
    vectors = lay_out((enc_zx,), (2 * nz * 16, width), vector_copies)
    vectors = vectors.reshape(2 * nz, 16, width)[:, 0, : 5 * block].reshape(2 * nz, 5, block)
    vectors = vectors.transpose(1, 0, 2).reshape(5, width).astype(f32)
    b_dec, gain_one, shift_one, gain_two, shift_two = (vectors[i : i + 1] for i in range(5))

    qkv_parts = qkv_weight.reshape(block, 3, nz, 2, 2, head)
    qkv_parts = pick(qkv_parts, 4, place.core)
    qkv_mine = pick(qkv_parts, 3, place.x).reshape(block, 3 * slice_width)
    qkv_theirs = pick(qkv_parts, 3, 1 - place.x).reshape(block, 3 * slice_width)
    qkv_pair = jnp.stack([qkv_mine, place.swap_x(qkv_theirs)]).reshape(2, 2, half, 3 * slice_width)
    out_parts = pick(out_weight.reshape(2, 2, half // 2, width), 0, place.core)
    dec_parts = pick(dec_weight.reshape(2, 2, half // 2, genes), 0, place.core)
    quarter = half // 2

    def piece(of):
        top = jnp.concatenate(
            [pick(qkv_pair, 1, of).reshape(block, 3 * slice_width), wide(pick(out_parts, 0, of))],
            axis=1,
        )
        return jnp.concatenate([top, pick(dec_parts, 0, of)], axis=0)

    near = piece(place.y)
    near = [near] + [place.shift_z(near, k) for k in range(1, nz)]
    far = [piece(1 - place.y)] + [place.swap_y(part) for part in near[1:]]

    def qkv_copies(y, core, z, x):
        return [
            (dy * nz + k, (dx * half, (dx + 1) * half), (0, 3 * slice_width),
             (2 * ((z - k) % nz) + (x ^ dx)) * block + (y ^ dy) * half, 0)
            for k in range(nz) for dy in range(2) for dx in range(2)
        ]

    def out_copies(y, core, z, x):
        return [
            (dy * nz + k, (j * quarter, (j + 1) * quarter), (3 * slice_width, width),
             ((z - k) % nz) * half + (y ^ dy) * quarter, j * slice_width)
            for k in range(nz) for dy in range(2) for j in range(4)
        ]

    def dec_copies(y, core, z, x):
        return [
            (dy * nz + k, (block, block + quarter), (0, width),
             ((z - k) % nz) * half + (y ^ dy) * quarter, 0)
            for k in range(nz) for dy in range(2)
        ]

    w_qkv = lay_out(near + far, (width, 3 * slice_width), qkv_copies)
    w_out = lay_out(near + far, (slice_width, width), out_copies)
    dec_z = lay_out(near + far, (slice_width, genes), dec_copies)
    dec_zx = jnp.concatenate([dec_z, place.swap_x(dec_z)], axis=0)
    dec_far = place.swap_core(dec_zx)

    def dec_all_copies(y, core, z, x):
        return [
            (dc, ((dx * nz + k) * half, (dx * nz + k + 1) * half), (0, genes),
             (2 * k + (x ^ dx)) * block + (core ^ dc) * half, 0)
            for dc in range(2) for dx in range(2) for k in range(nz)
        ]

    w_dec = lay_out((dec_zx, dec_far), (width, genes), dec_all_copies)

    up_parts = up_weight.reshape(block, nz, 2, 2, 2, ff // (8 * nz))
    up_parts = pick(pick(up_parts, 4, place.y), 3, place.core)
    up_mine = pick(up_parts, 2, place.x).reshape(block, ff_slice // 2)
    up_theirs = pick(up_parts, 2, 1 - place.x).reshape(block, ff_slice // 2)
    up_own = in_order(place.x, up_mine, place.swap_x(up_theirs)).reshape(2 * block, ff_slice // 2)
    down_parts = down_weight.reshape(2, 2, down_weight.shape[0] // 4, width)
    down_own = pick(pick(down_parts, 0, place.core), 0, place.y)
    w_up = lax.all_gather(up_own, ("y", "z"), axis=0).reshape(2, width, ff_slice // 2)
    w_down = lax.all_gather(down_own, ("y", "z"), axis=0).reshape(2, ff_slice // 2, width)

    first, second = place.to_group(logit_grad)
    cotangent = place.whole_group(jnp.concatenate([first, second], axis=0))
    grad_bias = jnp.sum(cotangent.astype(f32), axis=0, keepdims=True)
    grad_h2 = times_t(cotangent, w_dec)
    grad_down = grad_h2.astype(bf16)

    hidden0 = dot(express, w_enc) + embed
    normal1, factor1 = normalise(hidden0)
    normed1 = (normal1 * gain_one + shift_one).astype(bf16)
    qkv = dot(normed1, w_qkv).astype(bf16)
    pairs = heads * rows * rows
    context = in_vmem(
        functools.partial(attend_kernel, heads, head),
        (rows, slice_width), 4 * pairs * head, pairs, qkv, segment, segment_row,
    )
    half_rows = rows // 2
    hidden1 = hidden0[:half_rows] + place.sum_group(dot(context, w_out))
    normal2, factor2 = normalise(hidden1)
    normed2 = (normal2 * gain_two + shift_two).astype(bf16)
    normed2 = jnp.concatenate([normed2, place.swap_core(normed2)], axis=0)
    up_value = [dot(normed2, w_up[i]) for i in range(2)]
    active = [jax.nn.gelu(value).astype(bf16) for value in up_value]
    hidden2 = hidden1 + place.sum_group(dot(active[0], w_down[0]) + dot(active[1], w_down[1]))
    hidden2 = hidden2.astype(bf16)
    logits = (dot(hidden2[:own_rows], w_dec) + b_dec).astype(bf16)
    logits = place.from_group(logits.reshape(seqs, cells, genes))

    hidden2_parts = pick(hidden2.reshape(half_rows, nz, 2, 2, half), 2, place.x)
    hidden2_slice = jnp.concatenate(
        [
            pick(hidden2_parts, 2, place.core).reshape(half_rows, slice_width),
            place.swap_core(pick(hidden2_parts, 2, 1 - place.core).reshape(half_rows, slice_width)),
        ],
        axis=0,
    )
    grad_w_dec = inner(hidden2_slice, cotangent).astype(bf16)
    grad_w_down = [inner(part, grad_down).astype(bf16) for part in active]
    grad_active = [times_t(grad_down, w_down[i]) for i in range(2)]
    grad_up = [
        jax.vjp(jax.nn.gelu, up_value[i])[1](grad_active[i])[0].astype(bf16) for i in range(2)
    ]
    grad_w_up = jnp.concatenate([inner(normed2, part) for part in grad_up], axis=1).astype(bf16)
    grad_normed2 = place.sum_group(times_t(grad_up[0], w_up[0]) + times_t(grad_up[1], w_up[1]))
    part_two, sums_two = normalise_back(grad_normed2, normal2, factor2, gain_two)
    grad_h1 = grad_h2[:half_rows] + part_two
    grad_attn = grad_h1.astype(bf16)

    def beside_core(value, sums):
        both = jnp.concatenate([value, jnp.pad(sums.astype(bf16), ((0, 14), (0, 0)))], axis=0)
        other = place.swap_core(both)
        return (
            jnp.concatenate([value, other[:half_rows]], axis=0),
            sums + other[half_rows : half_rows + 2].astype(f32),
        )

    grad_attn, sums_two = beside_core(grad_attn, sums_two)
    grad_w_out = inner(context, grad_attn).astype(bf16)
    grad_context = times_t(grad_attn, w_out).astype(bf16)
    grad_qkv = in_vmem(
        functools.partial(attend_back_kernel, heads, head),
        (rows, 3 * slice_width), 10 * pairs * head, pairs, qkv, grad_context, segment, segment_row,
    )
    grad_w_qkv = inner(normed1, grad_qkv).astype(bf16)
    grad_normed1 = place.sum_group(times_t(grad_qkv, w_qkv))
    part_one, sums_one = normalise_back(
        grad_normed1, normal1[:half_rows], factor1[:half_rows], gain_one
    )
    grad_h0 = (grad_h1 + part_one).astype(bf16)
    input_grad = times_t(grad_h0[:own_rows], w_enc).astype(bf16)
    input_grad = place.from_group(input_grad.reshape(seqs, cells, genes))
    grad_h0, sums_one = beside_core(grad_h0, sums_one)
    express_slice = pick(pick(express.reshape(rows, nz, 2, 2, half), 2, place.x), 2, place.core)
    grad_w_enc = inner(express_slice.reshape(rows, slice_width), grad_h0)

    def over_z(value):
        return lax.psum_scatter(value, "z", scatter_dimension=0, tiled=False)

    def over_y(value):
        return value.astype(f32) + place.swap_y(value).astype(f32)

    ff_piece = ff_slice // (2 * nz)
    early = jnp.concatenate(
        [part.reshape(nz, ff_piece, width) for part in grad_w_down]
        + [grad_w_dec.reshape(nz, half, genes)],
        axis=1,
    )
    early = over_y(over_z(early))
    early = in_order(place.core, early, place.swap_core(early.astype(bf16)).astype(f32))
    out_down = early[:, : 2 * ff_piece].reshape(4 * ff_piece, width)
    out_dec = early[:, 2 * ff_piece :].reshape(block, genes)

    def whole_columns(value):
        low = value.astype(bf16)
        mine = pick(value, 0, place.x)
        theirs = place.swap_x(pick(low, 0, 1 - place.x)).astype(f32)
        both = in_order(place.x, mine, theirs)
        other = place.swap_core(both.astype(bf16)).astype(f32)
        return in_order(place.core, both, other)

    middle = over_y(over_z(grad_w_up.reshape(nz, 2 * block, ff_slice)))
    out_up = whole_columns(middle.reshape(2, block, ff_slice))
    out_up = out_up.reshape(2, 2, block, 2, nz, ff_piece).transpose(2, 4, 1, 0, 3, 5)
    out_up = out_up.reshape(block, ff)

    late = jnp.concatenate(
        [
            grad_w_qkv.reshape(nz, 2 * block, 3 * slice_width),
            grad_w_out.reshape(nz, half, 4, slice_width)
            .transpose(0, 2, 1, 3)
            .reshape(nz, 2 * block, slice_width),
        ],
        axis=2,
    )
    late = over_y(over_z(late))
    out_qkv = whole_columns(late[:, : 3 * slice_width].reshape(2, block, 3 * slice_width))
    out_qkv = out_qkv.reshape(2, 2, block, 3, nz, head).transpose(2, 3, 4, 1, 0, 5)
    out_qkv = out_qkv.reshape(block, 3 * width)
    out_out = late[:, 3 * slice_width :].reshape(4, half, slice_width).transpose(1, 0, 2)
    out_out = out_out.reshape(half, width)
    out_out = in_order(place.core, out_out, place.swap_core(out_out.astype(bf16)).astype(f32))
    out_out = out_out.reshape(block, width)

    sums = jnp.concatenate([grad_bias, sums_one, sums_two], axis=0).reshape(5, nz, 2, block)
    sums = pick(sums, 2, place.x).transpose(1, 0, 2).reshape(nz, 1, 5 * block)
    sums = jnp.pad(sums, ((0, 0), (0, 15), (0, width - 5 * block)))
    last = jnp.concatenate([grad_w_enc.reshape(nz, half, width), sums], axis=1)
    last_low = last.astype(bf16)
    total = pick(last, 0, place.z)
    for k in range(1, nz):
        total += place.shift_z(pick(last_low, 0, (place.z + k) % nz), k).astype(f32)
    total = total + place.swap_y(total.astype(bf16)).astype(f32)
    out_enc = total[:half]
    out_enc = in_order(place.core, out_enc, place.swap_core(out_enc.astype(bf16)).astype(f32))
    out_enc = out_enc.reshape(block, width)
    sums = total[half, : 5 * block].reshape(5, block)
    return (
        logits, input_grad, out_enc, out_qkv, out_out, out_up, out_down, out_dec,
        sums[0], sums[1], sums[2], sums[3], sums[4],
    )


IN_SPECS = (
    ("dp", "blk", None), (None, "dp", "blk"), ("dp", "blk"), ("dp", "blk", None),
    *[("blk", None)] * 6, *[("blk",)] * 5,
)
OUT_SPECS = (("dp", "blk", None), ("dp", "blk", None), *[("blk", None)] * 6, *[("blk",)] * 5)


def solution(mesh):
    groups, blocks = mesh.shape["dp"], mesh.shape["blk"]

    def run(*args):
        seqs = args[0].shape[0] // groups
        if groups == 4 and blocks == 4 * seqs and seqs == 2 and HEADS == 4 * (blocks // 2):
            sizes = (groups // 2, 2, blocks // 2, 2)
            fine = Mesh(mesh.devices.reshape(sizes), AXES)
            names = {"dp": ("y", "core"), "blk": ("z", "x"), None: None}
            plan = functools.partial(grouped_plan, sizes)
        else:
            fine, names, plan = mesh, {"dp": "dp", "blk": "blk", None: None}, spread_plan
        specs = lambda entries: tuple(P(*[names[axis] for axis in entry]) for entry in entries)
        return jax.shard_map(
            plan, mesh=fine, in_specs=specs(IN_SPECS), out_specs=specs(OUT_SPECS), check_vma=False
        )(*args)

    return run
```

```python
import functools
import math

import jax
import jax.numpy as jnp
from jax import lax
from jax.experimental import pallas as pl
from jax.experimental.pallas import tpu as pltpu
from jax.sharding import Mesh
from jax.sharding import PartitionSpec as P

HEADS = 16


NEGATIVE = -1e30
EPSILON = 1e-05


def layer_norm(inputs, gain_vec, shift_vec):
    centre = inputs - jnp.mean(inputs, axis=-1, keepdims=True)
    spread = jnp.mean(centre * centre, axis=-1, keepdims=True)
    return centre * lax.rsqrt(spread + EPSILON) * gain_vec + shift_vec


def sinusoids(coords, width):
    quarter = width // 4
    frequency = jnp.exp(jnp.arange(quarter, dtype=jnp.float32) * (-math.log(10000.0) / quarter))
    first_angle = coords[0].astype(jnp.float32)[..., None] * frequency
    second_angle = coords[1].astype(jnp.float32)[..., None] * frequency
    return jnp.concatenate(
        [jnp.sin(first_angle), jnp.cos(first_angle), jnp.sin(second_angle), jnp.cos(second_angle)],
        axis=-1,
    )


def inner(left, right):
    return lax.dot_general(
        left, right, (((0,), (0,)), ((), ())), preferred_element_type=jnp.float32
    )


def times_t(left, right):
    return lax.dot_general(
        left, right, (((1,), (1,)), ((), ())), preferred_element_type=jnp.float32
    )


def spread_plan(
    counts,
    coords,
    segment_ids,
    logit_grad,
    enc_weight,
    qkv_weight,
    out_weight,
    up_weight,
    down_weight,
    dec_weight,
    dec_bias,
    norm1_gain,
    norm1_shift,
    norm2_gain,
    norm2_shift,
):
    gathered = (
        lax.all_gather(enc_weight, "blk", axis=0, tiled=True),
        lax.all_gather(qkv_weight, "blk", axis=0, tiled=True),
        lax.all_gather(out_weight, "blk", axis=0, tiled=True),
        lax.all_gather(up_weight, "blk", axis=0, tiled=True),
        lax.all_gather(down_weight, "blk", axis=0, tiled=True),
        lax.all_gather(dec_weight, "blk", axis=0, tiled=True),
        lax.all_gather(dec_bias, "blk", axis=0, tiled=True),
        lax.all_gather(norm1_gain, "blk", axis=0, tiled=True),
        lax.all_gather(norm1_shift, "blk", axis=0, tiled=True),
        lax.all_gather(norm2_gain, "blk", axis=0, tiled=True),
        lax.all_gather(norm2_shift, "blk", axis=0, tiled=True),
    )
    w_enc, w_qkv, w_out, w_up, w_down, w_dec, b_dec, gain_one, shift_one, gain_two, shift_two = (
        gathered
    )
    seg_all = lax.all_gather(segment_ids, "blk", axis=1, tiled=True)
    seq_count, cell_count, gene_count = counts.shape
    width = w_enc.shape[1]
    head_count = HEADS
    head_size = width // head_count
    scaling = head_size ** (-0.5)
    row_count = seq_count * cell_count
    express = (
        jnp.log1p(counts.astype(jnp.float32)).astype(jnp.bfloat16).reshape(row_count, gene_count)
    )
    embed = sinusoids(coords, width).reshape(row_count, width)
    hidden0 = jnp.dot(express, w_enc, preferred_element_type=jnp.float32) + embed
    gain_one32 = gain_one.astype(jnp.float32)
    shift_one32 = shift_one.astype(jnp.float32)
    gain_two32 = gain_two.astype(jnp.float32)
    shift_two32 = shift_two.astype(jnp.float32)
    normed1 = layer_norm(hidden0, gain_one32, shift_one32).astype(jnp.bfloat16)
    qkv = jnp.dot(normed1, w_qkv, preferred_element_type=jnp.float32).astype(jnp.bfloat16)
    queries = qkv[:, :width].reshape(seq_count, cell_count, head_count, head_size)
    key_rows = qkv[:, width : 2 * width].reshape(seq_count, cell_count, head_count, head_size)
    values = qkv[:, 2 * width :].reshape(seq_count, cell_count, head_count, head_size)

    def masked_scores(query_part, key_part, seg_query, seg_key):
        scores = (
            jnp.einsum("sqhe,skhe->shqk", query_part, key_part, preferred_element_type=jnp.float32)
            * scaling
        )
        return jnp.where(seg_query[:, None, :, None] == seg_key[:, None, None, :], scores, NEGATIVE)

    start_max = jnp.full((seq_count, head_count, cell_count), NEGATIVE, jnp.float32)
    piece = (
        lax.all_gather(key_rows, "blk", axis=1, tiled=True),
        lax.all_gather(values, "blk", axis=1, tiled=True),
    )
    seg_part = seg_all
    incoming = (piece[0], piece[1], seg_part)
    running_max = start_max
    key_part, value_part, context_seg_part = incoming
    query_part = queries
    scores = masked_scores(query_part, key_part, segment_ids, context_seg_part)
    newest = jnp.maximum(running_max, jnp.max(scores, axis=-1))
    expo = jnp.exp(scores - newest[..., None])
    running_sum = jnp.sum(expo, axis=-1)
    update = jnp.einsum(
        "shqk,skhe->sqhe", expo.astype(jnp.bfloat16), value_part, preferred_element_type=jnp.float32
    )
    weighted = update
    running_max, running_sum, weighted = (newest, running_sum, weighted)
    context32 = weighted / jnp.transpose(running_sum, (0, 2, 1))[..., None]
    logsum = jnp.transpose(running_max + jnp.log(running_sum), (0, 2, 1))
    context = context32.astype(jnp.bfloat16).reshape(row_count, width)
    hidden1 = hidden0 + jnp.dot(context, w_out, preferred_element_type=jnp.float32)
    normed2 = layer_norm(hidden1, gain_two32, shift_two32).astype(jnp.bfloat16)
    up_value = jnp.dot(normed2, w_up, preferred_element_type=jnp.float32)
    active = jax.nn.gelu(up_value).astype(jnp.bfloat16)
    hidden2 = hidden1 + jnp.dot(active, w_down, preferred_element_type=jnp.float32)
    hidden2_low = hidden2.astype(jnp.bfloat16)
    logits = (
        jnp.dot(hidden2_low, w_dec, preferred_element_type=jnp.float32) + b_dec.astype(jnp.float32)
    ).astype(jnp.bfloat16)
    cotangent = logit_grad.reshape(row_count, gene_count)
    grad_dec = inner(hidden2_low, cotangent)
    grad_bias = jnp.sum(cotangent.astype(jnp.float32), axis=0)
    grad_h2 = times_t(cotangent, w_dec)
    grad_down = grad_h2.astype(jnp.bfloat16)
    grad_w_down = inner(active, grad_down)
    grad_active = times_t(grad_down, w_down)
    gelu_pull = jax.vjp(jax.nn.gelu, up_value)[1]
    grad_up = gelu_pull(grad_active)[0].astype(jnp.bfloat16)
    grad_w_up = inner(normed2, grad_up)
    grad_normed2 = times_t(grad_up, w_up)
    norm_pull_two = jax.vjp(layer_norm, hidden1, gain_two32, shift_two32)[1]
    part_two, grad_gain_two, grad_shift_two = norm_pull_two(grad_normed2)
    grad_h1 = grad_h2 + part_two
    grad_attn = grad_h1.astype(jnp.bfloat16)
    grad_w_out = inner(context, grad_attn)
    grad_context = (
        times_t(grad_attn, w_out)
        .astype(jnp.bfloat16)
        .reshape(seq_count, cell_count, head_count, head_size)
    )
    delta = jnp.sum(grad_context.astype(jnp.float32) * context32, axis=-1)
    logsum_all, delta_all = (
        lax.all_gather(logsum, "blk", axis=1, tiled=True),
        lax.all_gather(delta, "blk", axis=1, tiled=True),
    )
    seg_part = seg_all
    query_seg_part = seg_part
    query_part = queries
    gradout_part = grad_context
    logsum_part = logsum
    delta_part = delta
    scores = masked_scores(query_part, key_part, segment_ids, query_seg_part)
    probs = jnp.exp(scores - jnp.transpose(logsum_part, (0, 2, 1))[..., None])
    dprob = jnp.einsum(
        "sqhe,skhe->shqk", gradout_part, value_part, preferred_element_type=jnp.float32
    )
    dscore = (probs * (dprob - jnp.transpose(delta_part, (0, 2, 1))[..., None])).astype(
        jnp.bfloat16
    )
    grad_queries = (
        jnp.einsum("shqk,skhe->sqhe", dscore, key_part, preferred_element_type=jnp.float32)
        * scaling
    )
    piece = (
        lax.all_gather(queries, "blk", axis=1, tiled=True),
        lax.all_gather(grad_context, "blk", axis=1, tiled=True),
    )
    seg_part = seg_all
    logsum_part = logsum_all
    delta_part = delta_all
    incoming = (piece[0], piece[1], logsum_part, delta_part, seg_part)
    query_part, gradout_part, key_logsum_part, key_delta_part, key_seg_part = incoming
    key_part = key_rows
    scores = masked_scores(query_part, key_part, key_seg_part, segment_ids)
    probs = jnp.exp(scores - jnp.transpose(key_logsum_part, (0, 2, 1))[..., None])
    grad_values = jnp.einsum(
        "shqk,sqhe->skhe",
        probs.astype(jnp.bfloat16),
        gradout_part,
        preferred_element_type=jnp.float32,
    )
    dprob = jnp.einsum("sqhe,skhe->shqk", gradout_part, values, preferred_element_type=jnp.float32)
    dscore = (probs * (dprob - jnp.transpose(key_delta_part, (0, 2, 1))[..., None])).astype(
        jnp.bfloat16
    )
    grad_keys = (
        jnp.einsum("shqk,sqhe->skhe", dscore, query_part, preferred_element_type=jnp.float32)
        * scaling
    )
    grad_keys, grad_values = (grad_keys, grad_values)
    grad_qkv = jnp.concatenate(
        [
            grad_queries.reshape(row_count, width),
            grad_keys.reshape(row_count, width),
            grad_values.reshape(row_count, width),
        ],
        axis=1,
    ).astype(jnp.bfloat16)
    grad_w_qkv = inner(normed1, grad_qkv)
    grad_normed1 = times_t(grad_qkv, w_qkv)
    norm_pull_one = jax.vjp(layer_norm, hidden0, gain_one32, shift_one32)[1]
    part_one, grad_gain_one, grad_shift_one = norm_pull_one(grad_normed1)
    grad_h0 = (grad_h1 + part_one).astype(jnp.bfloat16)
    input_grad = (
        times_t(grad_h0, w_enc).astype(jnp.bfloat16).reshape(seq_count, cell_count, gene_count)
    )
    enc_share = lax.psum_scatter(inner(express, grad_h0), "blk", scatter_dimension=0, tiled=True)
    shares = (
        lax.psum_scatter(grad_w_qkv, "blk", scatter_dimension=0, tiled=True),
        lax.psum_scatter(grad_w_out, "blk", scatter_dimension=0, tiled=True),
        lax.psum_scatter(grad_w_up, "blk", scatter_dimension=0, tiled=True),
        lax.psum_scatter(grad_w_down, "blk", scatter_dimension=0, tiled=True),
        lax.psum_scatter(grad_dec, "blk", scatter_dimension=0, tiled=True),
        lax.psum_scatter(grad_bias, "blk", scatter_dimension=0, tiled=True),
        lax.psum_scatter(grad_gain_one, "blk", scatter_dimension=0, tiled=True),
        lax.psum_scatter(grad_shift_one, "blk", scatter_dimension=0, tiled=True),
        lax.psum_scatter(grad_gain_two, "blk", scatter_dimension=0, tiled=True),
        lax.psum_scatter(grad_shift_two, "blk", scatter_dimension=0, tiled=True),
    )
    summed = (
        lax.psum(enc_share.astype(jnp.bfloat16), "dp").astype(jnp.float32),
        lax.psum(shares[0].astype(jnp.bfloat16), "dp").astype(jnp.float32),
        lax.psum(shares[1].astype(jnp.bfloat16), "dp").astype(jnp.float32),
        lax.psum(shares[2].astype(jnp.bfloat16), "dp").astype(jnp.float32),
        lax.psum(shares[3].astype(jnp.bfloat16), "dp").astype(jnp.float32),
        lax.psum(shares[4].astype(jnp.bfloat16), "dp").astype(jnp.float32),
        lax.psum(shares[5].astype(jnp.bfloat16), "dp").astype(jnp.float32),
        lax.psum(shares[6].astype(jnp.bfloat16), "dp").astype(jnp.float32),
        lax.psum(shares[7].astype(jnp.bfloat16), "dp").astype(jnp.float32),
        lax.psum(shares[8].astype(jnp.bfloat16), "dp").astype(jnp.float32),
        lax.psum(shares[9].astype(jnp.bfloat16), "dp").astype(jnp.float32),
    )
    return (
        logits.reshape(seq_count, cell_count, gene_count),
        input_grad,
        summed[0],
        summed[1],
        summed[2],
        summed[3],
        summed[4],
        summed[5],
        summed[6],
        summed[7],
        summed[8],
        summed[9],
        summed[10],
    )


AXES = ("y", "core", "z", "x")
SPLIT = 64


class Place:
    def __init__(self, sizes):
        self.sizes = sizes
        self.y, self.core, self.z, self.x = (lax.axis_index(name) for name in AXES)

    def send(self, value, move):
        ny, nc, nz, nx = self.sizes

        def flat(place):
            y, c, z, x = place
            return ((y * nc + c) * nz + z) * nx + x

        everywhere = [
            (y, c, z, x) for y in range(ny) for c in range(nc) for z in range(nz) for x in range(nx)
        ]
        return lax.ppermute(value, AXES, [(flat(p), flat(move(*p))) for p in everywhere])

    def swap_core(self, value):
        return self.send(value, lambda y, c, z, x: (y, 1 - c, z, x))

    def swap_x(self, value):
        return self.send(value, lambda y, c, z, x: (y, c, z, 1 - x))

    def swap_y(self, value):
        return self.send(value, lambda y, c, z, x: (1 - y, c, z, x))

    def shift_z(self, value, step):
        nz = self.sizes[2]
        return self.send(value, lambda y, c, z, x: (y, c, (z + step) % nz, x))

    def to_group(self, value):
        low = self.z % 2 == 0
        first = self.send(
            jnp.where(low, value[0], value[1]), lambda y, c, z, x: (y, z // 2, 2 * c + z % 2, x)
        )
        second = self.send(
            jnp.where(low, value[1], value[0]),
            lambda y, c, z, x: (y, z // 2, 2 * c + 1 - z % 2, x),
        )
        return first, second

    def from_group(self, value):
        first, second = self.to_group_raw(value)
        low = self.z % 2 == 0
        return jnp.stack([jnp.where(low, first, second), jnp.where(low, second, first)])

    def to_group_raw(self, value):
        first = self.send(value[0], lambda y, c, z, x: (y, z // 2, 2 * c + z % 2, x))
        second = self.send(value[1], lambda y, c, z, x: (y, z // 2, 2 * c + 1 - z % 2, x))
        return first, second

    def whole_group(self, value):
        half = jnp.concatenate([value, self.swap_x(value)], axis=0)
        return jnp.concatenate([half, self.swap_core(half)], axis=0)

    def sum_group(self, part):
        half = part.shape[0] // 2
        low = part.astype(jnp.bfloat16)
        mine = (part[:half] + self.swap_core(low[half:]).astype(jnp.float32)).astype(jnp.bfloat16)
        other = self.swap_x(mine)
        quarter = half // 2
        other = jnp.concatenate([other[quarter:], other[:quarter]], axis=0)
        return mine.astype(jnp.float32) + other.astype(jnp.float32)


def in_order(index, mine, other):
    return jnp.where(index == 0, jnp.stack([mine, other]), jnp.stack([other, mine]))


def after(value, *earlier):
    return lax.optimization_barrier((value, *earlier))[0]


def coordinates():
    return tuple(lax.axis_index(name) for name in AXES)


def lay_out(pieces, out_shape, copies, dtype=jnp.bfloat16):
    def kernel(*refs):
        sources, target = refs[:-1], refs[-1]
        for piece, rows, columns, row, column in copies(*coordinates()):
            size = rows[1] - rows[0]
            width = columns[1] - columns[0]
            part = sources[piece][rows[0] : rows[1], columns[0] : columns[1]].astype(dtype)
            if not isinstance(row, int):
                row = pl.multiple_of(row, 16)
            if not isinstance(column, int):
                column = pl.multiple_of(column, 128)
            target[pl.ds(row, size), pl.ds(column, width)] = part

    return in_vmem(kernel, out_shape, 0, 0, *pieces, dtype=dtype)


def own_part(group, core, x, head):
    pair = jnp.where(x == 0, group[:, : 2 * head], group[:, 2 * head :])
    return jnp.where(core == 0, pair[:, :head], pair[:, head:])


def own_columns(value, first, count, head, flip_x=False, flip_core=False):
    def kernel(value_ref, out_ref):
        _, core, _, x = coordinates()
        core, x = (1 - core if flip_core else core), (1 - x if flip_x else x)
        for number in range(count):
            at = first + number * 4 * head
            part = own_part(value_ref[:, at : at + 4 * head], core, x, head)
            out_ref[:, number * head : (number + 1) * head] = part

    return in_vmem(kernel, (value.shape[0], count * head), 0, 0, value)


def dot(left, right):
    return jnp.dot(left, right, preferred_element_type=jnp.float32)


def soft(queries, keys, allowed, scaling):
    scores = times_t(queries, keys) * scaling
    scores = jnp.where(allowed, scores, NEGATIVE)
    expo = jnp.exp(scores - jnp.max(scores, axis=-1, keepdims=True))
    return expo / jnp.sum(expo, axis=-1, keepdims=True)


def attend_kernel(heads, size, qkv_ref, column_ref, row_ref, out_ref):
    width = heads * size
    allowed = column_ref[...] == row_ref[...]
    for head in range(heads):
        at = head * size
        queries = qkv_ref[:, at : at + size]
        keys = qkv_ref[:, width + at : width + at + size]
        values = qkv_ref[:, 2 * width + at : 2 * width + at + size]
        probs = soft(queries, keys, allowed, size**-0.5)
        out_ref[:, at : at + size] = dot(probs.astype(jnp.bfloat16), values).astype(jnp.bfloat16)


def attend_back_kernel(heads, size, qkv_ref, grad_ref, column_ref, row_ref, out_ref):
    width = heads * size
    allowed = column_ref[...] == row_ref[...]
    for head in range(heads):
        at = head * size
        queries = qkv_ref[:, at : at + size]
        keys = qkv_ref[:, width + at : width + at + size]
        values = qkv_ref[:, 2 * width + at : 2 * width + at + size]
        grad = grad_ref[:, at : at + size]
        probs = soft(queries, keys, allowed, size**-0.5)
        dprob = times_t(grad, values)
        weighted = probs * dprob
        delta = jnp.sum(weighted, axis=-1, keepdims=True)
        dscore = (weighted - probs * delta).astype(jnp.bfloat16)
        grad_queries = dot(dscore, keys) * size**-0.5
        grad_keys = inner(dscore, queries) * size**-0.5
        grad_values = inner(probs.astype(jnp.bfloat16), grad)
        out_ref[:, at : at + size] = grad_queries.astype(jnp.bfloat16)
        out_ref[:, width + at : width + at + size] = grad_keys.astype(jnp.bfloat16)
        out_ref[:, 2 * width + at : 2 * width + at + size] = grad_values.astype(jnp.bfloat16)


def in_vmem(kernel, out_shape, flops, transcendentals, *operands, dtype=jnp.bfloat16):
    whole = pl.BlockSpec(memory_space=pltpu.VMEM)
    return pl.pallas_call(
        kernel,
        out_shape=jax.ShapeDtypeStruct(out_shape, dtype),
        in_specs=[whole] * len(operands),
        out_specs=whole,
        compiler_params=pltpu.CompilerParams(vmem_limit_bytes=40 * 1024 * 1024),
        cost_estimate=pl.CostEstimate(
            flops=flops, bytes_accessed=4 * math.prod(out_shape), transcendentals=transcendentals
        ),
    )(*operands)


def sinusoids_of_whole(coords, width):
    quarter = width // 4
    frequency = jnp.exp(jnp.arange(quarter, dtype=jnp.float32) * (-math.log(10000.0) / quarter))
    number = jnp.arange(32, dtype=jnp.float32)[:, None]
    far, near = 32.0 * number * frequency, number * frequency
    far = jnp.concatenate([jnp.sin(far), jnp.cos(far)], axis=1)
    near = jnp.concatenate([jnp.sin(near), jnp.cos(near)], axis=1)
    parts = []
    for coord in coords:
        whole = coord.astype(jnp.int32)
        pick_far = (whole // 32 == jnp.arange(32)[None, :]).astype(jnp.float32)
        pick_near = (whole % 32 == jnp.arange(32)[None, :]).astype(jnp.float32)
        at_far = jnp.dot(pick_far, far, precision=lax.Precision.HIGHEST)
        at_near = jnp.dot(pick_near, near, precision=lax.Precision.HIGHEST)
        sin_far, cos_far = at_far[:, :quarter], at_far[:, quarter:]
        sin_near, cos_near = at_near[:, :quarter], at_near[:, quarter:]
        parts.append(sin_far * cos_near + cos_far * sin_near)
        parts.append(cos_far * cos_near - sin_far * sin_near)
    return jnp.concatenate(parts, axis=1)


def normalise(inputs):
    centre = inputs - jnp.mean(inputs, axis=-1, keepdims=True)
    factor = lax.rsqrt(jnp.mean(centre * centre, axis=-1, keepdims=True) + EPSILON)
    return centre * factor, factor


def normalise_back(grad, normal, factor, gain):
    scaled = grad * gain
    inside = (
        scaled
        - jnp.mean(scaled, axis=-1, keepdims=True)
        - normal * jnp.mean(scaled * normal, axis=-1, keepdims=True)
    )
    return factor * inside, jnp.stack([jnp.sum(grad * normal, axis=0), jnp.sum(grad, axis=0)])


def grouped_plan(
    sizes,
    counts,
    coords,
    segment_ids,
    logit_grad,
    enc_weight,
    qkv_weight,
    out_weight,
    up_weight,
    down_weight,
    dec_weight,
    dec_bias,
    norm1_gain,
    norm1_shift,
    norm2_gain,
    norm2_shift,
):
    place = Place(sizes)
    nz = sizes[2]
    seqs, cells, genes = counts.shape
    width = enc_weight.shape[1]
    block = enc_weight.shape[0]
    head = width // HEADS
    heads = HEADS // 4
    slice_width = width // 4
    own_rows = seqs * cells
    rows = 4 * own_rows
    ff = up_weight.shape[1]
    ff_slice = ff // 4
    bf16, f32 = jnp.bfloat16, jnp.float32

    def pick(value, axis, index):
        return lax.dynamic_index_in_dim(value, index, axis, keepdims=False)

    half, quarter = block // 2, block // 4
    three = 3 * slice_width

    vectors = jnp.stack([dec_bias, norm1_gain, norm1_shift, norm2_gain, norm2_shift])
    tall = half + 16

    def enc_kernel(enc_ref, vectors_ref, out_ref):
        _, core, _, _ = coordinates()
        out_ref[:half, :] = enc_ref[pl.ds(pl.multiple_of(core * half, 16), half), :]
        out_ref[half:, :] = jnp.zeros((16, width), bf16)
        out_ref[half : half + 5, :block] = vectors_ref[...]

    enc_own = in_vmem(enc_kernel, (tall, width), 0, 0, enc_weight, vectors)
    enc_near = [enc_own] + [place.shift_z(enc_own, k) for k in range(1, nz)]
    enc_pieces = enc_near + [place.swap_x(part) for part in enc_near]

    express = jnp.log1p(counts.astype(f32)).astype(bf16)
    whole = jnp.stack([coords[0], coords[1], segment_ids], axis=-1)
    beside = jnp.concatenate([whole // SPLIT, whole % SPLIT], axis=-1).astype(bf16)
    beside = jnp.pad(beside, ((0, 0), (0, 0), (0, 122)))
    first, second = place.to_group(jnp.concatenate([express, beside], axis=-1))
    cell_rows = place.whole_group(jnp.concatenate([first, second], axis=0))
    express = cell_rows[:, :genes]
    beside = cell_rows[:, genes:].astype(f32)
    beside = beside[:, :3] * SPLIT + beside[:, 3:6]
    segment = beside[:, 2:3]
    segment_row = segment.reshape(1, rows)
    embed = sinusoids_of_whole((beside[:, 0:1], beside[:, 1:2]), width)

    qkv_mine = own_columns(qkv_weight, 0, 3 * nz, head)
    qkv_theirs = own_columns(qkv_weight, 0, 3 * nz, head, flip_x=True)

    def rows_kernel(value_ref, out_ref):
        y, _, _, _ = coordinates()
        out_ref[...] = value_ref[pl.ds(pl.multiple_of(y * half, 16), half), :]

    qkv_theirs = place.swap_x(in_vmem(rows_kernel, (half, three), 0, 0, qkv_theirs))

    def qkv_kernel(mine_ref, theirs_ref, out_weight_ref, out_ref):
        y, core, _, _ = coordinates()
        out_ref[:half, :three] = mine_ref[pl.ds(pl.multiple_of(y * half, 16), half), :]
        out_ref[half:, :three] = theirs_ref[...]
        at = pl.multiple_of(core * half + y * quarter, 16)
        for j in range(4):
            out_ref[j * quarter : (j + 1) * quarter, three:] = out_weight_ref[
                pl.ds(at, quarter), j * slice_width : (j + 1) * slice_width
            ]

    qkv_own = in_vmem(qkv_kernel, (block, width), 0, 0, qkv_mine, qkv_theirs, out_weight)
    qkv_own = after(qkv_own, *enc_near[1:])
    near = [qkv_own] + [place.shift_z(qkv_own, k) for k in range(1, nz)]
    far = [place.swap_y(part) for part in near]

    lanes = ff // (8 * nz)
    up_half = nz * lanes

    def up_columns(up_ref, out_ref, x):
        y, core, _, _ = coordinates()
        for number in range(nz):
            at = ((2 * number + x) * 2 + core) * 2 + y
            out_ref[:block, number * lanes : (number + 1) * lanes] = up_ref[
                :, pl.ds(pl.multiple_of(at * lanes, lanes), lanes)
            ]

    def dec_rows(dec_ref):
        y, core, _, _ = coordinates()
        return dec_ref[pl.ds(pl.multiple_of(core * half + y * quarter, 16), quarter), :]

    def up_theirs_kernel(up_ref, dec_ref, out_ref):
        _, _, _, x = coordinates()
        up_columns(up_ref, out_ref, 1 - x)
        part = dec_rows(dec_ref)
        out_ref[block : block + quarter, :] = part[:, :up_half]
        out_ref[block + quarter :, :] = part[:, up_half:]

    up_theirs = in_vmem(up_theirs_kernel, (block + half, up_half), 0, 0, up_weight, dec_weight)
    up_theirs = place.swap_x(up_theirs)
    many = down_weight.shape[0] // 4
    dec_at = block + many

    def up_kernel(up_ref, theirs_ref, down_ref, dec_ref, out_ref):
        y, core, _, x = coordinates()
        up_columns(up_ref, out_ref, x)
        out_ref[:block, up_half:] = theirs_ref[:block, :]
        out_ref[block:dec_at, :] = down_ref[
            pl.ds(pl.multiple_of((2 * core + y) * many, 16), many), :
        ]
        out_ref[dec_at : dec_at + quarter, :] = dec_rows(dec_ref)
        out_ref[dec_at + quarter :, :up_half] = theirs_ref[block : block + quarter, :]
        out_ref[dec_at + quarter :, up_half:] = theirs_ref[block + quarter :, :]

    up_own = in_vmem(
        up_kernel, (dec_at + half, width), 0, 0, up_weight, up_theirs, down_weight, dec_weight
    )
    up_near, up_far = [after(up_own, *near[1:])], []
    for k in range(1, nz):
        up_far.append(place.swap_y(up_near[-1]))
        up_near.append(place.shift_z(after(up_near[-1], *up_far[k - 2 : k - 1]), 1))
    up_far.append(place.swap_y(up_near[-1]))
    up_pieces = up_near + up_far

    def enc_copies(y, core, z, x):
        return [
            (dx * nz + k, (0, half), (0, width), (2 * ((z - k) % nz) + (x ^ dx)) * half, 0)
            for dx in range(2) for k in range(nz)
        ]

    def vector_copies(y, core, z, x):
        return [
            (dx * nz + k, (half, tall), (0, block), 0, (2 * ((z - k) % nz) + (x ^ dx)) * block)
            for dx in range(2) for k in range(nz)
        ]

    def both_cores(count):
        def copies(y, core, z, x):
            return [
                (dc, (k * half, (k + 1) * half), (0, width), k * block + (core ^ dc) * half, 0)
                for dc in range(2) for k in range(count)
            ]

        return copies

    enc_half = lay_out(enc_pieces, (genes // 2, width), enc_copies)
    w_enc = lay_out((enc_half, place.swap_core(enc_half)), (genes, width), both_cores(2 * nz))
    vectors = lay_out(enc_pieces, (16, width), vector_copies, dtype=f32)
    b_dec, gain_one, shift_one, gain_two, shift_two = (vectors[i : i + 1] for i in range(5))

    def qkv_copies(y, core, z, x):
        return [
            (dy * nz + k, (dx * half, (dx + 1) * half), (0, three),
             (2 * ((z - k) % nz) + (x ^ dx)) * block + (y ^ dy) * half, 0)
            for k in range(nz) for dy in range(2) for dx in range(2)
        ]

    def out_copies(y, core, z, x):
        return [
            (dy * nz + k, (j * quarter, (j + 1) * quarter), (three, width),
             ((z - k) % nz) * half + (y ^ dy) * quarter, j * slice_width)
            for k in range(nz) for dy in range(2) for j in range(4)
        ]

    w_qkv = lay_out(near + far, (width, three), qkv_copies)
    w_out = lay_out(near + far, (slice_width, width), out_copies)

    def up_copies(y, core, z, x):
        return [
            (dy * nz + k, (0, block), (dx * up_half, (dx + 1) * up_half),
             (2 * ((z - k) % nz) + (x ^ dx)) * block, (y ^ dy) * up_half)
            for k in range(nz) for dy in range(2) for dx in range(2)
        ]

    def down_copies(y, core, z, x):
        return [
            (dy * nz + k, (block, dec_at), (0, width), ((y ^ dy) * nz + ((z - k) % nz)) * many, 0)
            for k in range(nz) for dy in range(2)
        ]

    def dec_copies(y, core, z, x):
        return [
            (dy * nz + k, (dec_at + dx * quarter, dec_at + (dx + 1) * quarter), (0, genes),
             (2 * ((z - k) % nz) + (x ^ dx)) * half + (y ^ dy) * quarter, 0)
            for k in range(nz) for dy in range(2) for dx in range(2)
        ]

    dec_half = lay_out(up_pieces, (width // 2, genes), dec_copies)
    w_dec = lay_out((dec_half, place.swap_core(dec_half)), (width, genes), both_cores(2 * nz))
    w_up = lay_out(up_pieces, (width, ff_slice), up_copies)
    w_down = lay_out(up_pieces, (ff_slice, width), down_copies)

    first, second = place.to_group(logit_grad)
    cotangent = place.whole_group(jnp.concatenate([first, second], axis=0))
    grad_bias = jnp.sum(cotangent.astype(f32), axis=0, keepdims=True)
    grad_h2 = times_t(cotangent, w_dec)
    grad_down = grad_h2.astype(bf16)

    hidden0 = dot(express, w_enc) + embed
    normal1, factor1 = normalise(hidden0)
    normed1 = (normal1 * gain_one + shift_one).astype(bf16)
    qkv = dot(normed1, w_qkv).astype(bf16)
    pairs = heads * rows * rows
    context = in_vmem(
        functools.partial(attend_kernel, heads, head),
        (rows, slice_width), 4 * pairs * head, pairs, qkv, segment, segment_row,
    )
    half_rows = rows // 2
    hidden1 = hidden0[:half_rows] + place.sum_group(dot(context, w_out))
    normal2, factor2 = normalise(hidden1)
    normed2 = (normal2 * gain_two + shift_two).astype(bf16)
    normed2 = jnp.concatenate([normed2, place.swap_core(normed2)], axis=0)
    up_value = dot(normed2, w_up)
    active = jax.nn.gelu(up_value).astype(bf16)
    hidden2 = hidden1 + place.sum_group(dot(active, w_down))
    hidden2 = hidden2.astype(bf16)
    logits = (dot(hidden2[:own_rows], w_dec) + b_dec).astype(bf16)
    logits = place.from_group(logits.reshape(seqs, cells, genes))

    hidden2_slice = jnp.concatenate(
        [
            own_columns(hidden2, 0, nz, half),
            place.swap_core(own_columns(hidden2, 0, nz, half, flip_core=True)),
        ],
        axis=0,
    )
    grad_w_dec = inner(hidden2_slice, cotangent).astype(bf16)
    grad_w_down = inner(active, grad_down).astype(bf16)
    grad_active = times_t(grad_down, w_down)
    grad_up = jax.vjp(jax.nn.gelu, up_value)[1](grad_active)[0].astype(bf16)
    grad_w_up = inner(normed2, grad_up).astype(bf16)
    grad_normed2 = place.sum_group(times_t(grad_up, w_up))
    part_two, sums_two = normalise_back(grad_normed2, normal2, factor2, gain_two)
    grad_h1 = grad_h2[:half_rows] + part_two
    grad_attn = grad_h1.astype(bf16)

    def beside_core(value, sums):
        both = jnp.concatenate([value, jnp.pad(sums.astype(bf16), ((0, 14), (0, 0)))], axis=0)
        other = place.swap_core(both)
        return (
            jnp.concatenate([value, other[:half_rows]], axis=0),
            sums + other[half_rows : half_rows + 2].astype(f32),
        )

    grad_attn, sums_two = beside_core(grad_attn, sums_two)
    grad_w_out = inner(context, grad_attn).astype(bf16)
    grad_context = times_t(grad_attn, w_out).astype(bf16)
    grad_qkv = in_vmem(
        functools.partial(attend_back_kernel, heads, head),
        (rows, 3 * slice_width), 10 * pairs * head, pairs, qkv, grad_context, segment, segment_row,
    )
    grad_w_qkv = inner(normed1, grad_qkv).astype(bf16)
    grad_normed1 = place.sum_group(times_t(grad_qkv, w_qkv))
    part_one, sums_one = normalise_back(
        grad_normed1, normal1[:half_rows], factor1[:half_rows], gain_one
    )
    grad_h0 = (grad_h1 + part_one).astype(bf16)
    input_grad = times_t(grad_h0[:own_rows], w_enc).astype(bf16)
    input_grad = place.from_group(input_grad.reshape(seqs, cells, genes))
    grad_h0, sums_one = beside_core(grad_h0, sums_one)
    express_slice = own_columns(cell_rows, 0, nz, half)
    grad_w_enc = inner(express_slice, grad_h0)

    def half_over_y(value):
        parts = value.reshape(nz, 2, value.shape[1] // 2, value.shape[2])
        other = place.swap_y(pick(parts, 1, 1 - place.y))
        return (pick(parts, 1, place.y).astype(f32) + other.astype(f32)).astype(bf16)

    def direct_over_z(value):
        total = pick(value, 0, place.z).astype(f32)
        for k in range(1, nz):
            total += place.shift_z(pick(value, 0, (place.z + k) % nz), k).astype(f32)
        return total

    down_sum = jnp.swapaxes(grad_w_down.reshape(2, nz, many, width), 0, 1)
    down_sum = half_over_y(down_sum.reshape(nz, 2 * many, width))
    down_sum = direct_over_z(down_sum).astype(bf16)
    down_sum = in_order(place.y, down_sum, place.swap_y(down_sum)).reshape(2 * many, width)

    def down_copies_out(y, core, z, x):
        return [
            (dc, (0, 2 * many), (0, width), (core ^ dc) * 2 * many, 0) for dc in range(2)
        ]

    out_down = lay_out(
        (down_sum, place.swap_core(down_sum)), (4 * many, width), down_copies_out, dtype=f32
    )

    def whole_columns(value):
        value = value.reshape(2, block, value.shape[-1])
        mine = pick(value, 0, place.x)
        both = jnp.concatenate([mine, place.swap_x(pick(value, 0, 1 - place.x))], axis=0)
        return both, place.swap_core(both)

    up_sum = half_over_y(grad_w_up.reshape(nz, 2 * block, ff_slice))
    up_sum = direct_over_z(up_sum).astype(bf16)
    up_sum = in_order(place.y, up_sum, place.swap_y(up_sum))

    def up_copies_out(y, core, z, x):
        return [
            (dc, (dx * block, (dx + 1) * block), ((j * nz + k) * lanes, (j * nz + k + 1) * lanes),
             0, (((2 * k + (x ^ dx)) * 2 + (core ^ dc)) * 2 + j) * lanes)
            for dc in range(2) for dx in range(2) for j in range(2) for k in range(nz)
        ]

    out_up = lay_out(whole_columns(up_sum), (block, ff), up_copies_out, dtype=f32)

    few = jnp.concatenate(
        [grad_w_out.reshape(nz, half, width), grad_w_dec.reshape(nz, half, genes)], axis=1
    )
    few = direct_over_z(half_over_y(few)).astype(bf16)
    few = in_order(place.y, few, place.swap_y(few)).reshape(block, width)

    def half_copies_out(first):
        def copies(y, core, z, x):
            return [
                (dc, (first, first + half), (0, width), (core ^ dc) * half, 0) for dc in range(2)
            ]

        return copies

    few = (few, place.swap_core(few))
    out_out = lay_out(few, (block, width), half_copies_out(0), dtype=f32)
    out_dec = lay_out(few, (block, genes), half_copies_out(half), dtype=f32)

    qkv_sum = half_over_y(grad_w_qkv.reshape(nz, 2 * block, three))
    qkv_sum = direct_over_z(qkv_sum).astype(bf16)
    qkv_sum = in_order(place.y, qkv_sum, place.swap_y(qkv_sum))

    def qkv_out_kernel(near_ref, far_ref, out_ref):
        _, core, _, x = coordinates()
        for dx in range(2):
            for number in range(3 * nz):
                at = slice(dx * block, (dx + 1) * block), slice(number * head, (number + 1) * head)
                near_part, far_part = near_ref[at].astype(f32), far_ref[at].astype(f32)
                low = jnp.where(core == 0, near_part, far_part)
                high = jnp.where(core == 0, far_part, near_part)
                column = pl.multiple_of(number * 4 * head + (x ^ dx) * 2 * head, 2 * head)
                out_ref[:, pl.ds(column, 2 * head)] = jnp.concatenate([low, high], axis=1)

    out_qkv = in_vmem(
        qkv_out_kernel, (block, 3 * width), 0, 0, *whole_columns(qkv_sum), dtype=f32
    )

    sums = jnp.concatenate([grad_bias, sums_one, sums_two], axis=0).reshape(5, nz, 2, block)
    sums = pick(sums, 2, place.x).transpose(1, 0, 2)
    sums = jnp.pad(sums, ((0, 0), (0, 11), (0, width - block)))
    last = jnp.concatenate([grad_w_enc.reshape(nz, half, width), sums], axis=1).astype(bf16)
    last = direct_over_z(last)
    last = last + place.swap_y(last.astype(bf16)).astype(f32)
    sums = last[half : half + 5, :block]
    last = last[:half].astype(bf16)
    out_enc = lay_out(
        (last, place.swap_core(last)), (block, width), half_copies_out(0), dtype=f32
    )
    return (
        logits, input_grad, out_enc, out_qkv, out_out, out_up, out_down, out_dec,
        sums[0], sums[1], sums[2], sums[3], sums[4],
    )


IN_SPECS = (
    ("dp", "blk", None), (None, "dp", "blk"), ("dp", "blk"), ("dp", "blk", None),
    *[("blk", None)] * 6, *[("blk",)] * 5,
)
OUT_SPECS = (("dp", "blk", None), ("dp", "blk", None), *[("blk", None)] * 6, *[("blk",)] * 5)


def solution(mesh):
    groups, blocks = mesh.shape["dp"], mesh.shape["blk"]

    def run(*args):
        seqs = args[0].shape[0] // groups
        if groups == 4 and blocks == 4 * seqs and seqs == 2 and HEADS == 4 * (blocks // 2):
            sizes = (groups // 2, 2, blocks // 2, 2)
            fine = Mesh(mesh.devices.reshape(sizes), AXES)
            names = {"dp": ("y", "core"), "blk": ("z", "x"), None: None}
            plan = functools.partial(grouped_plan, sizes)
        else:
            fine, names, plan = mesh, {"dp": "dp", "blk": "blk", None: None}, spread_plan
        specs = lambda entries: tuple(P(*[names[axis] for axis in entry]) for entry in entries)
        return jax.shard_map(
            plan, mesh=fine, in_specs=specs(IN_SPECS), out_specs=specs(OUT_SPECS), check_vma=False
        )(*args)

    return run
```

```python
import functools
import math

import jax
import jax.numpy as jnp
from jax import lax
from jax.experimental import pallas as pl
from jax.experimental.pallas import tpu as pltpu
from jax.sharding import Mesh
from jax.sharding import PartitionSpec as P

HEADS = 16


NEGATIVE = -1e30
EPSILON = 1e-05


def layer_norm(inputs, gain_vec, shift_vec):
    centre = inputs - jnp.mean(inputs, axis=-1, keepdims=True)
    spread = jnp.mean(centre * centre, axis=-1, keepdims=True)
    return centre * lax.rsqrt(spread + EPSILON) * gain_vec + shift_vec


def sinusoids(coords, width):
    quarter = width // 4
    frequency = jnp.exp(jnp.arange(quarter, dtype=jnp.float32) * (-math.log(10000.0) / quarter))
    first_angle = coords[0].astype(jnp.float32)[..., None] * frequency
    second_angle = coords[1].astype(jnp.float32)[..., None] * frequency
    return jnp.concatenate(
        [jnp.sin(first_angle), jnp.cos(first_angle), jnp.sin(second_angle), jnp.cos(second_angle)],
        axis=-1,
    )


def inner(left, right):
    return lax.dot_general(
        left, right, (((0,), (0,)), ((), ())), preferred_element_type=jnp.float32
    )


def times_t(left, right):
    return lax.dot_general(
        left, right, (((1,), (1,)), ((), ())), preferred_element_type=jnp.float32
    )


def spread_plan(
    counts,
    coords,
    segment_ids,
    logit_grad,
    enc_weight,
    qkv_weight,
    out_weight,
    up_weight,
    down_weight,
    dec_weight,
    dec_bias,
    norm1_gain,
    norm1_shift,
    norm2_gain,
    norm2_shift,
):
    gathered = (
        lax.all_gather(enc_weight, "blk", axis=0, tiled=True),
        lax.all_gather(qkv_weight, "blk", axis=0, tiled=True),
        lax.all_gather(out_weight, "blk", axis=0, tiled=True),
        lax.all_gather(up_weight, "blk", axis=0, tiled=True),
        lax.all_gather(down_weight, "blk", axis=0, tiled=True),
        lax.all_gather(dec_weight, "blk", axis=0, tiled=True),
        lax.all_gather(dec_bias, "blk", axis=0, tiled=True),
        lax.all_gather(norm1_gain, "blk", axis=0, tiled=True),
        lax.all_gather(norm1_shift, "blk", axis=0, tiled=True),
        lax.all_gather(norm2_gain, "blk", axis=0, tiled=True),
        lax.all_gather(norm2_shift, "blk", axis=0, tiled=True),
    )
    w_enc, w_qkv, w_out, w_up, w_down, w_dec, b_dec, gain_one, shift_one, gain_two, shift_two = (
        gathered
    )
    seg_all = lax.all_gather(segment_ids, "blk", axis=1, tiled=True)
    seq_count, cell_count, gene_count = counts.shape
    width = w_enc.shape[1]
    head_count = HEADS
    head_size = width // head_count
    scaling = head_size ** (-0.5)
    row_count = seq_count * cell_count
    express = (
        jnp.log1p(counts.astype(jnp.float32)).astype(jnp.bfloat16).reshape(row_count, gene_count)
    )
    embed = sinusoids(coords, width).reshape(row_count, width)
    hidden0 = jnp.dot(express, w_enc, preferred_element_type=jnp.float32) + embed
    gain_one32 = gain_one.astype(jnp.float32)
    shift_one32 = shift_one.astype(jnp.float32)
    gain_two32 = gain_two.astype(jnp.float32)
    shift_two32 = shift_two.astype(jnp.float32)
    normed1 = layer_norm(hidden0, gain_one32, shift_one32).astype(jnp.bfloat16)
    qkv = jnp.dot(normed1, w_qkv, preferred_element_type=jnp.float32).astype(jnp.bfloat16)
    queries = qkv[:, :width].reshape(seq_count, cell_count, head_count, head_size)
    key_rows = qkv[:, width : 2 * width].reshape(seq_count, cell_count, head_count, head_size)
    values = qkv[:, 2 * width :].reshape(seq_count, cell_count, head_count, head_size)

    def masked_scores(query_part, key_part, seg_query, seg_key):
        scores = (
            jnp.einsum("sqhe,skhe->shqk", query_part, key_part, preferred_element_type=jnp.float32)
            * scaling
        )
        return jnp.where(seg_query[:, None, :, None] == seg_key[:, None, None, :], scores, NEGATIVE)

    start_max = jnp.full((seq_count, head_count, cell_count), NEGATIVE, jnp.float32)
    piece = (
        lax.all_gather(key_rows, "blk", axis=1, tiled=True),
        lax.all_gather(values, "blk", axis=1, tiled=True),
    )
    seg_part = seg_all
    incoming = (piece[0], piece[1], seg_part)
    running_max = start_max
    key_part, value_part, context_seg_part = incoming
    query_part = queries
    scores = masked_scores(query_part, key_part, segment_ids, context_seg_part)
    newest = jnp.maximum(running_max, jnp.max(scores, axis=-1))
    expo = jnp.exp(scores - newest[..., None])
    running_sum = jnp.sum(expo, axis=-1)
    update = jnp.einsum(
        "shqk,skhe->sqhe", expo.astype(jnp.bfloat16), value_part, preferred_element_type=jnp.float32
    )
    weighted = update
    running_max, running_sum, weighted = (newest, running_sum, weighted)
    context32 = weighted / jnp.transpose(running_sum, (0, 2, 1))[..., None]
    logsum = jnp.transpose(running_max + jnp.log(running_sum), (0, 2, 1))
    context = context32.astype(jnp.bfloat16).reshape(row_count, width)
    hidden1 = hidden0 + jnp.dot(context, w_out, preferred_element_type=jnp.float32)
    normed2 = layer_norm(hidden1, gain_two32, shift_two32).astype(jnp.bfloat16)
    up_value = jnp.dot(normed2, w_up, preferred_element_type=jnp.float32)
    active = jax.nn.gelu(up_value).astype(jnp.bfloat16)
    hidden2 = hidden1 + jnp.dot(active, w_down, preferred_element_type=jnp.float32)
    hidden2_low = hidden2.astype(jnp.bfloat16)
    logits = (
        jnp.dot(hidden2_low, w_dec, preferred_element_type=jnp.float32) + b_dec.astype(jnp.float32)
    ).astype(jnp.bfloat16)
    cotangent = logit_grad.reshape(row_count, gene_count)
    grad_dec = inner(hidden2_low, cotangent)
    grad_bias = jnp.sum(cotangent.astype(jnp.float32), axis=0)
    grad_h2 = times_t(cotangent, w_dec)
    grad_down = grad_h2.astype(jnp.bfloat16)
    grad_w_down = inner(active, grad_down)
    grad_active = times_t(grad_down, w_down)
    gelu_pull = jax.vjp(jax.nn.gelu, up_value)[1]
    grad_up = gelu_pull(grad_active)[0].astype(jnp.bfloat16)
    grad_w_up = inner(normed2, grad_up)
    grad_normed2 = times_t(grad_up, w_up)
    norm_pull_two = jax.vjp(layer_norm, hidden1, gain_two32, shift_two32)[1]
    part_two, grad_gain_two, grad_shift_two = norm_pull_two(grad_normed2)
    grad_h1 = grad_h2 + part_two
    grad_attn = grad_h1.astype(jnp.bfloat16)
    grad_w_out = inner(context, grad_attn)
    grad_context = (
        times_t(grad_attn, w_out)
        .astype(jnp.bfloat16)
        .reshape(seq_count, cell_count, head_count, head_size)
    )
    delta = jnp.sum(grad_context.astype(jnp.float32) * context32, axis=-1)
    logsum_all, delta_all = (
        lax.all_gather(logsum, "blk", axis=1, tiled=True),
        lax.all_gather(delta, "blk", axis=1, tiled=True),
    )
    seg_part = seg_all
    query_seg_part = seg_part
    query_part = queries
    gradout_part = grad_context
    logsum_part = logsum
    delta_part = delta
    scores = masked_scores(query_part, key_part, segment_ids, query_seg_part)
    probs = jnp.exp(scores - jnp.transpose(logsum_part, (0, 2, 1))[..., None])
    dprob = jnp.einsum(
        "sqhe,skhe->shqk", gradout_part, value_part, preferred_element_type=jnp.float32
    )
    dscore = (probs * (dprob - jnp.transpose(delta_part, (0, 2, 1))[..., None])).astype(
        jnp.bfloat16
    )
    grad_queries = (
        jnp.einsum("shqk,skhe->sqhe", dscore, key_part, preferred_element_type=jnp.float32)
        * scaling
    )
    piece = (
        lax.all_gather(queries, "blk", axis=1, tiled=True),
        lax.all_gather(grad_context, "blk", axis=1, tiled=True),
    )
    seg_part = seg_all
    logsum_part = logsum_all
    delta_part = delta_all
    incoming = (piece[0], piece[1], logsum_part, delta_part, seg_part)
    query_part, gradout_part, key_logsum_part, key_delta_part, key_seg_part = incoming
    key_part = key_rows
    scores = masked_scores(query_part, key_part, key_seg_part, segment_ids)
    probs = jnp.exp(scores - jnp.transpose(key_logsum_part, (0, 2, 1))[..., None])
    grad_values = jnp.einsum(
        "shqk,sqhe->skhe",
        probs.astype(jnp.bfloat16),
        gradout_part,
        preferred_element_type=jnp.float32,
    )
    dprob = jnp.einsum("sqhe,skhe->shqk", gradout_part, values, preferred_element_type=jnp.float32)
    dscore = (probs * (dprob - jnp.transpose(key_delta_part, (0, 2, 1))[..., None])).astype(
        jnp.bfloat16
    )
    grad_keys = (
        jnp.einsum("shqk,sqhe->skhe", dscore, query_part, preferred_element_type=jnp.float32)
        * scaling
    )
    grad_keys, grad_values = (grad_keys, grad_values)
    grad_qkv = jnp.concatenate(
        [
            grad_queries.reshape(row_count, width),
            grad_keys.reshape(row_count, width),
            grad_values.reshape(row_count, width),
        ],
        axis=1,
    ).astype(jnp.bfloat16)
    grad_w_qkv = inner(normed1, grad_qkv)
    grad_normed1 = times_t(grad_qkv, w_qkv)
    norm_pull_one = jax.vjp(layer_norm, hidden0, gain_one32, shift_one32)[1]
    part_one, grad_gain_one, grad_shift_one = norm_pull_one(grad_normed1)
    grad_h0 = (grad_h1 + part_one).astype(jnp.bfloat16)
    input_grad = (
        times_t(grad_h0, w_enc).astype(jnp.bfloat16).reshape(seq_count, cell_count, gene_count)
    )
    enc_share = lax.psum_scatter(inner(express, grad_h0), "blk", scatter_dimension=0, tiled=True)
    shares = (
        lax.psum_scatter(grad_w_qkv, "blk", scatter_dimension=0, tiled=True),
        lax.psum_scatter(grad_w_out, "blk", scatter_dimension=0, tiled=True),
        lax.psum_scatter(grad_w_up, "blk", scatter_dimension=0, tiled=True),
        lax.psum_scatter(grad_w_down, "blk", scatter_dimension=0, tiled=True),
        lax.psum_scatter(grad_dec, "blk", scatter_dimension=0, tiled=True),
        lax.psum_scatter(grad_bias, "blk", scatter_dimension=0, tiled=True),
        lax.psum_scatter(grad_gain_one, "blk", scatter_dimension=0, tiled=True),
        lax.psum_scatter(grad_shift_one, "blk", scatter_dimension=0, tiled=True),
        lax.psum_scatter(grad_gain_two, "blk", scatter_dimension=0, tiled=True),
        lax.psum_scatter(grad_shift_two, "blk", scatter_dimension=0, tiled=True),
    )
    summed = (
        lax.psum(enc_share.astype(jnp.bfloat16), "dp").astype(jnp.float32),
        lax.psum(shares[0].astype(jnp.bfloat16), "dp").astype(jnp.float32),
        lax.psum(shares[1].astype(jnp.bfloat16), "dp").astype(jnp.float32),
        lax.psum(shares[2].astype(jnp.bfloat16), "dp").astype(jnp.float32),
        lax.psum(shares[3].astype(jnp.bfloat16), "dp").astype(jnp.float32),
        lax.psum(shares[4].astype(jnp.bfloat16), "dp").astype(jnp.float32),
        lax.psum(shares[5].astype(jnp.bfloat16), "dp").astype(jnp.float32),
        lax.psum(shares[6].astype(jnp.bfloat16), "dp").astype(jnp.float32),
        lax.psum(shares[7].astype(jnp.bfloat16), "dp").astype(jnp.float32),
        lax.psum(shares[8].astype(jnp.bfloat16), "dp").astype(jnp.float32),
        lax.psum(shares[9].astype(jnp.bfloat16), "dp").astype(jnp.float32),
    )
    return (
        logits.reshape(seq_count, cell_count, gene_count),
        input_grad,
        summed[0],
        summed[1],
        summed[2],
        summed[3],
        summed[4],
        summed[5],
        summed[6],
        summed[7],
        summed[8],
        summed[9],
        summed[10],
    )


AXES = ("y", "core", "z", "x")
SPLIT = 64


class Place:
    def __init__(self, sizes):
        self.sizes = sizes
        self.y, self.core, self.z, self.x = (lax.axis_index(name) for name in AXES)

    def send(self, value, move):
        ny, nc, nz, nx = self.sizes

        def flat(place):
            y, c, z, x = place
            return ((y * nc + c) * nz + z) * nx + x

        everywhere = [
            (y, c, z, x) for y in range(ny) for c in range(nc) for z in range(nz) for x in range(nx)
        ]
        return lax.ppermute(value, AXES, [(flat(p), flat(move(*p))) for p in everywhere])

    def swap_core(self, value):
        return self.send(value, lambda y, c, z, x: (y, 1 - c, z, x))

    def swap_x(self, value):
        return self.send(value, lambda y, c, z, x: (y, c, z, 1 - x))

    def swap_y(self, value):
        return self.send(value, lambda y, c, z, x: (1 - y, c, z, x))

    def shift_z(self, value, step):
        nz = self.sizes[2]
        return self.send(value, lambda y, c, z, x: (y, c, (z + step) % nz, x))

    def swap_z(self, value, distance):
        return self.send(value, lambda y, c, z, x: (y, c, z ^ distance, x))

    def exchange_z(self, value):
        return lax.all_to_all(value, "z", split_axis=0, concat_axis=0, tiled=True)

    def regroup(self, first, second):
        return (
            self.send(first, lambda y, c, z, x: (y, z // 2, 2 * c + z % 2, x)),
            self.send(second, lambda y, c, z, x: (y, z // 2, 2 * c + 1 - z % 2, x)),
        )

    def by_parity(self, pair):
        even = self.z % 2 == 0
        return jnp.where(even, pair[0], pair[1]), jnp.where(even, pair[1], pair[0])


def after(value, *earlier):
    return lax.optimization_barrier((value, *earlier))[0]


def coordinates():
    return tuple(lax.axis_index(name) for name in AXES)


def put(target, row, column, part):
    if not isinstance(row, int):
        row = pl.multiple_of(row, 16)
    if not isinstance(column, int):
        column = pl.multiple_of(column, 128)
    target[pl.ds(row, part.shape[0]), pl.ds(column, part.shape[1])] = part.astype(target.dtype)


def rows_at(source, row, count):
    return source[pl.ds(pl.multiple_of(row, 16), count), :]


def own_part(group, core, x, head):
    pair = jnp.where(x == 0, group[:, : 2 * head], group[:, 2 * head :])
    return jnp.where(core == 0, pair[:, :head], pair[:, head:])


def dot(left, right):
    return jnp.dot(left, right, preferred_element_type=jnp.float32)


def soft(queries, keys, allowed, scaling):
    scores = times_t(queries, keys) * scaling
    scores = jnp.where(allowed, scores, NEGATIVE)
    expo = jnp.exp(scores - jnp.max(scores, axis=-1, keepdims=True))
    return expo / jnp.sum(expo, axis=-1, keepdims=True)


def one_head(ref, part, heads, number, size):
    at = (part * heads + number) * size
    return ref[:, at : at + size]


def in_vmem(kernel, outs, *operands, flops=0, exps=0, scratch=()):
    whole = pl.BlockSpec(memory_space=pltpu.VMEM)
    shapes = [jax.ShapeDtypeStruct(shape, dtype) for shape, dtype in outs]
    held = sum(math.prod(v.shape) * v.dtype.itemsize for v in (*operands, *shapes))
    kept = sum(math.prod(shape) * jnp.dtype(dtype).itemsize for shape, dtype in scratch)
    results = pl.pallas_call(
        kernel,
        out_shape=shapes,
        in_specs=[whole] * len(operands),
        out_specs=[whole] * len(shapes),
        scratch_shapes=[pltpu.VMEM(shape, dtype) for shape, dtype in scratch],
        compiler_params=pltpu.CompilerParams(
            vmem_limit_bytes=(held // 2 if flops else held) + kept + (8 if flops else 4) * 1024 * 1024
        ),
        cost_estimate=pl.CostEstimate(flops=0, bytes_accessed=1024, transcendentals=0),
    )(*operands)
    return results if len(shapes) > 1 else results[0]


def sinusoids_of_whole(coords, width):
    quarter = width // 4
    frequency = jnp.exp(jnp.arange(quarter, dtype=jnp.float32) * (-math.log(10000.0) / quarter))
    number = jnp.arange(32, dtype=jnp.float32)[:, None]
    far, near = 32.0 * number * frequency, number * frequency
    far = jnp.concatenate([jnp.sin(far), jnp.cos(far)], axis=1)
    near = jnp.concatenate([jnp.sin(near), jnp.cos(near)], axis=1)
    parts = []
    for coord in coords:
        whole = coord.astype(jnp.int32)
        pick_far = (whole // 32 == jnp.arange(32)[None, :]).astype(jnp.float32)
        pick_near = (whole % 32 == jnp.arange(32)[None, :]).astype(jnp.float32)
        at_far = jnp.dot(pick_far, far, precision=lax.Precision.HIGHEST)
        at_near = jnp.dot(pick_near, near, precision=lax.Precision.HIGHEST)
        sin_far, cos_far = at_far[:, :quarter], at_far[:, quarter:]
        sin_near, cos_near = at_near[:, :quarter], at_near[:, quarter:]
        parts.append(sin_far * cos_near + cos_far * sin_near)
        parts.append(cos_far * cos_near - sin_far * sin_near)
    return jnp.concatenate(parts, axis=1)


def normalise(inputs):
    centre = inputs - jnp.mean(inputs, axis=-1, keepdims=True)
    factor = lax.rsqrt(jnp.mean(centre * centre, axis=-1, keepdims=True) + EPSILON)
    return centre * factor, factor


def normalise_back(inputs, grad, gain):
    normal, factor = normalise(inputs)
    scaled = grad * gain
    inside = (
        scaled
        - jnp.mean(scaled, axis=-1, keepdims=True)
        - normal * jnp.mean(scaled * normal, axis=-1, keepdims=True)
    )
    return (
        factor * inside,
        jnp.sum(grad * normal, axis=0, keepdims=True),
        jnp.sum(grad, axis=0, keepdims=True),
    )


def gelu_parts(value):
    root = math.sqrt(2.0 / math.pi)
    square = value * value
    bent = jnp.tanh(root * value * (1.0 + 0.044715 * square))
    slope = 0.5 * (1.0 + bent) + 0.5 * value * (1.0 - bent * bent) * root * (1.0 + 0.134145 * square)
    return 0.5 * value * (1.0 + bent), slope


def grouped_plan(
    sizes,
    counts,
    coords,
    segment_ids,
    logit_grad,
    enc_weight,
    qkv_weight,
    out_weight,
    up_weight,
    down_weight,
    dec_weight,
    dec_bias,
    norm1_gain,
    norm1_shift,
    norm2_gain,
    norm2_shift,
):
    place = Place(sizes)
    nz = sizes[2]
    seqs, cells, genes = counts.shape
    width = enc_weight.shape[1]
    block = enc_weight.shape[0]
    head = width // HEADS
    heads = HEADS // 4
    slice_width = width // 4
    own_rows = seqs * cells
    rows = 4 * own_rows
    ff = up_weight.shape[1]
    ff_slice = ff // 4
    bf16, f32 = jnp.bfloat16, jnp.float32

    half, quarter = block // 2, block // 4
    three = 3 * slice_width
    lanes = ff // (8 * nz)
    up_half = nz * lanes
    many = down_weight.shape[0] // 4
    half_rows = rows // 2
    pairs = heads * rows * rows
    square = 2 * rows * width * width // 4

    vectors = jnp.stack([dec_bias, norm1_gain, norm1_shift, norm2_gain, norm2_shift])
    tall = half + quarter + 16

    def whole_kernel(enc_ref, dec_ref, vectors_ref, out_ref):
        y, core, _, _ = coordinates()
        for k in range(nz):
            at = k * tall
            put(out_ref, at, 0, rows_at(enc_ref, core * half, half))
            put(out_ref, at + half, 0, rows_at(dec_ref, core * half + y * quarter, quarter))
            out_ref[at + half + quarter : at + tall, :] = jnp.zeros((16, width), bf16)
            out_ref[at + half + quarter : at + half + quarter + 5, :block] = vectors_ref[...]

    whole_own = in_vmem(
        whole_kernel, [((nz * tall, width), bf16)], enc_weight, dec_weight, vectors
    )
    whole_near = place.exchange_z(whole_own)

    def up_columns(up_ref, out_ref, first, x):
        y, core, _, _ = coordinates()
        for number in range(nz):
            at = ((2 * number + x) * 2 + core) * 2 + y
            out_ref[first : first + block, number * lanes : (number + 1) * lanes] = up_ref[
                :, pl.ds(pl.multiple_of(at * lanes, lanes), lanes)
            ]

    def qkv_columns(qkv_ref, out_ref, core, x, y):
        at_rows = pl.ds(pl.multiple_of(y * half, 16), half)
        for at in range(3 * nz):
            part = own_part(qkv_ref[at_rows, at * 4 * head : (at + 1) * 4 * head], core, x, head)
            out_ref[:half, at * head : (at + 1) * head] = part

    def theirs_kernel(qkv_ref, up_ref, out_ref):
        y, core, _, x = coordinates()
        qkv_columns(qkv_ref, out_ref, core, 1 - x, y)
        up_columns(up_ref, out_ref, half, 1 - x)
        out_ref[half:, up_half:] = jnp.zeros((block, three - up_half), bf16)

    theirs = in_vmem(
        theirs_kernel, [((half + block, three), bf16)], after(qkv_weight, whole_own), up_weight
    )
    theirs = place.swap_x(theirs)

    def qkv_kernel(qkv_ref, theirs_ref, out_weight_ref, out_ref):
        y, core, _, x = coordinates()
        qkv_columns(qkv_ref, out_ref, core, x, y)
        out_ref[half:, :three] = theirs_ref[:half, :]
        part = rows_at(out_weight_ref, core * half + y * quarter, quarter)
        for j in range(4):
            out_ref[j * quarter : (j + 1) * quarter, three:] = part[
                :, j * slice_width : (j + 1) * slice_width
            ]

    qkv_own = in_vmem(qkv_kernel, [((block, width), bf16)], qkv_weight, theirs, out_weight)
    qkv_own = after(qkv_own, whole_near)
    near = [qkv_own] + [place.shift_z(qkv_own, k) for k in range(1, nz)]
    qkv_pieces = near + [place.swap_y(part) for part in near]

    def up_kernel(up_ref, theirs_ref, down_ref, out_ref):
        y, core, _, x = coordinates()
        up_columns(up_ref, out_ref, 0, x)
        out_ref[:block, up_half:] = theirs_ref[half:, :up_half]
        out_ref[block:, :] = rows_at(down_ref, (2 * core + y) * many, many)

    up_own = in_vmem(
        up_kernel, [((block + many, width), bf16)], up_weight, theirs, down_weight
    )
    up_near, up_far = [up_own], [place.swap_y(up_own)]
    for k in range(1, nz):
        up_near.append(place.shift_z(after(up_near[-1], up_far[0], near[1]), 1))
        if k < nz - 1:
            up_far.append(place.swap_y(up_near[-1]))
    up_far.append(place.shift_z(up_far[-1], 1))

    whole_far = place.swap_x(after(whole_near, qkv_pieces[nz]))

    express = jnp.log1p(counts.astype(f32)).astype(bf16)
    numbers = jnp.stack([coords[0], coords[1], segment_ids], axis=-1)
    beside = jnp.concatenate([numbers // SPLIT, numbers % SPLIT], axis=-1).astype(bf16)
    beside = jnp.pad(beside, ((0, 0), (0, 0), (0, 122)))
    pair = place.by_parity(jnp.concatenate([express, logit_grad, beside], axis=-1))
    near_cells = jnp.concatenate(
        place.regroup(*(after(part, theirs) for part in pair)), axis=0
    )
    near_cells = jnp.concatenate(
        [near_cells, after(
                place.swap_x(near_cells), up_far[0], *near[1:], up_near[1], whole_far,
            )], axis=0
    )
    far_cells = place.swap_core(near_cells)
    beside = jnp.concatenate([near_cells[:, 2 * genes :], far_cells[:, 2 * genes :]], axis=0).astype(f32)
    beside = beside[:, :3] * SPLIT + beside[:, 3:6]
    segment = beside[:, 2:3]
    segment_row = segment.reshape(1, rows)
    embed = sinusoids_of_whole((beside[:, 0:1], beside[:, 1:2]), width)


    def enc_half_kernel(near_ref, far_ref, out_ref, vectors_ref):
        _, _, _, x = coordinates()
        for dx, ref in enumerate((near_ref, far_ref)):
            for k in range(nz):
                at = k * tall
                put(out_ref, (2 * k + (x ^ dx)) * half, 0, ref[at : at + half, :])
                part = ref[at + half + quarter : at + tall, :block]
                put(vectors_ref, 0, (2 * k + (x ^ dx)) * block, part)

    enc_half, vectors = in_vmem(
        enc_half_kernel, [((genes // 2, width), bf16), ((16, width), f32)], whole_near, whole_far
    )
    enc_far = place.swap_core(enc_half)

    def both_cores(near_ref, far_ref, out_ref):
        _, core, _, _ = coordinates()
        for dc, ref in enumerate((near_ref, far_ref)):
            for k in range(2 * nz):
                put(out_ref, k * block + (core ^ dc) * half, 0, ref[k * half : (k + 1) * half, :])

    def by_y(out_mine, out_send, value, first):
        y, _, _, _ = coordinates()
        for k in range(nz):
            low = value[:, 2 * k * block : (2 * k + 1) * block]
            high = value[:, (2 * k + 1) * block : (2 * k + 2) * block]
            at = slice(first, first + value.shape[0]), slice(k * block, (k + 1) * block)
            out_mine[at] = jnp.where(y == 0, low, high)
            out_send[at] = jnp.where(y == 0, high, low)

    def first_kernel(
        near_ref, far_ref, enc_near_ref, enc_far_ref, embed_ref, vectors_ref,
        enc_ref, hidden_ref, normed_ref, mine_ref, send_ref,
    ):
        both_cores(enc_near_ref, enc_far_ref, enc_ref)
        for number, ref in enumerate((near_ref, far_ref)):
            first = number * half_rows
            hidden = dot(ref[:, :genes], enc_ref[...]) + embed_ref[first : first + half_rows, :]
            if number == 0:
                hidden_ref[...] = hidden
            normal, _ = normalise(hidden)
            normed = (normal * vectors_ref[1:2, :] + vectors_ref[2:3, :]).astype(bf16)
            normed_ref[first : first + half_rows, :] = normed
            by_y(mine_ref, send_ref, normed, first)

    square_bf16, half_bf16 = ((width, width), bf16), ((half_rows, width), bf16)
    half_f32 = ((half_rows, width), f32)
    columns_bf16 = ((rows, width // 2), bf16)
    w_enc, hidden0, normed1, normed1_mine, normed1_send = in_vmem(
        first_kernel, [square_bf16, half_f32, ((rows, width), bf16), columns_bf16, columns_bf16],
        near_cells, far_cells, enc_half, enc_far, embed, vectors, flops=4 * square,
    )

    def attend_kernel(normed_ref, *refs):
        pieces, refs = refs[: 2 * nz], refs[2 * nz :]
        column_ref, row_ref, w_ref, w_out_ref, qkv_ref, out_ref, own_ref, send_ref = refs
        y, _, z, x = coordinates()
        for dy in range(2):
            for k in range(nz):
                ref = pieces[dy * nz + k]
                there = (z - k) % nz
                for dx in range(2):
                    row = (2 * there + (x ^ dx)) * block + (y ^ dy) * half
                    put(w_ref, row, 0, ref[dx * half : (dx + 1) * half, :three])
                for j in range(4):
                    row = there * half + (y ^ dy) * quarter
                    part = ref[j * quarter : (j + 1) * quarter, three:]
                    put(w_out_ref, row, j * slice_width, part)
        qkv_ref[...] = dot(normed_ref[...], w_ref[...]).astype(bf16)
        allowed = column_ref[...] == row_ref[...]
        for number in range(heads):
            queries, keys, values = (one_head(qkv_ref, i, heads, number, head) for i in range(3))
            probs = soft(queries, keys, allowed, head**-0.5)
            at = slice(number * head, (number + 1) * head)
            out_ref[:, at] = dot(probs.astype(bf16), values).astype(bf16)
        own_ref[...] = dot(out_ref[:half_rows, :], w_out_ref[...])
        send_ref[...] = dot(out_ref[half_rows:, :], w_out_ref[...]).astype(bf16)

    w_qkv, w_out, qkv, context, own, send = in_vmem(
        attend_kernel,
        [((width, three), bf16), ((slice_width, width), bf16), ((rows, three), bf16),
         ((rows, slice_width), bf16), half_f32, half_bf16],
        after(normed1, up_near[2], up_far[1]), *qkv_pieces, segment, segment_row,
        flops=4 * square + 4 * pairs * head, exps=pairs,
    )

    def add_kernel(own_ref, other_ref, out_ref):
        out_ref[...] = (own_ref[...].astype(f32) + other_ref[...].astype(f32)).astype(out_ref.dtype)

    def add(own, other, dtype=bf16):
        return in_vmem(add_kernel, [(own.shape, dtype)], own, other)

    def sum_x(mine_ref, other_ref):
        other = jnp.concatenate([other_ref[own_rows:, :], other_ref[:own_rows, :]], axis=0)
        return mine_ref[...].astype(f32) + other.astype(f32)

    mine = add(own, after(place.swap_core(send), up_far[1], up_near[3], up_far[2]))

    def second_kernel(hidden_ref, mine_ref, other_ref, vectors_ref, out_ref, normed_ref):
        hidden = hidden_ref[...] + sum_x(mine_ref, other_ref)
        out_ref[...] = hidden
        normal, _ = normalise(hidden)
        normed_ref[...] = (normal * vectors_ref[3:4, :] + vectors_ref[4:5, :]).astype(bf16)

    hidden1, normed2 = in_vmem(
        second_kernel, [half_f32, half_bf16],
        hidden0, mine, after(place.swap_x(mine), up_far[3]), vectors,
    )
    normed2_far = place.swap_core(normed2)

    def dec_rows_kernel(near_ref, far_ref, out_ref):
        for dx, ref in enumerate((near_ref, far_ref)):
            for k in range(nz):
                at, out = k * tall + half, (dx * nz + k) * quarter
                out_ref[out : out + quarter, :] = ref[at : at + quarter, :]

    dec_near = in_vmem(
        dec_rows_kernel, [((2 * nz * quarter, genes), bf16)], whole_near, after(whole_far, qkv)
    )

    def dec_half_kernel(near_ref, far_ref, out_ref):
        y, _, _, x = coordinates()
        for dy, ref in enumerate((near_ref, far_ref)):
            for dx in range(2):
                for k in range(nz):
                    at = (dx * nz + k) * quarter
                    row = (2 * k + (x ^ dx)) * half + (y ^ dy) * quarter
                    put(out_ref, row, 0, ref[at : at + quarter, :])

    dec_half = in_vmem(
        dec_half_kernel, [((width // 2, genes), bf16)],
        dec_near, after(place.swap_y(dec_near), mine),
    )
    dec_far = place.swap_core(dec_half)

    def decoder_kernel(near_ref, far_ref, dec_near_ref, dec_far_ref, dec_ref, grad_ref, low_ref, sums_ref):
        both_cores(dec_near_ref, dec_far_ref, dec_ref)
        grad = times_t(near_ref[:, genes : 2 * genes], dec_ref[...])
        grad_ref[...] = grad
        low_ref[:half_rows, :] = grad.astype(bf16)
        low_ref[half_rows:, :] = times_t(far_ref[:, genes : 2 * genes], dec_ref[...]).astype(bf16)
        sums_ref[...] = sum(
            jnp.sum(ref[:, genes : 2 * genes].astype(f32), axis=0, keepdims=True)
            for ref in (near_ref, far_ref)
        )

    w_dec, grad_h2, grad_down, bias_sums = in_vmem(
        decoder_kernel,
        [square_bf16, half_f32, ((rows, width), bf16), ((1, width), f32)],
        near_cells, far_cells, dec_half, dec_far, flops=4 * square,
    )

    def feed_kernel(normed_ref, normed_far_ref, grad_ref, *refs):
        pieces, refs = refs[: 2 * nz], refs[2 * nz :]
        active_ref, grad_up_ref, own_ref, send_ref, own2_ref, send2_ref, mine_ref, theirs_ref = refs[:8]
        w_up_ref, w_down_ref, normed_all, back, ahead = refs[8:]
        y, _, z, x = coordinates()
        for dy in range(2):
            for k in range(nz):
                ref = pieces[dy * nz + k]
                there = (z - k) % nz
                for dx in range(2):
                    for number in range(nz):
                        at = dx * up_half + number * lanes
                        column = (2 * number + (y ^ dy)) * lanes
                        put(w_up_ref, (2 * there + (x ^ dx)) * block, column, ref[:block, at : at + lanes])
                put(w_down_ref, (2 * there + (y ^ dy)) * many, 0, ref[block:, :])
        normed_all[:half_rows, :] = normed_ref[...]
        normed_all[half_rows:, :] = normed_far_ref[...]
        by_y(mine_ref, theirs_ref, normed_ref[...], 0)
        by_y(mine_ref, theirs_ref, normed_far_ref[...], half_rows)
        chunk = 2 * lanes
        for number in range(nz):
            at = slice(number * chunk, (number + 1) * chunk)
            active, slope = gelu_parts(dot(normed_all[...], w_up_ref[:, at]))
            active = active.astype(bf16)
            active_ref[:, at] = active
            grad_up = (times_t(grad_ref[...], w_down_ref[at, :]) * slope).astype(bf16)
            grad_up_ref[:, at] = grad_up
            part, part2 = times_t(grad_up, w_up_ref[:, at]), dot(active, w_down_ref[at, :])
            back[...] = part if number == 0 else back[...] + part
            ahead[...] = part2 if number == 0 else ahead[...] + part2
        for sums, one, two in ((back, own_ref, send_ref), (ahead, own2_ref, send2_ref)):
            one[...] = sums[:half_rows, :]
            two[...] = sums[half_rows:, :].astype(bf16)

    full_bf16, full_f32 = ((rows, width), bf16), ((rows, width), f32)
    active, grad_up, own, send, own2, send2, normed2_mine, normed2_send = in_vmem(
        feed_kernel,
        [full_bf16, full_bf16, half_f32, half_bf16, half_f32, half_bf16, columns_bf16, columns_bf16],
        normed2, normed2_far, grad_down, *up_near, *up_far,
        flops=16 * square, exps=rows * ff_slice,
        scratch=[square_bf16, square_bf16, full_bf16, full_f32, full_f32],
    )
    mine = add(own, place.swap_core(send))

    def down_halve_kernel(value_ref, *refs):
        _, _, z, _ = coordinates()
        for number in range(2):
            for ref, low in ((refs[2 * number], z % 2), (refs[2 * number + 1], 1 - z % 2)):
                for high in range(2):
                    part = rows_at(value_ref, ((2 * high + low) * 2 + number) * many, many)
                    ref[high * many : (high + 1) * many, :] = part

    def sum_halve_kernel(*refs):
        parts, (out_ref, send_ref, all_ref) = refs[:-3], refs[-3:]
        at = 0
        for ref in parts[1:]:
            rows_here = slice(at, at + ref.shape[0])
            all_ref[rows_here, :] = parts[0][rows_here, :].astype(f32) + ref[...].astype(f32)
            at += ref.shape[0]
        _, _, z, _ = coordinates()
        count = out_ref.shape[0] // 2
        for high in range(2):
            at = slice(high * count, (high + 1) * count)
            out_ref[at, :] = rows_at(all_ref, (2 * high + z % 2) * count, count).astype(bf16)
            send_ref[at, :] = rows_at(all_ref, (2 * high + 1 - z % 2) * count, count).astype(bf16)

    def sum_halve(own, *others):
        shape = ((own.shape[0] // 2, own.shape[1]), bf16)
        return in_vmem(
            sum_halve_kernel, [shape, shape], own, *others, scratch=[(own.shape, f32)]
        )

    def add_split_kernel(own_ref, other_ref, out_ref, send_ref):
        _, _, z, _ = coordinates()
        count = out_ref.shape[0]
        for ref, part in ((out_ref, z // 2), (send_ref, 1 - z // 2)):
            own, other = (rows_at(r, part * count, count).astype(f32) for r in (own_ref, other_ref))
            ref[...] = (own + other).astype(bf16)

    def add_halve(own, other):
        shape = ((own.shape[0] // 2, own.shape[1]), bf16)
        return in_vmem(add_split_kernel, [shape, shape], own, other)

    down_one = in_vmem(
        down_halve_kernel, [((2 * many, width), bf16)] * 4, inner(active, grad_down).astype(bf16)
    )
    down_one = [down_one[:2], down_one[2:]]
    down_other = place.swap_z(down_one[0][1], 1)
    up_mine = inner(after(normed2_mine, mine), grad_up).astype(bf16)
    up_send = inner(after(normed2_send, mine), grad_up).astype(bf16)
    low_rows = nz * block // 2
    up_other_low = place.swap_y(up_send[:low_rows])
    ahead = add(own2, after(place.swap_core(send2), mine))
    other = after(place.swap_x(mine), up_mine, up_send, ahead, up_other_low, down_other)
    up_other_high = place.swap_y(after(up_send[low_rows:], other))
    down_two = [add_halve(down_one[0][0], after(down_other, other))]
    down_two_other = place.swap_z(down_two[0][1], 2)
    down_other = place.swap_z(after(down_one[1][1], other), 1)

    def back_kernel(hidden_ref, mine_ref, other_ref, grad_ref, vectors_ref, out_ref, low_ref, row):
        inside, gain_sums, shift_sums = normalise_back(
            hidden_ref[...], sum_x(mine_ref, other_ref), vectors_ref[row : row + 1, :]
        )
        grad = grad_ref[...] + inside
        if out_ref is not None:
            out_ref[...] = grad
        low_ref[:half_rows, :] = grad.astype(bf16)
        low_ref[half_rows:, :] = jnp.zeros((16, width), bf16)
        low_ref[half_rows : half_rows + 1, :] = gain_sums.astype(bf16)
        low_ref[half_rows + 1 : half_rows + 2, :] = shift_sums.astype(bf16)

    def second_back_kernel(*refs):
        back_kernel(*refs, 3)

    def first_back_kernel(*refs):
        back_kernel(*refs[:5], None, refs[5], 1)

    message = ((half_rows + 16, width), bf16)
    grad_h1, near_two = in_vmem(
        second_back_kernel, [half_f32, message], hidden1, mine, other, grad_h2, vectors
    )
    far_two = place.swap_core(near_two)
    ahead_other = place.swap_x(after(ahead, other))

    def attend_back_kernel(
        near_ref, far_ref, w_out_ref, qkv_ref, column_ref, row_ref, w_ref,
        out_ref, own_ref, send_ref, all_ref, grad_ref,
    ):
        all_ref[:half_rows, :] = near_ref[:half_rows, :]
        all_ref[half_rows:, :] = far_ref[:half_rows, :]
        grad_ref[...] = times_t(all_ref[...], w_out_ref[...]).astype(bf16)
        allowed = column_ref[...] == row_ref[...]
        scaling = head**-0.5
        for number in range(heads):
            queries, keys, values = (one_head(qkv_ref, i, heads, number, head) for i in range(3))
            grad = one_head(grad_ref, 0, heads, number, head)
            probs = soft(queries, keys, allowed, scaling)
            weighted = probs * times_t(grad, values)
            delta = jnp.sum(weighted, axis=-1, keepdims=True)
            dscore = (weighted - probs * delta).astype(bf16)
            parts = (
                dot(dscore, keys) * scaling,
                inner(dscore, queries) * scaling,
                inner(probs.astype(bf16), grad),
            )
            for i, part in enumerate(parts):
                at = (i * heads + number) * head
                out_ref[:, at : at + head] = part.astype(bf16)
        own_ref[...] = times_t(out_ref[:half_rows, :], w_ref[...])
        send_ref[...] = times_t(out_ref[half_rows:, :], w_ref[...]).astype(bf16)

    grad_qkv, own, send, grad_attn = in_vmem(
        attend_back_kernel, [((rows, three), bf16), half_f32, half_bf16, full_bf16],
        near_two, far_two, w_out, qkv, segment, segment_row, w_qkv,
        flops=4 * square + 10 * pairs * head, exps=pairs,
        scratch=[((rows, slice_width), bf16)],
    )
    qkv_send = inner(normed1_send, grad_qkv).astype(bf16)
    qkv_other = place.swap_y(qkv_send)
    up_one = sum_halve(up_mine, up_other_low, after(up_other_high, grad_qkv))
    down_two.append(add_halve(down_one[1][0], after(down_other, grad_qkv)))
    down_sum = [add(down_two[0][0], after(down_two_other, grad_qkv))]
    mine = add(
        own, after(
            place.swap_core(send), qkv_send, up_one[1], ahead_other, down_two[1][1], down_sum[0]
        ),
    )
    other = place.swap_x(mine)
    down_two_other = place.swap_z(after(down_two[1][1], mine), 2)
    up_one_other = place.swap_z(up_one[1], 1)

    qkv_mine = inner(normed1_mine, grad_qkv).astype(bf16)
    grad_w_out = inner(context, grad_attn).astype(bf16)

    def logits_kernel(hidden_ref, mine_ref, other_ref, dec_ref, vectors_ref, one_ref, two_ref, own_ref, send_ref):
        _, core, _, x = coordinates()
        hidden = (hidden_ref[...] + sum_x(mine_ref, other_ref)).astype(bf16)
        logits = (dot(hidden[:own_rows, :], dec_ref[...]) + vectors_ref[0:1, :]).astype(bf16)
        one_ref[...] = logits[:cells, :]
        two_ref[...] = logits[cells:, :]
        for k in range(nz):
            group = hidden[:, 2 * k * block : (2 * k + 2) * block]
            at = slice(k * half, (k + 1) * half)
            own_ref[:, at] = own_part(group, core, x, half)
            send_ref[:, at] = own_part(group, 1 - core, x, half)

    cells_bf16, part_bf16 = ((cells, genes), bf16), ((half_rows, slice_width), bf16)
    one, two, hidden2_own, hidden2_send = in_vmem(
        logits_kernel, [cells_bf16, cells_bf16, part_bf16, part_bf16],
        hidden1, ahead, after(ahead_other, mine), w_dec, vectors, flops=square,
    )
    hidden2_far = place.swap_core(hidden2_send)
    grad_w_dec = inner(hidden2_own, near_cells[:, genes : 2 * genes])
    grad_w_dec += inner(hidden2_far, far_cells[:, genes : 2 * genes])
    grad_w_dec = grad_w_dec.astype(bf16)
    few_mine = jnp.where(place.y == 0, grad_w_out, grad_w_dec)
    few_send = jnp.where(place.y == 0, grad_w_dec, grad_w_out)
    few_other = place.swap_y(few_send)

    other = after(other, qkv_mine, few_send, qkv_other, up_one_other, down_two_other)
    qkv_one = sum_halve(qkv_mine, qkv_other)
    qkv_one_other = place.swap_z(qkv_one[1], 1)
    up_two = add_halve(up_one[0], after(up_one_other, other))
    up_two_other = place.swap_z(up_two[1], 2)
    near_one = in_vmem(first_back_kernel, [message], hidden0, mine, other, grad_h1, vectors)
    far_one = place.swap_core(near_one)
    input_grad = times_t(near_one[:own_rows], w_enc).astype(bf16)

    def last_kernel(near_ref, far_ref, one_ref, one_far_ref, two_ref, two_far_ref, bias_ref, *refs):
        own_ref, send_ref, slice_ref, grad_ref, sums_ref = refs
        _, core, z, x = coordinates()
        for number, ref in enumerate((near_ref, far_ref)):
            for k in range(nz):
                group = ref[:, 2 * k * block : (2 * k + 2) * block]
                slice_ref[
                    number * half_rows : (number + 1) * half_rows, k * half : (k + 1) * half
                ] = own_part(group, core, x, half)
        grad_ref[...] = inner(slice_ref[:half_rows, :], one_ref[:half_rows, :]) + inner(
            slice_ref[half_rows:, :], one_far_ref[:half_rows, :]
        )
        sums_ref[...] = jnp.zeros((8, width), f32)
        sums_ref[0:1, :] = bias_ref[...]
        at = slice(half_rows, half_rows + 2)
        sums_ref[1:3, :] = one_ref[at, :].astype(f32) + one_far_ref[at, :].astype(f32)
        sums_ref[3:5, :] = two_ref[at, :].astype(f32) + two_far_ref[at, :].astype(f32)
        for ref, low in ((own_ref, z % 2), (send_ref, 1 - z % 2)):
            ref[...] = jnp.zeros(ref.shape, bf16)
            for high in range(2):
                there, first = 2 * high + low, high * (half + 16)
                ref[first : first + half, :] = rows_at(grad_ref, there * half, half).astype(bf16)
                column = pl.multiple_of((2 * there + x) * block, block)
                part = sums_ref[:, pl.ds(column, block)].astype(bf16)
                ref[first + half : first + half + 8, :block] = part

    last_one = in_vmem(
        last_kernel, [((2 * (half + 16), width), bf16)] * 2,
        near_cells, far_cells, near_one, after(far_one, few_other, qkv_one_other, up_two_other),
        near_two, far_two, bias_sums, flops=square,
        scratch=[((rows, slice_width), bf16), ((slice_width, width), f32), ((8, width), f32)],
    )
    last_one_other = place.swap_z(last_one[1], 1)
    qkv_two = add_halve(qkv_one[0], after(qkv_one_other, last_one[1]))
    qkv_two_other = place.swap_z(qkv_two[1], 2)
    up_sum = add(up_two[0], after(up_two_other, last_one[1]))
    up_other = place.swap_y(up_sum)
    down_sum.append(add(down_two[1][0], after(down_two_other, last_one[1])))
    down_sum = jnp.concatenate(down_sum, axis=0)
    down_other = place.swap_y(down_sum)
    few_one = sum_halve(few_mine, after(few_other, last_one[1]))
    few_one_other = place.swap_z(few_one[1], 1)

    def by_x_kernel(own_ref, other_ref, mine_ref, send_ref):
        y, _, _, x = coordinates()
        at = slice(0, mine_ref.shape[0]), slice(0, mine_ref.shape[1])
        mine_ref[...] = jnp.where(y == x, own_ref[at], other_ref[at])
        send_ref[...] = jnp.where(y == x, other_ref[at], own_ref[at])

    def by_x(own, other, width):
        return in_vmem(by_x_kernel, [((block, width), bf16)] * 2, own, other)

    qkv_sum = add(
        qkv_two[0], after(qkv_two_other, last_one_other, few_one_other, down_other, up_other)
    )
    qkv_other = place.swap_y(qkv_sum)
    up_mine, up_send = by_x(up_sum, up_other, ff_slice)
    up_both = place.swap_x(up_send)
    down_sum = add(down_sum, down_other)
    down_far = place.swap_core(down_sum)
    last_two = add_halve(last_one[0], after(last_one_other, qkv_sum))
    last_two_other = place.swap_z(last_two[1], 2)
    few_two = add_halve(few_one[0], after(few_one_other, qkv_sum))
    few_two_other = place.swap_z(few_two[1], 2)
    qkv_other, up_both, down_far, last_two_other, few_two_other, one, two = lax.optimization_barrier(
        (qkv_other, up_both, down_far, last_two_other, few_two_other, one, two)
    )
    logits = place.regroup(one, two)
    last = add(last_two[0], last_two_other)
    last_other = place.swap_y(last)

    def last_add_kernel(one_ref, other_ref, out_ref, sums_ref):
        total = one_ref[...].astype(f32) + other_ref[...].astype(f32)
        out_ref[...] = total[:half, :].astype(bf16)
        sums_ref[...] = total[half : half + 8, :block]

    out_enc, sums = in_vmem(
        last_add_kernel, [((half, width), bf16), ((8, block), f32)], last, last_other
    )

    def halves_kernel(near_ref, far_ref, out_ref):
        _, core, _, _ = coordinates()
        count = near_ref.shape[0]
        for dc, ref in enumerate((near_ref, far_ref)):
            put(out_ref, (core ^ dc) * count, 0, ref[...])

    def halves(near, far):
        return in_vmem(
            halves_kernel, [((2 * near.shape[0], near.shape[1]), f32)], near, far
        )

    out_enc = halves(out_enc, place.swap_core(out_enc))
    out_down = halves(down_sum, down_far)

    up_both = jnp.concatenate([up_mine, up_both], axis=0)

    def up_out_kernel(near_ref, far_ref, out_ref):
        _, core, _, x = coordinates()
        for dc, ref in enumerate((near_ref, far_ref)):
            for dx in range(2):
                for k in range(nz):
                    part = ref[dx * block : (dx + 1) * block, 2 * k * lanes : 2 * (k + 1) * lanes]
                    put(out_ref, 0, ((2 * k + (x ^ dx)) * 2 + (core ^ dc)) * 2 * lanes, part)

    out_up = in_vmem(up_out_kernel, [((block, ff), f32)], up_both, place.swap_core(up_both))

    qkv_mine, qkv_send = by_x(qkv_sum, qkv_other, three)
    qkv_both = jnp.concatenate([qkv_mine, place.swap_x(qkv_send)], axis=0)
    few_sum = add(few_two[0], few_two_other)
    pair = place.regroup(
        *(after(input_grad[i * cells : (i + 1) * cells], qkv_other) for i in range(2))
    )
    input_grad = jnp.stack(place.by_parity(pair))
    logits = jnp.stack(place.by_parity(logits))

    def few_kernel(own_ref, other_ref, out_ref):
        y, _, _, _ = coordinates()
        put(out_ref, y * half, 0, own_ref[...])
        put(out_ref, (1 - y) * half, 0, other_ref[...])

    few = in_vmem(few_kernel, [((block, genes), bf16)], few_sum, place.swap_y(few_sum))

    def few_out_kernel(near_ref, far_ref, out_ref, dec_ref):
        _, core, _, _ = coordinates()
        for dc, ref in enumerate((near_ref, far_ref)):
            put(out_ref, (core ^ dc) * half, 0, ref[:half, :])
            put(dec_ref, (core ^ dc) * half, 0, ref[half:, :])

    out_out, out_dec = in_vmem(
        few_out_kernel, [((block, width), f32), ((block, genes), f32)], few, place.swap_core(few)
    )

    def qkv_out_kernel(near_ref, far_ref, out_ref):
        _, core, _, x = coordinates()
        for dx in range(2):
            for number in range(3 * nz):
                at = slice(dx * block, (dx + 1) * block), slice(number * head, (number + 1) * head)
                near_part, far_part = near_ref[at].astype(f32), far_ref[at].astype(f32)
                low = jnp.where(core == 0, near_part, far_part)
                high = jnp.where(core == 0, far_part, near_part)
                put(
                    out_ref, 0, number * 4 * head + (x ^ dx) * 2 * head,
                    jnp.concatenate([low, high], axis=1),
                )

    out_qkv = in_vmem(
        qkv_out_kernel, [((block, 3 * width), f32)], qkv_both, place.swap_core(qkv_both)
    )
    return (
        logits, input_grad, out_enc, out_qkv, out_out, out_up, out_down, out_dec,
        sums[0], sums[1], sums[2], sums[3], sums[4],
    )


IN_SPECS = (
    ("dp", "blk", None), (None, "dp", "blk"), ("dp", "blk"), ("dp", "blk", None),
    *[("blk", None)] * 6, *[("blk",)] * 5,
)
OUT_SPECS = (("dp", "blk", None), ("dp", "blk", None), *[("blk", None)] * 6, *[("blk",)] * 5)


def solution(mesh):
    groups, blocks = mesh.shape["dp"], mesh.shape["blk"]

    def run(*args):
        seqs = args[0].shape[0] // groups
        if groups == 4 and blocks == 4 * seqs and seqs == 2 and HEADS == 4 * (blocks // 2):
            sizes = (groups // 2, 2, blocks // 2, 2)
            fine = Mesh(mesh.devices.reshape(sizes), AXES)
            names = {"dp": ("y", "core"), "blk": ("z", "x"), None: None}
            plan = functools.partial(grouped_plan, sizes)
        else:
            fine, names, plan = mesh, {"dp": "dp", "blk": "blk", None: None}, spread_plan
        specs = lambda entries: tuple(P(*[names[axis] for axis in entry]) for entry in entries)
        return jax.shard_map(
            plan, mesh=fine, in_specs=specs(IN_SPECS), out_specs=specs(OUT_SPECS), check_vma=False
        )(*args)

    return run
```

```python
import functools
import math

import jax
import jax.numpy as jnp
from jax import lax
from jax.experimental import pallas as pl
from jax.experimental.pallas import tpu as pltpu
from jax.sharding import Mesh
from jax.sharding import PartitionSpec as P

HEADS = 16


NEGATIVE = -1e30
EPSILON = 1e-05


def layer_norm(inputs, gain_vec, shift_vec):
    centre = inputs - jnp.mean(inputs, axis=-1, keepdims=True)
    spread = jnp.mean(centre * centre, axis=-1, keepdims=True)
    return centre * lax.rsqrt(spread + EPSILON) * gain_vec + shift_vec


def sinusoids(coords, width):
    quarter = width // 4
    frequency = jnp.exp(jnp.arange(quarter, dtype=jnp.float32) * (-math.log(10000.0) / quarter))
    first_angle = coords[0].astype(jnp.float32)[..., None] * frequency
    second_angle = coords[1].astype(jnp.float32)[..., None] * frequency
    return jnp.concatenate(
        [jnp.sin(first_angle), jnp.cos(first_angle), jnp.sin(second_angle), jnp.cos(second_angle)],
        axis=-1,
    )


def inner(left, right):
    return lax.dot_general(
        left, right, (((0,), (0,)), ((), ())), preferred_element_type=jnp.float32
    )


def times_t(left, right):
    return lax.dot_general(
        left, right, (((1,), (1,)), ((), ())), preferred_element_type=jnp.float32
    )


def spread_plan(
    counts,
    coords,
    segment_ids,
    logit_grad,
    enc_weight,
    qkv_weight,
    out_weight,
    up_weight,
    down_weight,
    dec_weight,
    dec_bias,
    norm1_gain,
    norm1_shift,
    norm2_gain,
    norm2_shift,
):
    gathered = (
        lax.all_gather(enc_weight, "blk", axis=0, tiled=True),
        lax.all_gather(qkv_weight, "blk", axis=0, tiled=True),
        lax.all_gather(out_weight, "blk", axis=0, tiled=True),
        lax.all_gather(up_weight, "blk", axis=0, tiled=True),
        lax.all_gather(down_weight, "blk", axis=0, tiled=True),
        lax.all_gather(dec_weight, "blk", axis=0, tiled=True),
        lax.all_gather(dec_bias, "blk", axis=0, tiled=True),
        lax.all_gather(norm1_gain, "blk", axis=0, tiled=True),
        lax.all_gather(norm1_shift, "blk", axis=0, tiled=True),
        lax.all_gather(norm2_gain, "blk", axis=0, tiled=True),
        lax.all_gather(norm2_shift, "blk", axis=0, tiled=True),
    )
    w_enc, w_qkv, w_out, w_up, w_down, w_dec, b_dec, gain_one, shift_one, gain_two, shift_two = (
        gathered
    )
    seg_all = lax.all_gather(segment_ids, "blk", axis=1, tiled=True)
    seq_count, cell_count, gene_count = counts.shape
    width = w_enc.shape[1]
    head_count = HEADS
    head_size = width // head_count
    scaling = head_size ** (-0.5)
    row_count = seq_count * cell_count
    express = (
        jnp.log1p(counts.astype(jnp.float32)).astype(jnp.bfloat16).reshape(row_count, gene_count)
    )
    embed = sinusoids(coords, width).reshape(row_count, width)
    hidden0 = jnp.dot(express, w_enc, preferred_element_type=jnp.float32) + embed
    gain_one32 = gain_one.astype(jnp.float32)
    shift_one32 = shift_one.astype(jnp.float32)
    gain_two32 = gain_two.astype(jnp.float32)
    shift_two32 = shift_two.astype(jnp.float32)
    normed1 = layer_norm(hidden0, gain_one32, shift_one32).astype(jnp.bfloat16)
    qkv = jnp.dot(normed1, w_qkv, preferred_element_type=jnp.float32).astype(jnp.bfloat16)
    queries = qkv[:, :width].reshape(seq_count, cell_count, head_count, head_size)
    key_rows = qkv[:, width : 2 * width].reshape(seq_count, cell_count, head_count, head_size)
    values = qkv[:, 2 * width :].reshape(seq_count, cell_count, head_count, head_size)

    def masked_scores(query_part, key_part, seg_query, seg_key):
        scores = (
            jnp.einsum("sqhe,skhe->shqk", query_part, key_part, preferred_element_type=jnp.float32)
            * scaling
        )
        return jnp.where(seg_query[:, None, :, None] == seg_key[:, None, None, :], scores, NEGATIVE)

    start_max = jnp.full((seq_count, head_count, cell_count), NEGATIVE, jnp.float32)
    piece = (
        lax.all_gather(key_rows, "blk", axis=1, tiled=True),
        lax.all_gather(values, "blk", axis=1, tiled=True),
    )
    seg_part = seg_all
    incoming = (piece[0], piece[1], seg_part)
    running_max = start_max
    key_part, value_part, context_seg_part = incoming
    query_part = queries
    scores = masked_scores(query_part, key_part, segment_ids, context_seg_part)
    newest = jnp.maximum(running_max, jnp.max(scores, axis=-1))
    expo = jnp.exp(scores - newest[..., None])
    running_sum = jnp.sum(expo, axis=-1)
    update = jnp.einsum(
        "shqk,skhe->sqhe", expo.astype(jnp.bfloat16), value_part, preferred_element_type=jnp.float32
    )
    weighted = update
    running_max, running_sum, weighted = (newest, running_sum, weighted)
    context32 = weighted / jnp.transpose(running_sum, (0, 2, 1))[..., None]
    logsum = jnp.transpose(running_max + jnp.log(running_sum), (0, 2, 1))
    context = context32.astype(jnp.bfloat16).reshape(row_count, width)
    hidden1 = hidden0 + jnp.dot(context, w_out, preferred_element_type=jnp.float32)
    normed2 = layer_norm(hidden1, gain_two32, shift_two32).astype(jnp.bfloat16)
    up_value = jnp.dot(normed2, w_up, preferred_element_type=jnp.float32)
    active = jax.nn.gelu(up_value).astype(jnp.bfloat16)
    hidden2 = hidden1 + jnp.dot(active, w_down, preferred_element_type=jnp.float32)
    hidden2_low = hidden2.astype(jnp.bfloat16)
    logits = (
        jnp.dot(hidden2_low, w_dec, preferred_element_type=jnp.float32) + b_dec.astype(jnp.float32)
    ).astype(jnp.bfloat16)
    cotangent = logit_grad.reshape(row_count, gene_count)
    grad_dec = inner(hidden2_low, cotangent)
    grad_bias = jnp.sum(cotangent.astype(jnp.float32), axis=0)
    grad_h2 = times_t(cotangent, w_dec)
    grad_down = grad_h2.astype(jnp.bfloat16)
    grad_w_down = inner(active, grad_down)
    grad_active = times_t(grad_down, w_down)
    gelu_pull = jax.vjp(jax.nn.gelu, up_value)[1]
    grad_up = gelu_pull(grad_active)[0].astype(jnp.bfloat16)
    grad_w_up = inner(normed2, grad_up)
    grad_normed2 = times_t(grad_up, w_up)
    norm_pull_two = jax.vjp(layer_norm, hidden1, gain_two32, shift_two32)[1]
    part_two, grad_gain_two, grad_shift_two = norm_pull_two(grad_normed2)
    grad_h1 = grad_h2 + part_two
    grad_attn = grad_h1.astype(jnp.bfloat16)
    grad_w_out = inner(context, grad_attn)
    grad_context = (
        times_t(grad_attn, w_out)
        .astype(jnp.bfloat16)
        .reshape(seq_count, cell_count, head_count, head_size)
    )
    delta = jnp.sum(grad_context.astype(jnp.float32) * context32, axis=-1)
    logsum_all, delta_all = (
        lax.all_gather(logsum, "blk", axis=1, tiled=True),
        lax.all_gather(delta, "blk", axis=1, tiled=True),
    )
    seg_part = seg_all
    query_seg_part = seg_part
    query_part = queries
    gradout_part = grad_context
    logsum_part = logsum
    delta_part = delta
    scores = masked_scores(query_part, key_part, segment_ids, query_seg_part)
    probs = jnp.exp(scores - jnp.transpose(logsum_part, (0, 2, 1))[..., None])
    dprob = jnp.einsum(
        "sqhe,skhe->shqk", gradout_part, value_part, preferred_element_type=jnp.float32
    )
    dscore = (probs * (dprob - jnp.transpose(delta_part, (0, 2, 1))[..., None])).astype(
        jnp.bfloat16
    )
    grad_queries = (
        jnp.einsum("shqk,skhe->sqhe", dscore, key_part, preferred_element_type=jnp.float32)
        * scaling
    )
    piece = (
        lax.all_gather(queries, "blk", axis=1, tiled=True),
        lax.all_gather(grad_context, "blk", axis=1, tiled=True),
    )
    seg_part = seg_all
    logsum_part = logsum_all
    delta_part = delta_all
    incoming = (piece[0], piece[1], logsum_part, delta_part, seg_part)
    query_part, gradout_part, key_logsum_part, key_delta_part, key_seg_part = incoming
    key_part = key_rows
    scores = masked_scores(query_part, key_part, key_seg_part, segment_ids)
    probs = jnp.exp(scores - jnp.transpose(key_logsum_part, (0, 2, 1))[..., None])
    grad_values = jnp.einsum(
        "shqk,sqhe->skhe",
        probs.astype(jnp.bfloat16),
        gradout_part,
        preferred_element_type=jnp.float32,
    )
    dprob = jnp.einsum("sqhe,skhe->shqk", gradout_part, values, preferred_element_type=jnp.float32)
    dscore = (probs * (dprob - jnp.transpose(key_delta_part, (0, 2, 1))[..., None])).astype(
        jnp.bfloat16
    )
    grad_keys = (
        jnp.einsum("shqk,sqhe->skhe", dscore, query_part, preferred_element_type=jnp.float32)
        * scaling
    )
    grad_keys, grad_values = (grad_keys, grad_values)
    grad_qkv = jnp.concatenate(
        [
            grad_queries.reshape(row_count, width),
            grad_keys.reshape(row_count, width),
            grad_values.reshape(row_count, width),
        ],
        axis=1,
    ).astype(jnp.bfloat16)
    grad_w_qkv = inner(normed1, grad_qkv)
    grad_normed1 = times_t(grad_qkv, w_qkv)
    norm_pull_one = jax.vjp(layer_norm, hidden0, gain_one32, shift_one32)[1]
    part_one, grad_gain_one, grad_shift_one = norm_pull_one(grad_normed1)
    grad_h0 = (grad_h1 + part_one).astype(jnp.bfloat16)
    input_grad = (
        times_t(grad_h0, w_enc).astype(jnp.bfloat16).reshape(seq_count, cell_count, gene_count)
    )
    enc_share = lax.psum_scatter(inner(express, grad_h0), "blk", scatter_dimension=0, tiled=True)
    shares = (
        lax.psum_scatter(grad_w_qkv, "blk", scatter_dimension=0, tiled=True),
        lax.psum_scatter(grad_w_out, "blk", scatter_dimension=0, tiled=True),
        lax.psum_scatter(grad_w_up, "blk", scatter_dimension=0, tiled=True),
        lax.psum_scatter(grad_w_down, "blk", scatter_dimension=0, tiled=True),
        lax.psum_scatter(grad_dec, "blk", scatter_dimension=0, tiled=True),
        lax.psum_scatter(grad_bias, "blk", scatter_dimension=0, tiled=True),
        lax.psum_scatter(grad_gain_one, "blk", scatter_dimension=0, tiled=True),
        lax.psum_scatter(grad_shift_one, "blk", scatter_dimension=0, tiled=True),
        lax.psum_scatter(grad_gain_two, "blk", scatter_dimension=0, tiled=True),
        lax.psum_scatter(grad_shift_two, "blk", scatter_dimension=0, tiled=True),
    )
    summed = (
        lax.psum(enc_share.astype(jnp.bfloat16), "dp").astype(jnp.float32),
        lax.psum(shares[0].astype(jnp.bfloat16), "dp").astype(jnp.float32),
        lax.psum(shares[1].astype(jnp.bfloat16), "dp").astype(jnp.float32),
        lax.psum(shares[2].astype(jnp.bfloat16), "dp").astype(jnp.float32),
        lax.psum(shares[3].astype(jnp.bfloat16), "dp").astype(jnp.float32),
        lax.psum(shares[4].astype(jnp.bfloat16), "dp").astype(jnp.float32),
        lax.psum(shares[5].astype(jnp.bfloat16), "dp").astype(jnp.float32),
        lax.psum(shares[6].astype(jnp.bfloat16), "dp").astype(jnp.float32),
        lax.psum(shares[7].astype(jnp.bfloat16), "dp").astype(jnp.float32),
        lax.psum(shares[8].astype(jnp.bfloat16), "dp").astype(jnp.float32),
        lax.psum(shares[9].astype(jnp.bfloat16), "dp").astype(jnp.float32),
    )
    return (
        logits.reshape(seq_count, cell_count, gene_count),
        input_grad,
        summed[0],
        summed[1],
        summed[2],
        summed[3],
        summed[4],
        summed[5],
        summed[6],
        summed[7],
        summed[8],
        summed[9],
        summed[10],
    )


AXES = ("y", "core", "z", "x")
SPLIT = 64


class Place:
    def __init__(self, sizes):
        self.sizes = sizes
        self.y, self.core, self.z, self.x = (lax.axis_index(name) for name in AXES)

    def send(self, value, move):
        ny, nc, nz, nx = self.sizes

        def flat(place):
            y, c, z, x = place
            return ((y * nc + c) * nz + z) * nx + x

        everywhere = [
            (y, c, z, x) for y in range(ny) for c in range(nc) for z in range(nz) for x in range(nx)
        ]
        return lax.ppermute(value, AXES, [(flat(p), flat(move(*p))) for p in everywhere])

    def swap_core(self, value):
        return self.send(value, lambda y, c, z, x: (y, 1 - c, z, x))

    def swap_x(self, value):
        return self.send(value, lambda y, c, z, x: (y, c, z, 1 - x))

    def swap_y(self, value):
        return self.send(value, lambda y, c, z, x: (1 - y, c, z, x))

    def shift_z(self, value, step):
        nz = self.sizes[2]
        return self.send(value, lambda y, c, z, x: (y, c, (z + step) % nz, x))

    def swap_z(self, value, distance):
        return self.send(value, lambda y, c, z, x: (y, c, z ^ distance, x))

    def exchange_z(self, value):
        return lax.all_to_all(value, "z", split_axis=0, concat_axis=0, tiled=True)

    def regroup(self, first, second):
        return (
            self.send(first, lambda y, c, z, x: (y, z // 2, 2 * c + z % 2, x)),
            self.send(second, lambda y, c, z, x: (y, z // 2, 2 * c + 1 - z % 2, x)),
        )

    def by_parity(self, pair):
        even = self.z % 2 == 0
        return jnp.where(even, pair[0], pair[1]), jnp.where(even, pair[1], pair[0])


def after(value, *earlier):
    return lax.optimization_barrier((value, *earlier))[0]


def coordinates():
    return tuple(lax.axis_index(name) for name in AXES)


def put(target, row, column, part):
    if not isinstance(row, int):
        row = pl.multiple_of(row, 16)
    if not isinstance(column, int):
        column = pl.multiple_of(column, 128)
    target[pl.ds(row, part.shape[0]), pl.ds(column, part.shape[1])] = part.astype(target.dtype)


def rows_at(source, row, count):
    return source[pl.ds(pl.multiple_of(row, 16), count), :]


def own_part(group, core, x, head):
    pair = jnp.where(x == 0, group[:, : 2 * head], group[:, 2 * head :])
    return jnp.where(core == 0, pair[:, :head], pair[:, head:])


def dot(left, right):
    return jnp.dot(left, right, preferred_element_type=jnp.float32)


def soft(queries, keys, allowed, scaling):
    scores = times_t(queries, keys) * scaling
    scores = jnp.where(allowed, scores, NEGATIVE)
    expo = jnp.exp(scores - jnp.max(scores, axis=-1, keepdims=True))
    return expo / jnp.sum(expo, axis=-1, keepdims=True)


def one_head(ref, part, heads, number, size):
    at = (part * heads + number) * size
    return ref[:, at : at + size]


def in_vmem(kernel, outs, *operands, flops=0, exps=0, scratch=()):
    whole = pl.BlockSpec(memory_space=pltpu.VMEM)
    shapes = [jax.ShapeDtypeStruct(shape, dtype) for shape, dtype in outs]
    held = sum(math.prod(v.shape) * v.dtype.itemsize for v in (*operands, *shapes))
    kept = sum(math.prod(shape) * jnp.dtype(dtype).itemsize for shape, dtype in scratch)
    results = pl.pallas_call(
        kernel,
        out_shape=shapes,
        in_specs=[whole] * len(operands),
        out_specs=[whole] * len(shapes),
        scratch_shapes=[pltpu.VMEM(shape, dtype) for shape, dtype in scratch],
        compiler_params=pltpu.CompilerParams(
            vmem_limit_bytes=(held // 2 if flops else held) + kept + (8 if flops else 4) * 1024 * 1024
        ),
        cost_estimate=pl.CostEstimate(flops=0, bytes_accessed=1024, transcendentals=0),
    )(*operands)
    return results if len(shapes) > 1 else results[0]


def sinusoids_of_whole(coords, width):
    quarter = width // 4
    frequency = jnp.exp(jnp.arange(quarter, dtype=jnp.float32) * (-math.log(10000.0) / quarter))
    number = jnp.arange(32, dtype=jnp.float32)[:, None]
    far, near = 32.0 * number * frequency, number * frequency
    far = jnp.concatenate([jnp.sin(far), jnp.cos(far)], axis=1)
    near = jnp.concatenate([jnp.sin(near), jnp.cos(near)], axis=1)
    parts = []
    for coord in coords:
        whole = coord.astype(jnp.int32)
        pick_far = (whole // 32 == jnp.arange(32)[None, :]).astype(jnp.float32)
        pick_near = (whole % 32 == jnp.arange(32)[None, :]).astype(jnp.float32)
        at_far = jnp.dot(pick_far, far, precision=lax.Precision.HIGHEST)
        at_near = jnp.dot(pick_near, near, precision=lax.Precision.HIGHEST)
        sin_far, cos_far = at_far[:, :quarter], at_far[:, quarter:]
        sin_near, cos_near = at_near[:, :quarter], at_near[:, quarter:]
        parts.append(sin_far * cos_near + cos_far * sin_near)
        parts.append(cos_far * cos_near - sin_far * sin_near)
    return jnp.concatenate(parts, axis=1)


def normalise(inputs):
    centre = inputs - jnp.mean(inputs, axis=-1, keepdims=True)
    factor = lax.rsqrt(jnp.mean(centre * centre, axis=-1, keepdims=True) + EPSILON)
    return centre * factor, factor


def normalise_back(inputs, grad, gain):
    normal, factor = normalise(inputs)
    scaled = grad * gain
    inside = (
        scaled
        - jnp.mean(scaled, axis=-1, keepdims=True)
        - normal * jnp.mean(scaled * normal, axis=-1, keepdims=True)
    )
    return (
        factor * inside,
        jnp.sum(grad * normal, axis=0, keepdims=True),
        jnp.sum(grad, axis=0, keepdims=True),
    )


def gelu_parts(value):
    root = math.sqrt(2.0 / math.pi)
    square = value * value
    bent = jnp.tanh(root * value * (1.0 + 0.044715 * square))
    slope = 0.5 * (1.0 + bent) + 0.5 * value * (1.0 - bent * bent) * root * (1.0 + 0.134145 * square)
    return 0.5 * value * (1.0 + bent), slope


def grouped_plan(
    sizes,
    counts,
    coords,
    segment_ids,
    logit_grad,
    enc_weight,
    qkv_weight,
    out_weight,
    up_weight,
    down_weight,
    dec_weight,
    dec_bias,
    norm1_gain,
    norm1_shift,
    norm2_gain,
    norm2_shift,
):
    place = Place(sizes)
    nz = sizes[2]
    seqs, cells, genes = counts.shape
    width = enc_weight.shape[1]
    block = enc_weight.shape[0]
    head = width // HEADS
    heads = HEADS // 4
    slice_width = width // 4
    own_rows = seqs * cells
    rows = 4 * own_rows
    ff = up_weight.shape[1]
    ff_slice = ff // 4
    bf16, f32 = jnp.bfloat16, jnp.float32

    half, quarter = block // 2, block // 4
    three = 3 * slice_width
    lanes = ff // (8 * nz)
    up_half = nz * lanes
    many = down_weight.shape[0] // 4
    half_rows = rows // 2
    pairs = heads * rows * rows
    square = 2 * rows * width * width // 4

    vectors = jnp.stack([dec_bias, norm1_gain, norm1_shift, norm2_gain, norm2_shift])
    tall = half + quarter + 16

    def whole_kernel(enc_ref, dec_ref, vectors_ref, out_ref):
        y, core, _, _ = coordinates()
        for k in range(nz):
            at = k * tall
            put(out_ref, at, 0, rows_at(enc_ref, core * half, half))
            put(out_ref, at + half, 0, rows_at(dec_ref, core * half + y * quarter, quarter))
            out_ref[at + half + quarter : at + tall, :] = jnp.zeros((16, width), bf16)
            out_ref[at + half + quarter : at + half + quarter + 5, :block] = vectors_ref[...]

    whole_own = in_vmem(
        whole_kernel, [((nz * tall, width), bf16)], enc_weight, dec_weight, vectors
    )
    whole_near = place.exchange_z(whole_own)

    express = jnp.log1p(counts.astype(f32)).astype(bf16)
    numbers = jnp.stack([coords[0], coords[1], segment_ids], axis=-1)
    beside = jnp.concatenate([numbers // SPLIT, numbers % SPLIT], axis=-1).astype(bf16)
    beside = jnp.pad(beside, ((0, 0), (0, 0), (0, 122)))
    pair = place.by_parity(
        jnp.concatenate([express, logit_grad, after(beside, whole_own)], axis=-1)
    )
    own_cells = place.regroup(*pair)
    def up_columns(up_ref, out_ref, first, x):
        y, core, _, _ = coordinates()
        for number in range(nz):
            at = ((2 * number + x) * 2 + core) * 2 + y
            out_ref[first : first + block, number * lanes : (number + 1) * lanes] = up_ref[
                :, pl.ds(pl.multiple_of(at * lanes, lanes), lanes)
            ]

    def qkv_columns(qkv_ref, out_ref, row, core, x, first, count):
        for at in range(3 * nz):
            columns = slice(at * 4 * head, (at + 1) * 4 * head)
            part = own_part(
                qkv_ref[pl.ds(pl.multiple_of(first, 16), count), columns], core, x, head
            )
            out_ref[row : row + count, at * head : (at + 1) * head] = part

    def theirs_kernel(qkv_ref, up_ref, out_ref):
        _, core, _, x = coordinates()
        qkv_columns(qkv_ref, out_ref, 0, core, 1 - x, 0, block)
        up_columns(up_ref, out_ref, block, 1 - x)
        out_ref[block:, up_half:] = jnp.zeros((block, three - up_half), bf16)

    theirs = in_vmem(
        theirs_kernel, [((2 * block, three), bf16)], after(qkv_weight, *pair), up_weight
    )
    theirs = place.swap_x(theirs)

    def qkv_kernel(qkv_ref, theirs_ref, out_weight_ref, own_ref, other_ref):
        y, core, _, x = coordinates()
        for out_ref, there in ((own_ref, y), (other_ref, 1 - y)):
            qkv_columns(qkv_ref, out_ref, 0, core, x, there * half, half)
            out_ref[half:, :three] = rows_at(theirs_ref, there * half, half)
            part = rows_at(out_weight_ref, core * half + there * quarter, quarter)
            for j in range(4):
                out_ref[j * quarter : (j + 1) * quarter, three:] = part[
                    :, j * slice_width : (j + 1) * slice_width
                ]

    qkv_own, qkv_own_far = in_vmem(
        qkv_kernel, [((block, width), bf16)] * 2, qkv_weight, theirs, out_weight
    )
    qkv_own = after(qkv_own, whole_near)

    def up_kernel(up_ref, theirs_ref, down_ref, out_ref):
        y, core, _, x = coordinates()
        up_columns(up_ref, out_ref, 0, x)
        out_ref[:block, up_half:] = theirs_ref[block:, :up_half]
        out_ref[block:, :] = rows_at(down_ref, (2 * core + y) * many, many)

    up_own = in_vmem(
        up_kernel, [((block + many, width), bf16)], up_weight, theirs, down_weight
    )
    up_near, up_far = [up_own], [place.swap_y(up_own)]
    for k in range(1, nz):
        up_near.append(place.shift_z(after(up_near[-1], whole_near), 1))
        if k < nz - 1:
            up_far.append(place.swap_y(up_near[-1]))
    up_far.append(place.shift_z(up_far[-1], 1))
    near = [qkv_own, place.shift_z(qkv_own, 1)]
    near += [place.shift_z(after(qkv_own, up_near[1]), k) for k in range(2, nz)]

    def two_kernel(one_ref, two_ref, out_ref):
        out_ref[:block, :] = one_ref[...]
        out_ref[block:, :] = two_ref[...]

    far_one = place.swap_y(near[1])
    far_two = place.swap_y(in_vmem(two_kernel, [((2 * block, width), bf16)], *near[2:]))
    qkv_pieces = (*near, qkv_own_far, far_one, far_two)

    whole_far = place.swap_x(whole_near)

    near_cells = jnp.concatenate(after(own_cells, near[1]), axis=0)
    near_cells = jnp.concatenate(
        [near_cells, after(
                place.swap_x(near_cells), up_far[0], *near[1:], up_near[1], whole_far,
                up_far[1], far_one,
            )], axis=0
    )
    far_cells = place.swap_core(near_cells)
    beside = jnp.concatenate([near_cells[:, 2 * genes :], far_cells[:, 2 * genes :]], axis=0).astype(f32)
    beside = beside[:, :3] * SPLIT + beside[:, 3:6]
    segment = beside[:, 2:3]
    segment_row = segment.reshape(1, rows)
    embed = sinusoids_of_whole((beside[:, 0:1], beside[:, 1:2]), width)


    def enc_half_kernel(near_ref, far_ref, out_ref, vectors_ref):
        _, _, _, x = coordinates()
        for dx, ref in enumerate((near_ref, far_ref)):
            for k in range(nz):
                at = k * tall
                put(out_ref, (2 * k + (x ^ dx)) * half, 0, ref[at : at + half, :])
                part = ref[at + half + quarter : at + tall, :block]
                put(vectors_ref, 0, (2 * k + (x ^ dx)) * block, part)

    enc_half, vectors = in_vmem(
        enc_half_kernel, [((genes // 2, width), bf16), ((16, width), f32)], whole_near, whole_far
    )
    enc_far = place.swap_core(enc_half)

    b_dec_row = vectors[0:1]

    def both_cores(near_ref, far_ref, out_ref):
        _, core, _, _ = coordinates()
        for dc, ref in enumerate((near_ref, far_ref)):
            for k in range(2 * nz):
                put(out_ref, k * block + (core ^ dc) * half, 0, ref[k * half : (k + 1) * half, :])

    def by_y(out_mine, out_send, value, first):
        y, _, _, _ = coordinates()
        for k in range(nz):
            low = value[:, 2 * k * block : (2 * k + 1) * block]
            high = value[:, (2 * k + 1) * block : (2 * k + 2) * block]
            at = slice(first, first + value.shape[0]), slice(k * block, (k + 1) * block)
            out_mine[at] = jnp.where(y == 0, low, high)
            out_send[at] = jnp.where(y == 0, high, low)

    def first_kernel(
        near_ref, far_ref, enc_near_ref, enc_far_ref, embed_ref, vectors_ref,
        enc_ref, hidden_ref, normed_ref, mine_ref, send_ref,
    ):
        both_cores(enc_near_ref, enc_far_ref, enc_ref)
        for number, ref in enumerate((near_ref, far_ref)):
            first = number * half_rows
            hidden = dot(ref[:, :genes], enc_ref[...]) + embed_ref[first : first + half_rows, :]
            if number == 0:
                hidden_ref[...] = hidden
            normal, _ = normalise(hidden)
            normed = (normal * vectors_ref[1:2, :] + vectors_ref[2:3, :]).astype(bf16)
            normed_ref[first : first + half_rows, :] = normed
            by_y(mine_ref, send_ref, normed, first)

    square_bf16, half_bf16 = ((width, width), bf16), ((half_rows, width), bf16)
    half_f32 = ((half_rows, width), f32)
    columns_bf16 = ((rows, width // 2), bf16)
    w_enc, hidden0, normed1, normed1_mine, normed1_send = in_vmem(
        first_kernel, [square_bf16, half_f32, ((rows, width), bf16), columns_bf16, columns_bf16],
        near_cells, far_cells, enc_half, enc_far, embed, vectors, flops=4 * square,
    )

    def attend_kernel(normed_ref, *refs):
        pieces, refs = refs[: nz + 3], refs[nz + 3 :]
        column_ref, row_ref, w_ref, w_out_ref, qkv_ref, out_ref, own_ref, send_ref = refs
        y, _, z, x = coordinates()
        parts = [(0, k, pieces[k], 0) for k in range(nz)]
        parts += [(1, k, pieces[nz + min(k, 2)], max(k - 2, 0) * block) for k in range(nz)]
        for dy, k, ref, first in parts:
            there = (z - k) % nz
            for dx in range(2):
                row = (2 * there + (x ^ dx)) * block + (y ^ dy) * half
                put(w_ref, row, 0, ref[first + dx * half : first + (dx + 1) * half, :three])
            for j in range(4):
                row = there * half + (y ^ dy) * quarter
                part = ref[first + j * quarter : first + (j + 1) * quarter, three:]
                put(w_out_ref, row, j * slice_width, part)
        qkv_ref[...] = dot(normed_ref[...], w_ref[...]).astype(bf16)
        allowed = column_ref[...] == row_ref[...]
        for number in range(heads):
            queries, keys, values = (one_head(qkv_ref, i, heads, number, head) for i in range(3))
            probs = soft(queries, keys, allowed, head**-0.5)
            at = slice(number * head, (number + 1) * head)
            out_ref[:, at] = dot(probs.astype(bf16), values).astype(bf16)
        own_ref[...] = dot(out_ref[:half_rows, :], w_out_ref[...])
        send_ref[...] = dot(out_ref[half_rows:, :], w_out_ref[...]).astype(bf16)

    w_qkv, w_out, qkv, context, own, send = in_vmem(
        attend_kernel,
        [((width, three), bf16), ((slice_width, width), bf16), ((rows, three), bf16),
         ((rows, slice_width), bf16), half_f32, half_bf16],
        after(normed1, up_near[2]), *qkv_pieces, segment, segment_row,
        flops=4 * square + 4 * pairs * head, exps=pairs,
    )

    def add_kernel(own_ref, other_ref, out_ref):
        out_ref[...] = (own_ref[...].astype(f32) + other_ref[...].astype(f32)).astype(out_ref.dtype)

    def add(own, other, dtype=bf16):
        return in_vmem(add_kernel, [(own.shape, dtype)], own, other)

    def sum_x(mine_ref, other_ref):
        other = jnp.concatenate([other_ref[own_rows:, :], other_ref[:own_rows, :]], axis=0)
        return mine_ref[...].astype(f32) + other.astype(f32)

    mine = add(own, after(place.swap_core(send), up_near[3], up_far[2]))

    def second_kernel(hidden_ref, mine_ref, other_ref, vectors_ref, out_ref, normed_ref):
        hidden = hidden_ref[...] + sum_x(mine_ref, other_ref)
        out_ref[...] = hidden
        normal, _ = normalise(hidden)
        normed_ref[...] = (normal * vectors_ref[3:4, :] + vectors_ref[4:5, :]).astype(bf16)

    hidden1, normed2 = in_vmem(
        second_kernel, [half_f32, half_bf16],
        hidden0, mine, after(place.swap_x(mine), up_far[3]), vectors,
    )
    normed2_far = place.swap_core(normed2)

    def dec_rows_kernel(near_ref, far_ref, out_ref):
        for dx, ref in enumerate((near_ref, far_ref)):
            for k in range(nz):
                at, out = k * tall + half, (dx * nz + k) * quarter
                out_ref[out : out + quarter, :] = ref[at : at + quarter, :]

    dec_near = in_vmem(
        dec_rows_kernel, [((2 * nz * quarter, genes), bf16)], whole_near, after(whole_far, qkv)
    )

    def dec_half_kernel(near_ref, far_ref, out_ref):
        y, _, _, x = coordinates()
        for dy, ref in enumerate((near_ref, far_ref)):
            for dx in range(2):
                for k in range(nz):
                    at = (dx * nz + k) * quarter
                    row = (2 * k + (x ^ dx)) * half + (y ^ dy) * quarter
                    put(out_ref, row, 0, ref[at : at + quarter, :])

    dec_half = in_vmem(
        dec_half_kernel, [((width // 2, genes), bf16)],
        dec_near, after(place.swap_y(dec_near), mine),
    )
    dec_far = place.swap_core(dec_half)

    def decoder_kernel(near_ref, far_ref, dec_near_ref, dec_far_ref, dec_ref, grad_ref, low_ref, sums_ref):
        both_cores(dec_near_ref, dec_far_ref, dec_ref)
        grad = times_t(near_ref[:, genes : 2 * genes], dec_ref[...])
        grad_ref[...] = grad
        low_ref[:half_rows, :] = grad.astype(bf16)
        low_ref[half_rows:, :] = times_t(far_ref[:, genes : 2 * genes], dec_ref[...]).astype(bf16)
        sums_ref[...] = sum(
            jnp.sum(ref[:, genes : 2 * genes].astype(f32), axis=0, keepdims=True)
            for ref in (near_ref, far_ref)
        )

    w_dec, grad_h2, grad_down, bias_sums = in_vmem(
        decoder_kernel,
        [square_bf16, half_f32, ((rows, width), bf16), ((1, width), f32)],
        near_cells, far_cells, dec_half, dec_far, flops=4 * square,
    )

    def feed_kernel(normed_ref, normed_far_ref, grad_ref, *refs):
        pieces, refs = refs[: 2 * nz], refs[2 * nz :]
        active_ref, grad_up_ref, own_ref, send_ref, own2_ref, send2_ref, mine_ref, theirs_ref = refs[:8]
        w_up_ref, w_down_ref, normed_all, back, ahead = refs[8:]
        y, _, z, x = coordinates()
        for dy in range(2):
            for k in range(nz):
                ref = pieces[dy * nz + k]
                there = (z - k) % nz
                for dx in range(2):
                    for number in range(nz):
                        at = dx * up_half + number * lanes
                        column = (2 * number + (y ^ dy)) * lanes
                        put(w_up_ref, (2 * there + (x ^ dx)) * block, column, ref[:block, at : at + lanes])
                put(w_down_ref, (2 * there + (y ^ dy)) * many, 0, ref[block:, :])
        normed_all[:half_rows, :] = normed_ref[...]
        normed_all[half_rows:, :] = normed_far_ref[...]
        by_y(mine_ref, theirs_ref, normed_ref[...], 0)
        by_y(mine_ref, theirs_ref, normed_far_ref[...], half_rows)
        chunk = 2 * lanes
        for number in range(nz):
            at = slice(number * chunk, (number + 1) * chunk)
            active, slope = gelu_parts(dot(normed_all[...], w_up_ref[:, at]))
            active = active.astype(bf16)
            active_ref[:, at] = active
            grad_up = (times_t(grad_ref[...], w_down_ref[at, :]) * slope).astype(bf16)
            grad_up_ref[:, at] = grad_up
            part, part2 = times_t(grad_up, w_up_ref[:, at]), dot(active, w_down_ref[at, :])
            back[...] = part if number == 0 else back[...] + part
            ahead[...] = part2 if number == 0 else ahead[...] + part2
        for sums, one, two in ((back, own_ref, send_ref), (ahead, own2_ref, send2_ref)):
            one[...] = sums[:half_rows, :]
            two[...] = sums[half_rows:, :].astype(bf16)

    full_bf16, full_f32 = ((rows, width), bf16), ((rows, width), f32)
    active, grad_up, own, send, own2, send2, normed2_mine, normed2_send = in_vmem(
        feed_kernel,
        [full_bf16, full_bf16, half_f32, half_bf16, half_f32, half_bf16, columns_bf16, columns_bf16],
        normed2, normed2_far, grad_down, *up_near, *up_far,
        flops=16 * square, exps=rows * ff_slice,
        scratch=[square_bf16, square_bf16, full_bf16, full_f32, full_f32],
    )
    mine = add(own, place.swap_core(send))

    def down_halve_kernel(value_ref, *refs):
        _, _, z, _ = coordinates()
        for number in range(2):
            for ref, low in ((refs[2 * number], z % 2), (refs[2 * number + 1], 1 - z % 2)):
                for high in range(2):
                    part = rows_at(value_ref, ((2 * high + low) * 2 + number) * many, many)
                    ref[high * many : (high + 1) * many, :] = part

    def sum_halve_kernel(*refs):
        parts, (out_ref, send_ref, all_ref) = refs[:-3], refs[-3:]
        at = 0
        for ref in parts[1:]:
            rows_here = slice(at, at + ref.shape[0])
            all_ref[rows_here, :] = parts[0][rows_here, :].astype(f32) + ref[...].astype(f32)
            at += ref.shape[0]
        _, _, z, _ = coordinates()
        count = out_ref.shape[0] // 2
        for high in range(2):
            at = slice(high * count, (high + 1) * count)
            out_ref[at, :] = rows_at(all_ref, (2 * high + z % 2) * count, count).astype(bf16)
            send_ref[at, :] = rows_at(all_ref, (2 * high + 1 - z % 2) * count, count).astype(bf16)

    def sum_halve(own, *others):
        shape = ((own.shape[0] // 2, own.shape[1]), bf16)
        return in_vmem(
            sum_halve_kernel, [shape, shape], own, *others, scratch=[(own.shape, f32)]
        )

    def add_split_kernel(own_ref, other_ref, out_ref, send_ref):
        _, _, z, _ = coordinates()
        count = out_ref.shape[0]
        for ref, part in ((out_ref, z // 2), (send_ref, 1 - z // 2)):
            own, other = (rows_at(r, part * count, count).astype(f32) for r in (own_ref, other_ref))
            ref[...] = (own + other).astype(bf16)

    def add_halve(own, other):
        shape = ((own.shape[0] // 2, own.shape[1]), bf16)
        return in_vmem(add_split_kernel, [shape, shape], own, other)

    down_one = in_vmem(
        down_halve_kernel, [((2 * many, width), bf16)] * 4, inner(active, grad_down).astype(bf16)
    )
    down_one = [down_one[:2], down_one[2:]]
    down_other = place.swap_z(down_one[0][1], 1)
    up_mine = inner(after(normed2_mine, mine), grad_up).astype(bf16)
    up_send = inner(after(normed2_send, mine), grad_up).astype(bf16)
    low_rows = nz * block // 2
    up_other_low = place.swap_y(up_send[:low_rows])
    ahead = add(own2, after(place.swap_core(send2), mine))
    other = after(place.swap_x(mine), up_mine, up_send, ahead, up_other_low, down_other)
    up_other_high = place.swap_y(after(up_send[low_rows:], other))
    down_two = [add_halve(down_one[0][0], after(down_other, other))]
    down_two_other = place.swap_z(down_two[0][1], 2)
    down_other = place.swap_z(after(down_one[1][1], other), 1)

    def back_kernel(hidden_ref, mine_ref, other_ref, grad_ref, vectors_ref, out_ref, low_ref, row):
        inside, gain_sums, shift_sums = normalise_back(
            hidden_ref[...], sum_x(mine_ref, other_ref), vectors_ref[row : row + 1, :]
        )
        grad = grad_ref[...] + inside
        if out_ref is not None:
            out_ref[...] = grad
        low_ref[:half_rows, :] = grad.astype(bf16)
        low_ref[half_rows:, :] = jnp.zeros((16, width), bf16)
        low_ref[half_rows : half_rows + 1, :] = gain_sums.astype(bf16)
        low_ref[half_rows + 1 : half_rows + 2, :] = shift_sums.astype(bf16)

    def second_back_kernel(*refs):
        back_kernel(*refs, 3)

    def first_back_kernel(*refs):
        back_kernel(*refs[:5], None, refs[5], 1)

    message = ((half_rows + 16, width), bf16)
    grad_h1, near_two = in_vmem(
        second_back_kernel, [half_f32, message], hidden1, mine, other, grad_h2, vectors
    )
    far_two = place.swap_core(near_two)
    ahead_other = place.swap_x(after(ahead, other))

    def attend_back_kernel(
        near_ref, far_ref, w_out_ref, qkv_ref, column_ref, row_ref, w_ref,
        out_ref, own_ref, send_ref, all_ref, grad_ref,
    ):
        all_ref[:half_rows, :] = near_ref[:half_rows, :]
        all_ref[half_rows:, :] = far_ref[:half_rows, :]
        grad_ref[...] = times_t(all_ref[...], w_out_ref[...]).astype(bf16)
        allowed = column_ref[...] == row_ref[...]
        scaling = head**-0.5
        for number in range(heads):
            queries, keys, values = (one_head(qkv_ref, i, heads, number, head) for i in range(3))
            grad = one_head(grad_ref, 0, heads, number, head)
            probs = soft(queries, keys, allowed, scaling)
            weighted = probs * times_t(grad, values)
            delta = jnp.sum(weighted, axis=-1, keepdims=True)
            dscore = (weighted - probs * delta).astype(bf16)
            parts = (
                dot(dscore, keys) * scaling,
                inner(dscore, queries) * scaling,
                inner(probs.astype(bf16), grad),
            )
            for i, part in enumerate(parts):
                at = (i * heads + number) * head
                out_ref[:, at : at + head] = part.astype(bf16)
        own_ref[...] = times_t(out_ref[:half_rows, :], w_ref[...])
        send_ref[...] = times_t(out_ref[half_rows:, :], w_ref[...]).astype(bf16)

    grad_qkv, own, send, grad_attn = in_vmem(
        attend_back_kernel, [((rows, three), bf16), half_f32, half_bf16, full_bf16],
        near_two, far_two, w_out, qkv, segment, segment_row, w_qkv,
        flops=4 * square + 10 * pairs * head, exps=pairs,
        scratch=[((rows, slice_width), bf16)],
    )
    qkv_send = inner(normed1_send, grad_qkv).astype(bf16)
    qkv_other = place.swap_y(qkv_send)
    up_other_high, down_other, down_two_other, ahead_other = after(
        (up_other_high, down_other, down_two_other, ahead_other), grad_qkv
    )
    mine = add(
        own, after(place.swap_core(send), qkv_send, up_other_high, down_other, down_two_other, ahead_other)
    )
    up_one = sum_halve(up_mine, up_other_low, after(up_other_high, mine))
    down_two.append(add_halve(down_one[1][0], after(down_other, mine)))
    down_sum = [add(down_two[0][0], after(down_two_other, mine))]
    other = place.swap_x(mine)
    down_two_other = place.swap_z(down_two[1][1], 2)
    up_one_other = place.swap_z(up_one[1], 1)

    qkv_mine = inner(normed1_mine, grad_qkv).astype(bf16)
    grad_w_out = inner(context, grad_attn).astype(bf16)

    other = after(other, qkv_mine, qkv_other, up_one_other, down_two_other)
    qkv_one = sum_halve(qkv_mine, qkv_other)
    qkv_one_other = place.swap_z(qkv_one[1], 1)
    up_two = add_halve(up_one[0], after(up_one_other, other))
    up_two_other = place.swap_z(up_two[1], 2)
    near_one = in_vmem(first_back_kernel, [message], hidden0, mine, other, grad_h1, vectors)
    far_one = place.swap_core(near_one)

    def hidden_kernel(hidden_ref, mine_ref, other_ref, low_ref, own_ref, send_ref):
        _, core, _, x = coordinates()
        hidden = (hidden_ref[...] + sum_x(mine_ref, other_ref)).astype(bf16)
        low_ref[...] = hidden[:own_rows, :]
        for k in range(nz):
            group = hidden[:, 2 * k * block : (2 * k + 2) * block]
            at = slice(k * half, (k + 1) * half)
            own_ref[:, at] = own_part(group, core, x, half)
            send_ref[:, at] = own_part(group, 1 - core, x, half)

    part_bf16 = ((half_rows, slice_width), bf16)
    hidden2, hidden2_own, hidden2_send = in_vmem(
        hidden_kernel, [((own_rows, width), bf16), part_bf16, part_bf16],
        hidden1, ahead, after(ahead_other, near_one),
    )
    hidden2_far = place.swap_core(hidden2_send)

    def few_rows_kernel(own_ref, far_ref, near_cells_ref, far_cells_ref, out_grad_ref, mine_ref, send_ref):
        y, _, _, _ = coordinates()
        columns = slice(genes, 2 * genes)
        grad = inner(own_ref[...], near_cells_ref[:, columns])
        grad = (grad + inner(far_ref[...], far_cells_ref[:, columns])).astype(bf16)
        mine_ref[...] = jnp.where(y == 0, out_grad_ref[...], grad)
        send_ref[...] = jnp.where(y == 0, grad, out_grad_ref[...])

    few_shape = ((slice_width, genes), bf16)
    few_mine, few_send = in_vmem(
        few_rows_kernel, [few_shape, few_shape],
        hidden2_own, hidden2_far, near_cells, far_cells, grad_w_out, flops=square,
    )
    few_other = place.swap_y(few_send)
    logits = (dot(hidden2, w_dec) + b_dec_row).astype(bf16)
    one, two = logits[:cells], logits[cells:]

    input_grad = times_t(near_one[:own_rows], w_enc).astype(bf16)

    def last_kernel(near_ref, far_ref, one_ref, one_far_ref, two_ref, two_far_ref, bias_ref, *refs):
        own_ref, send_ref, slice_ref, grad_ref, sums_ref = refs
        _, core, z, x = coordinates()
        for number, ref in enumerate((near_ref, far_ref)):
            for k in range(nz):
                group = ref[:, 2 * k * block : (2 * k + 2) * block]
                slice_ref[
                    number * half_rows : (number + 1) * half_rows, k * half : (k + 1) * half
                ] = own_part(group, core, x, half)
        grad_ref[...] = inner(slice_ref[:half_rows, :], one_ref[:half_rows, :]) + inner(
            slice_ref[half_rows:, :], one_far_ref[:half_rows, :]
        )
        sums_ref[...] = jnp.zeros((8, width), f32)
        sums_ref[0:1, :] = bias_ref[...]
        at = slice(half_rows, half_rows + 2)
        sums_ref[1:3, :] = one_ref[at, :].astype(f32) + one_far_ref[at, :].astype(f32)
        sums_ref[3:5, :] = two_ref[at, :].astype(f32) + two_far_ref[at, :].astype(f32)
        for ref, low in ((own_ref, z % 2), (send_ref, 1 - z % 2)):
            ref[...] = jnp.zeros(ref.shape, bf16)
            for high in range(2):
                there, first = 2 * high + low, high * (half + 16)
                ref[first : first + half, :] = rows_at(grad_ref, there * half, half).astype(bf16)
                column = pl.multiple_of((2 * there + x) * block, block)
                part = sums_ref[:, pl.ds(column, block)].astype(bf16)
                ref[first + half : first + half + 8, :block] = part

    last_one = in_vmem(
        last_kernel, [((2 * (half + 16), width), bf16)] * 2,
        near_cells, far_cells, near_one, after(far_one, few_other, qkv_one_other, up_two_other),
        near_two, far_two, bias_sums, flops=square,
        scratch=[((rows, slice_width), bf16), ((slice_width, width), f32), ((8, width), f32)],
    )
    last_one_other = place.swap_z(last_one[1], 1)
    qkv_two = add_halve(qkv_one[0], after(qkv_one_other, last_one[1]))
    qkv_two_other = place.swap_z(qkv_two[1], 2)
    up_sum = add(up_two[0], after(up_two_other, last_one[1]))
    up_other = place.swap_y(up_sum)
    down_sum.append(add(down_two[1][0], after(down_two_other, last_one[1])))
    down_sum = jnp.concatenate(down_sum, axis=0)
    down_other = place.swap_y(down_sum)
    few_one = sum_halve(few_mine, after(few_other, last_one[1]))
    few_one_other = place.swap_z(few_one[1], 1)

    def by_x_kernel(own_ref, other_ref, mine_ref, send_ref):
        y, _, _, x = coordinates()
        at = slice(0, mine_ref.shape[0]), slice(0, mine_ref.shape[1])
        mine_ref[...] = jnp.where(y == x, own_ref[at], other_ref[at])
        send_ref[...] = jnp.where(y == x, other_ref[at], own_ref[at])

    def by_x(own, other, width):
        return in_vmem(by_x_kernel, [((block, width), bf16)] * 2, own, other)

    qkv_sum = add(
        qkv_two[0], after(qkv_two_other, last_one_other, few_one_other, down_other, up_other)
    )
    qkv_other = place.swap_y(qkv_sum)
    up_mine, up_send = by_x(up_sum, up_other, ff_slice)
    up_both = place.swap_x(up_send)
    down_sum = add(down_sum, down_other)
    down_far = place.swap_core(down_sum)
    last_two = add_halve(last_one[0], after(last_one_other, qkv_sum))
    last_two_other = place.swap_z(last_two[1], 2)
    few_two = add_halve(few_one[0], after(few_one_other, qkv_sum))
    few_two_other = place.swap_z(few_two[1], 2)
    qkv_other, up_both, down_far, last_two_other, few_two_other, one, two = lax.optimization_barrier(
        (qkv_other, up_both, down_far, last_two_other, few_two_other, one, two)
    )
    last = add(last_two[0], last_two_other)
    last_other = place.swap_y(last)

    def last_add_kernel(one_ref, other_ref, out_ref, sums_ref):
        total = one_ref[...].astype(f32) + other_ref[...].astype(f32)
        out_ref[...] = total[:half, :].astype(bf16)
        sums_ref[...] = total[half : half + 8, :block]

    out_enc, sums = in_vmem(
        last_add_kernel, [((half, width), bf16), ((8, block), f32)], last, last_other
    )

    def halves_kernel(near_ref, far_ref, out_ref):
        _, core, _, _ = coordinates()
        count = near_ref.shape[0]
        for dc, ref in enumerate((near_ref, far_ref)):
            put(out_ref, (core ^ dc) * count, 0, ref[...])

    def halves(near, far):
        return in_vmem(
            halves_kernel, [((2 * near.shape[0], near.shape[1]), f32)], near, far
        )

    out_enc = halves(out_enc, place.swap_core(out_enc))

    up_both = jnp.concatenate([up_mine, up_both], axis=0)

    def up_out_kernel(near_ref, far_ref, out_ref):
        _, core, _, x = coordinates()
        for dc, ref in enumerate((near_ref, far_ref)):
            for dx in range(2):
                for k in range(nz):
                    part = ref[dx * block : (dx + 1) * block, 2 * k * lanes : 2 * (k + 1) * lanes]
                    put(out_ref, 0, ((2 * k + (x ^ dx)) * 2 + (core ^ dc)) * 2 * lanes, part)


    qkv_mine, qkv_send = by_x(qkv_sum, qkv_other, three)
    qkv_there = place.swap_x(qkv_send)
    qkv_both = jnp.concatenate([qkv_mine, qkv_there], axis=0)
    out_down = halves(down_sum, after(down_far, qkv_there))
    up_far_both = after(place.swap_core(up_both), qkv_there)
    out_up = in_vmem(up_out_kernel, [((block, ff), f32)], up_both, up_far_both)
    few_sum = add(few_two[0], few_two_other)
    pair = place.regroup(
        *(
            jnp.concatenate(
                [part, after(input_grad[i * cells : (i + 1) * cells], qkv_other)], axis=1
            )
            for i, part in enumerate((one, two))
        )
    )
    pair = jnp.stack(place.by_parity(pair))
    logits, input_grad = pair[:, :, :genes], pair[:, :, genes:]

    def few_kernel(own_ref, other_ref, out_ref):
        y, _, _, _ = coordinates()
        put(out_ref, y * half, 0, own_ref[...])
        put(out_ref, (1 - y) * half, 0, other_ref[...])

    few = in_vmem(few_kernel, [((block, genes), bf16)], few_sum, place.swap_y(few_sum))

    def few_out_kernel(near_ref, far_ref, out_ref, dec_ref):
        _, core, _, _ = coordinates()
        for dc, ref in enumerate((near_ref, far_ref)):
            put(out_ref, (core ^ dc) * half, 0, ref[:half, :])
            put(dec_ref, (core ^ dc) * half, 0, ref[half:, :])

    out_out, out_dec = in_vmem(
        few_out_kernel, [((block, width), f32), ((block, genes), f32)], few, place.swap_core(few)
    )

    def qkv_out_kernel(near_ref, far_ref, out_ref):
        _, core, _, x = coordinates()
        for dx in range(2):
            for number in range(3 * nz):
                at = slice(dx * block, (dx + 1) * block), slice(number * head, (number + 1) * head)
                near_part, far_part = near_ref[at].astype(f32), far_ref[at].astype(f32)
                low = jnp.where(core == 0, near_part, far_part)
                high = jnp.where(core == 0, far_part, near_part)
                put(
                    out_ref, 0, number * 4 * head + (x ^ dx) * 2 * head,
                    jnp.concatenate([low, high], axis=1),
                )

    out_qkv = in_vmem(
        qkv_out_kernel, [((block, 3 * width), f32)], qkv_both, place.swap_core(qkv_both)
    )
    return (
        logits, input_grad, out_enc, out_qkv, out_out, out_up, out_down, out_dec,
        sums[0], sums[1], sums[2], sums[3], sums[4],
    )


IN_SPECS = (
    ("dp", "blk", None), (None, "dp", "blk"), ("dp", "blk"), ("dp", "blk", None),
    *[("blk", None)] * 6, *[("blk",)] * 5,
)
OUT_SPECS = (("dp", "blk", None), ("dp", "blk", None), *[("blk", None)] * 6, *[("blk",)] * 5)


def solution(mesh):
    groups, blocks = mesh.shape["dp"], mesh.shape["blk"]

    def run(*args):
        seqs = args[0].shape[0] // groups
        if groups == 4 and blocks == 4 * seqs and seqs == 2 and HEADS == 4 * (blocks // 2):
            sizes = (groups // 2, 2, blocks // 2, 2)
            fine = Mesh(mesh.devices.reshape(sizes), AXES)
            names = {"dp": ("y", "core"), "blk": ("z", "x"), None: None}
            plan = functools.partial(grouped_plan, sizes)
        else:
            fine, names, plan = mesh, {"dp": "dp", "blk": "blk", None: None}, spread_plan
        specs = lambda entries: tuple(P(*[names[axis] for axis in entry]) for entry in entries)
        return jax.shard_map(
            plan, mesh=fine, in_specs=specs(IN_SPECS), out_specs=specs(OUT_SPECS), check_vma=False
        )(*args)

    return run
```

```python
import functools
import math

import jax
import jax.numpy as jnp
from jax import lax
from jax.experimental import pallas as pl
from jax.experimental.pallas import tpu as pltpu
from jax.sharding import Mesh
from jax.sharding import PartitionSpec as P

HEADS = 16


NEGATIVE = -1e30
EPSILON = 1e-05


def layer_norm(inputs, gain_vec, shift_vec):
    centre = inputs - jnp.mean(inputs, axis=-1, keepdims=True)
    spread = jnp.mean(centre * centre, axis=-1, keepdims=True)
    return centre * lax.rsqrt(spread + EPSILON) * gain_vec + shift_vec


def sinusoids(coords, width):
    quarter = width // 4
    frequency = jnp.exp(jnp.arange(quarter, dtype=jnp.float32) * (-math.log(10000.0) / quarter))
    first_angle = coords[0].astype(jnp.float32)[..., None] * frequency
    second_angle = coords[1].astype(jnp.float32)[..., None] * frequency
    return jnp.concatenate(
        [jnp.sin(first_angle), jnp.cos(first_angle), jnp.sin(second_angle), jnp.cos(second_angle)],
        axis=-1,
    )


def inner(left, right):
    return lax.dot_general(
        left, right, (((0,), (0,)), ((), ())), preferred_element_type=jnp.float32
    )


def times_t(left, right):
    return lax.dot_general(
        left, right, (((1,), (1,)), ((), ())), preferred_element_type=jnp.float32
    )


def spread_plan(
    counts,
    coords,
    segment_ids,
    logit_grad,
    enc_weight,
    qkv_weight,
    out_weight,
    up_weight,
    down_weight,
    dec_weight,
    dec_bias,
    norm1_gain,
    norm1_shift,
    norm2_gain,
    norm2_shift,
):
    gathered = (
        lax.all_gather(enc_weight, "blk", axis=0, tiled=True),
        lax.all_gather(qkv_weight, "blk", axis=0, tiled=True),
        lax.all_gather(out_weight, "blk", axis=0, tiled=True),
        lax.all_gather(up_weight, "blk", axis=0, tiled=True),
        lax.all_gather(down_weight, "blk", axis=0, tiled=True),
        lax.all_gather(dec_weight, "blk", axis=0, tiled=True),
        lax.all_gather(dec_bias, "blk", axis=0, tiled=True),
        lax.all_gather(norm1_gain, "blk", axis=0, tiled=True),
        lax.all_gather(norm1_shift, "blk", axis=0, tiled=True),
        lax.all_gather(norm2_gain, "blk", axis=0, tiled=True),
        lax.all_gather(norm2_shift, "blk", axis=0, tiled=True),
    )
    w_enc, w_qkv, w_out, w_up, w_down, w_dec, b_dec, gain_one, shift_one, gain_two, shift_two = (
        gathered
    )
    seg_all = lax.all_gather(segment_ids, "blk", axis=1, tiled=True)
    seq_count, cell_count, gene_count = counts.shape
    width = w_enc.shape[1]
    head_count = HEADS
    head_size = width // head_count
    scaling = head_size ** (-0.5)
    row_count = seq_count * cell_count
    express = (
        jnp.log1p(counts.astype(jnp.float32)).astype(jnp.bfloat16).reshape(row_count, gene_count)
    )
    embed = sinusoids(coords, width).reshape(row_count, width)
    hidden0 = jnp.dot(express, w_enc, preferred_element_type=jnp.float32) + embed
    gain_one32 = gain_one.astype(jnp.float32)
    shift_one32 = shift_one.astype(jnp.float32)
    gain_two32 = gain_two.astype(jnp.float32)
    shift_two32 = shift_two.astype(jnp.float32)
    normed1 = layer_norm(hidden0, gain_one32, shift_one32).astype(jnp.bfloat16)
    qkv = jnp.dot(normed1, w_qkv, preferred_element_type=jnp.float32).astype(jnp.bfloat16)
    queries = qkv[:, :width].reshape(seq_count, cell_count, head_count, head_size)
    key_rows = qkv[:, width : 2 * width].reshape(seq_count, cell_count, head_count, head_size)
    values = qkv[:, 2 * width :].reshape(seq_count, cell_count, head_count, head_size)

    def masked_scores(query_part, key_part, seg_query, seg_key):
        scores = (
            jnp.einsum("sqhe,skhe->shqk", query_part, key_part, preferred_element_type=jnp.float32)
            * scaling
        )
        return jnp.where(seg_query[:, None, :, None] == seg_key[:, None, None, :], scores, NEGATIVE)

    start_max = jnp.full((seq_count, head_count, cell_count), NEGATIVE, jnp.float32)
    piece = (
        lax.all_gather(key_rows, "blk", axis=1, tiled=True),
        lax.all_gather(values, "blk", axis=1, tiled=True),
    )
    seg_part = seg_all
    incoming = (piece[0], piece[1], seg_part)
    running_max = start_max
    key_part, value_part, context_seg_part = incoming
    query_part = queries
    scores = masked_scores(query_part, key_part, segment_ids, context_seg_part)
    newest = jnp.maximum(running_max, jnp.max(scores, axis=-1))
    expo = jnp.exp(scores - newest[..., None])
    running_sum = jnp.sum(expo, axis=-1)
    update = jnp.einsum(
        "shqk,skhe->sqhe", expo.astype(jnp.bfloat16), value_part, preferred_element_type=jnp.float32
    )
    weighted = update
    running_max, running_sum, weighted = (newest, running_sum, weighted)
    context32 = weighted / jnp.transpose(running_sum, (0, 2, 1))[..., None]
    logsum = jnp.transpose(running_max + jnp.log(running_sum), (0, 2, 1))
    context = context32.astype(jnp.bfloat16).reshape(row_count, width)
    hidden1 = hidden0 + jnp.dot(context, w_out, preferred_element_type=jnp.float32)
    normed2 = layer_norm(hidden1, gain_two32, shift_two32).astype(jnp.bfloat16)
    up_value = jnp.dot(normed2, w_up, preferred_element_type=jnp.float32)
    active = jax.nn.gelu(up_value).astype(jnp.bfloat16)
    hidden2 = hidden1 + jnp.dot(active, w_down, preferred_element_type=jnp.float32)
    hidden2_low = hidden2.astype(jnp.bfloat16)
    logits = (
        jnp.dot(hidden2_low, w_dec, preferred_element_type=jnp.float32) + b_dec.astype(jnp.float32)
    ).astype(jnp.bfloat16)
    cotangent = logit_grad.reshape(row_count, gene_count)
    grad_dec = inner(hidden2_low, cotangent)
    grad_bias = jnp.sum(cotangent.astype(jnp.float32), axis=0)
    grad_h2 = times_t(cotangent, w_dec)
    grad_down = grad_h2.astype(jnp.bfloat16)
    grad_w_down = inner(active, grad_down)
    grad_active = times_t(grad_down, w_down)
    gelu_pull = jax.vjp(jax.nn.gelu, up_value)[1]
    grad_up = gelu_pull(grad_active)[0].astype(jnp.bfloat16)
    grad_w_up = inner(normed2, grad_up)
    grad_normed2 = times_t(grad_up, w_up)
    norm_pull_two = jax.vjp(layer_norm, hidden1, gain_two32, shift_two32)[1]
    part_two, grad_gain_two, grad_shift_two = norm_pull_two(grad_normed2)
    grad_h1 = grad_h2 + part_two
    grad_attn = grad_h1.astype(jnp.bfloat16)
    grad_w_out = inner(context, grad_attn)
    grad_context = (
        times_t(grad_attn, w_out)
        .astype(jnp.bfloat16)
        .reshape(seq_count, cell_count, head_count, head_size)
    )
    delta = jnp.sum(grad_context.astype(jnp.float32) * context32, axis=-1)
    logsum_all, delta_all = (
        lax.all_gather(logsum, "blk", axis=1, tiled=True),
        lax.all_gather(delta, "blk", axis=1, tiled=True),
    )
    seg_part = seg_all
    query_seg_part = seg_part
    query_part = queries
    gradout_part = grad_context
    logsum_part = logsum
    delta_part = delta
    scores = masked_scores(query_part, key_part, segment_ids, query_seg_part)
    probs = jnp.exp(scores - jnp.transpose(logsum_part, (0, 2, 1))[..., None])
    dprob = jnp.einsum(
        "sqhe,skhe->shqk", gradout_part, value_part, preferred_element_type=jnp.float32
    )
    dscore = (probs * (dprob - jnp.transpose(delta_part, (0, 2, 1))[..., None])).astype(
        jnp.bfloat16
    )
    grad_queries = (
        jnp.einsum("shqk,skhe->sqhe", dscore, key_part, preferred_element_type=jnp.float32)
        * scaling
    )
    piece = (
        lax.all_gather(queries, "blk", axis=1, tiled=True),
        lax.all_gather(grad_context, "blk", axis=1, tiled=True),
    )
    seg_part = seg_all
    logsum_part = logsum_all
    delta_part = delta_all
    incoming = (piece[0], piece[1], logsum_part, delta_part, seg_part)
    query_part, gradout_part, key_logsum_part, key_delta_part, key_seg_part = incoming
    key_part = key_rows
    scores = masked_scores(query_part, key_part, key_seg_part, segment_ids)
    probs = jnp.exp(scores - jnp.transpose(key_logsum_part, (0, 2, 1))[..., None])
    grad_values = jnp.einsum(
        "shqk,sqhe->skhe",
        probs.astype(jnp.bfloat16),
        gradout_part,
        preferred_element_type=jnp.float32,
    )
    dprob = jnp.einsum("sqhe,skhe->shqk", gradout_part, values, preferred_element_type=jnp.float32)
    dscore = (probs * (dprob - jnp.transpose(key_delta_part, (0, 2, 1))[..., None])).astype(
        jnp.bfloat16
    )
    grad_keys = (
        jnp.einsum("shqk,sqhe->skhe", dscore, query_part, preferred_element_type=jnp.float32)
        * scaling
    )
    grad_keys, grad_values = (grad_keys, grad_values)
    grad_qkv = jnp.concatenate(
        [
            grad_queries.reshape(row_count, width),
            grad_keys.reshape(row_count, width),
            grad_values.reshape(row_count, width),
        ],
        axis=1,
    ).astype(jnp.bfloat16)
    grad_w_qkv = inner(normed1, grad_qkv)
    grad_normed1 = times_t(grad_qkv, w_qkv)
    norm_pull_one = jax.vjp(layer_norm, hidden0, gain_one32, shift_one32)[1]
    part_one, grad_gain_one, grad_shift_one = norm_pull_one(grad_normed1)
    grad_h0 = (grad_h1 + part_one).astype(jnp.bfloat16)
    input_grad = (
        times_t(grad_h0, w_enc).astype(jnp.bfloat16).reshape(seq_count, cell_count, gene_count)
    )
    enc_share = lax.psum_scatter(inner(express, grad_h0), "blk", scatter_dimension=0, tiled=True)
    shares = (
        lax.psum_scatter(grad_w_qkv, "blk", scatter_dimension=0, tiled=True),
        lax.psum_scatter(grad_w_out, "blk", scatter_dimension=0, tiled=True),
        lax.psum_scatter(grad_w_up, "blk", scatter_dimension=0, tiled=True),
        lax.psum_scatter(grad_w_down, "blk", scatter_dimension=0, tiled=True),
        lax.psum_scatter(grad_dec, "blk", scatter_dimension=0, tiled=True),
        lax.psum_scatter(grad_bias, "blk", scatter_dimension=0, tiled=True),
        lax.psum_scatter(grad_gain_one, "blk", scatter_dimension=0, tiled=True),
        lax.psum_scatter(grad_shift_one, "blk", scatter_dimension=0, tiled=True),
        lax.psum_scatter(grad_gain_two, "blk", scatter_dimension=0, tiled=True),
        lax.psum_scatter(grad_shift_two, "blk", scatter_dimension=0, tiled=True),
    )
    summed = (
        lax.psum(enc_share.astype(jnp.bfloat16), "dp").astype(jnp.float32),
        lax.psum(shares[0].astype(jnp.bfloat16), "dp").astype(jnp.float32),
        lax.psum(shares[1].astype(jnp.bfloat16), "dp").astype(jnp.float32),
        lax.psum(shares[2].astype(jnp.bfloat16), "dp").astype(jnp.float32),
        lax.psum(shares[3].astype(jnp.bfloat16), "dp").astype(jnp.float32),
        lax.psum(shares[4].astype(jnp.bfloat16), "dp").astype(jnp.float32),
        lax.psum(shares[5].astype(jnp.bfloat16), "dp").astype(jnp.float32),
        lax.psum(shares[6].astype(jnp.bfloat16), "dp").astype(jnp.float32),
        lax.psum(shares[7].astype(jnp.bfloat16), "dp").astype(jnp.float32),
        lax.psum(shares[8].astype(jnp.bfloat16), "dp").astype(jnp.float32),
        lax.psum(shares[9].astype(jnp.bfloat16), "dp").astype(jnp.float32),
    )
    return (
        logits.reshape(seq_count, cell_count, gene_count),
        input_grad,
        summed[0],
        summed[1],
        summed[2],
        summed[3],
        summed[4],
        summed[5],
        summed[6],
        summed[7],
        summed[8],
        summed[9],
        summed[10],
    )


AXES = ("y", "core", "z", "x")
SPLIT = 64


class Place:
    def __init__(self, sizes):
        self.sizes = sizes
        self.y, self.core, self.z, self.x = (lax.axis_index(name) for name in AXES)

    def send(self, value, move):
        ny, nc, nz, nx = self.sizes

        def flat(place):
            y, c, z, x = place
            return ((y * nc + c) * nz + z) * nx + x

        everywhere = [
            (y, c, z, x) for y in range(ny) for c in range(nc) for z in range(nz) for x in range(nx)
        ]
        return lax.ppermute(value, AXES, [(flat(p), flat(move(*p))) for p in everywhere])

    def swap_core(self, value):
        return self.send(value, lambda y, c, z, x: (y, 1 - c, z, x))

    def swap_x(self, value):
        return self.send(value, lambda y, c, z, x: (y, c, z, 1 - x))

    def swap_y(self, value):
        return self.send(value, lambda y, c, z, x: (1 - y, c, z, x))

    def shift_z(self, value, step):
        nz = self.sizes[2]
        return self.send(value, lambda y, c, z, x: (y, c, (z + step) % nz, x))

    def swap_z(self, value, distance):
        return self.send(value, lambda y, c, z, x: (y, c, z ^ distance, x))

    def exchange_z(self, value):
        return lax.all_to_all(value, "z", split_axis=0, concat_axis=0, tiled=True)

    def regroup(self, first, second):
        return (
            self.send(first, lambda y, c, z, x: (y, z // 2, 2 * c + z % 2, x)),
            self.send(second, lambda y, c, z, x: (y, z // 2, 2 * c + 1 - z % 2, x)),
        )

    def by_parity(self, pair):
        even = self.z % 2 == 0
        return jnp.where(even, pair[0], pair[1]), jnp.where(even, pair[1], pair[0])


def after(value, *earlier):
    return lax.optimization_barrier((value, *earlier))[0]


def coordinates():
    return tuple(lax.axis_index(name) for name in AXES)


def put(target, row, column, part):
    if not isinstance(row, int):
        row = pl.multiple_of(row, 16)
    if not isinstance(column, int):
        column = pl.multiple_of(column, 128)
    target[pl.ds(row, part.shape[0]), pl.ds(column, part.shape[1])] = part.astype(target.dtype)


def rows_at(source, row, count):
    return source[pl.ds(pl.multiple_of(row, 16), count), :]


def own_part(group, core, x, head):
    pair = jnp.where(x == 0, group[:, : 2 * head], group[:, 2 * head :])
    return jnp.where(core == 0, pair[:, :head], pair[:, head:])


def dot(left, right):
    return jnp.dot(left, right, preferred_element_type=jnp.float32)


def soft(queries, keys, allowed, scaling):
    scores = times_t(queries, keys) * scaling
    scores = jnp.where(allowed, scores, NEGATIVE)
    expo = jnp.exp(scores - jnp.max(scores, axis=-1, keepdims=True))
    return expo / jnp.sum(expo, axis=-1, keepdims=True)


def one_head(ref, part, heads, number, size):
    at = (part * heads + number) * size
    return ref[:, at : at + size]


def in_vmem(kernel, outs, *operands, flops=0, exps=0, scratch=()):
    whole = pl.BlockSpec(memory_space=pltpu.VMEM)
    shapes = [jax.ShapeDtypeStruct(shape, dtype) for shape, dtype in outs]
    held = sum(math.prod(v.shape) * v.dtype.itemsize for v in (*operands, *shapes))
    kept = sum(math.prod(shape) * jnp.dtype(dtype).itemsize for shape, dtype in scratch)
    results = pl.pallas_call(
        kernel,
        out_shape=shapes,
        in_specs=[whole] * len(operands),
        out_specs=[whole] * len(shapes),
        scratch_shapes=[pltpu.VMEM(shape, dtype) for shape, dtype in scratch],
        compiler_params=pltpu.CompilerParams(
            vmem_limit_bytes=(held // 2 if flops else held) + kept + (8 if flops else 4) * 1024 * 1024
        ),
        cost_estimate=pl.CostEstimate(flops=0, bytes_accessed=1024, transcendentals=0),
    )(*operands)
    return results if len(shapes) > 1 else results[0]


def sinusoids_of_whole(coords, width):
    quarter = width // 4
    frequency = jnp.exp(jnp.arange(quarter, dtype=jnp.float32) * (-math.log(10000.0) / quarter))
    number = jnp.arange(32, dtype=jnp.float32)[:, None]
    far, near = 32.0 * number * frequency, number * frequency
    far = jnp.concatenate([jnp.sin(far), jnp.cos(far)], axis=1)
    near = jnp.concatenate([jnp.sin(near), jnp.cos(near)], axis=1)
    parts = []
    for coord in coords:
        whole = coord.astype(jnp.int32)
        pick_far = (whole // 32 == jnp.arange(32)[None, :]).astype(jnp.float32)
        pick_near = (whole % 32 == jnp.arange(32)[None, :]).astype(jnp.float32)
        at_far = jnp.dot(pick_far, far, precision=lax.Precision.HIGHEST)
        at_near = jnp.dot(pick_near, near, precision=lax.Precision.HIGHEST)
        sin_far, cos_far = at_far[:, :quarter], at_far[:, quarter:]
        sin_near, cos_near = at_near[:, :quarter], at_near[:, quarter:]
        parts.append(sin_far * cos_near + cos_far * sin_near)
        parts.append(cos_far * cos_near - sin_far * sin_near)
    return jnp.concatenate(parts, axis=1)


def normalise(inputs):
    centre = inputs - jnp.mean(inputs, axis=-1, keepdims=True)
    factor = lax.rsqrt(jnp.mean(centre * centre, axis=-1, keepdims=True) + EPSILON)
    return centre * factor, factor


def normalise_back(inputs, grad, gain):
    normal, factor = normalise(inputs)
    scaled = grad * gain
    inside = (
        scaled
        - jnp.mean(scaled, axis=-1, keepdims=True)
        - normal * jnp.mean(scaled * normal, axis=-1, keepdims=True)
    )
    return (
        factor * inside,
        jnp.sum(grad * normal, axis=0, keepdims=True),
        jnp.sum(grad, axis=0, keepdims=True),
    )


def gelu_parts(value):
    root = math.sqrt(2.0 / math.pi)
    square = value * value
    bent = jnp.tanh(root * value * (1.0 + 0.044715 * square))
    slope = 0.5 * (1.0 + bent) + 0.5 * value * (1.0 - bent * bent) * root * (1.0 + 0.134145 * square)
    return 0.5 * value * (1.0 + bent), slope


def grouped_plan(
    sizes,
    counts,
    coords,
    segment_ids,
    logit_grad,
    enc_weight,
    qkv_weight,
    out_weight,
    up_weight,
    down_weight,
    dec_weight,
    dec_bias,
    norm1_gain,
    norm1_shift,
    norm2_gain,
    norm2_shift,
):
    place = Place(sizes)
    nz = sizes[2]
    seqs, cells, genes = counts.shape
    width = enc_weight.shape[1]
    block = enc_weight.shape[0]
    head = width // HEADS
    heads = HEADS // 4
    slice_width = width // 4
    own_rows = seqs * cells
    rows = 4 * own_rows
    ff = up_weight.shape[1]
    ff_slice = ff // 4
    bf16, f32 = jnp.bfloat16, jnp.float32

    half, quarter = block // 2, block // 4
    three = 3 * slice_width
    lanes = ff // (8 * nz)
    up_half = nz * lanes
    many = down_weight.shape[0] // 4
    half_rows = rows // 2
    pairs = heads * rows * rows
    square = 2 * rows * width * width // 4

    vectors = jnp.stack([dec_bias, norm1_gain, norm1_shift, norm2_gain, norm2_shift])
    tall = half + quarter + 16

    def whole_kernel(enc_ref, dec_ref, vectors_ref, out_ref):
        y, core, _, _ = coordinates()
        for k in range(nz):
            at = k * tall
            put(out_ref, at, 0, rows_at(enc_ref, core * half, half))
            put(out_ref, at + half, 0, rows_at(dec_ref, core * half + y * quarter, quarter))
            out_ref[at + half + quarter : at + tall, :] = jnp.zeros((16, width), bf16)
            out_ref[at + half + quarter : at + half + quarter + 5, :block] = vectors_ref[...]

    whole_own = in_vmem(
        whole_kernel, [((nz * tall, width), bf16)], enc_weight, dec_weight, vectors
    )
    whole_near = place.exchange_z(whole_own)

    express = jnp.log1p(counts.astype(f32)).astype(bf16)
    numbers = jnp.stack([coords[0], coords[1], segment_ids], axis=-1)
    beside = jnp.concatenate([numbers // SPLIT, numbers % SPLIT], axis=-1).astype(bf16)
    beside = jnp.pad(beside, ((0, 0), (0, 0), (0, 122)))
    pair = place.by_parity(
        jnp.concatenate([express, logit_grad, after(beside, whole_own)], axis=-1)
    )
    own_cells = place.regroup(*pair)
    def up_columns(up_ref, out_ref, first, x):
        y, core, _, _ = coordinates()
        for number in range(nz):
            at = ((2 * number + x) * 2 + core) * 2 + y
            out_ref[first : first + block, number * lanes : (number + 1) * lanes] = up_ref[
                :, pl.ds(pl.multiple_of(at * lanes, lanes), lanes)
            ]

    def qkv_columns(qkv_ref, out_ref, row, core, x, first, count):
        for at in range(3 * nz):
            columns = slice(at * 4 * head, (at + 1) * 4 * head)
            part = own_part(
                qkv_ref[pl.ds(pl.multiple_of(first, 16), count), columns], core, x, head
            )
            out_ref[row : row + count, at * head : (at + 1) * head] = part

    def theirs_kernel(qkv_ref, up_ref, out_ref):
        _, core, _, x = coordinates()
        qkv_columns(qkv_ref, out_ref, 0, core, 1 - x, 0, block)
        up_columns(up_ref, out_ref, block, 1 - x)
        out_ref[block:, up_half:] = jnp.zeros((block, three - up_half), bf16)

    theirs = in_vmem(
        theirs_kernel, [((2 * block, three), bf16)], after(qkv_weight, *pair), up_weight
    )
    theirs = place.swap_x(theirs)

    def qkv_kernel(qkv_ref, theirs_ref, out_weight_ref, own_ref, other_ref):
        y, core, _, x = coordinates()
        for out_ref, there in ((own_ref, y), (other_ref, 1 - y)):
            qkv_columns(qkv_ref, out_ref, 0, core, x, there * half, half)
            out_ref[half:, :three] = rows_at(theirs_ref, there * half, half)
            part = rows_at(out_weight_ref, core * half + there * quarter, quarter)
            for j in range(4):
                out_ref[j * quarter : (j + 1) * quarter, three:] = part[
                    :, j * slice_width : (j + 1) * slice_width
                ]

    qkv_own, qkv_own_far = in_vmem(
        qkv_kernel, [((block, width), bf16)] * 2, qkv_weight, theirs, out_weight
    )
    qkv_own = after(qkv_own, whole_near)

    def up_kernel(up_ref, theirs_ref, down_ref, out_ref):
        y, core, _, x = coordinates()
        up_columns(up_ref, out_ref, 0, x)
        out_ref[:block, up_half:] = theirs_ref[block:, :up_half]
        out_ref[block:, :] = rows_at(down_ref, (2 * core + y) * many, many)

    up_own = in_vmem(
        up_kernel, [((block + many, width), bf16)], up_weight, theirs, down_weight
    )
    up_near, up_far = [up_own], [place.swap_y(up_own)]
    for k in range(1, nz):
        up_near.append(place.shift_z(after(up_near[-1], whole_near), 1))
        if k < nz - 1:
            up_far.append(place.swap_y(up_near[-1]))
    up_far.append(place.shift_z(up_far[-1], 1))
    near = [qkv_own, place.shift_z(qkv_own, 1)]
    near += [place.shift_z(after(qkv_own, up_near[1]), k) for k in range(2, nz)]

    def two_kernel(one_ref, two_ref, out_ref):
        out_ref[:block, :] = one_ref[...]
        out_ref[block:, :] = two_ref[...]

    far_one = place.swap_y(near[1])
    far_two = place.swap_y(in_vmem(two_kernel, [((2 * block, width), bf16)], *near[2:]))
    qkv_pieces = (*near, qkv_own_far, far_one, far_two)

    whole_far = place.swap_x(whole_near)

    near_cells = jnp.concatenate(after(own_cells, near[1]), axis=0)
    near_cells = jnp.concatenate(
        [near_cells, after(
                place.swap_x(near_cells), up_far[0], *near[1:], up_near[1], whole_far,
                up_far[1], far_one,
            )], axis=0
    )
    far_cells = place.swap_core(near_cells)
    beside = jnp.concatenate([near_cells[:, 2 * genes :], far_cells[:, 2 * genes :]], axis=0).astype(f32)
    beside = beside[:, :3] * SPLIT + beside[:, 3:6]
    segment = beside[:, 2:3]
    segment_row = segment.reshape(1, rows)
    embed = sinusoids_of_whole((beside[:, 0:1], beside[:, 1:2]), width)


    def enc_half_kernel(near_ref, far_ref, out_ref, vectors_ref):
        _, _, _, x = coordinates()
        for dx, ref in enumerate((near_ref, far_ref)):
            for k in range(nz):
                at = k * tall
                put(out_ref, (2 * k + (x ^ dx)) * half, 0, ref[at : at + half, :])
                part = ref[at + half + quarter : at + tall, :block]
                put(vectors_ref, 0, (2 * k + (x ^ dx)) * block, part)

    enc_half, vectors = in_vmem(
        enc_half_kernel, [((genes // 2, width), bf16), ((16, width), f32)], whole_near, whole_far
    )
    enc_far = place.swap_core(enc_half)

    b_dec_row = vectors[0:1]

    def both_cores(near_ref, far_ref, out_ref):
        _, core, _, _ = coordinates()
        for dc, ref in enumerate((near_ref, far_ref)):
            for k in range(2 * nz):
                put(out_ref, k * block + (core ^ dc) * half, 0, ref[k * half : (k + 1) * half, :])

    def by_y(out_mine, out_send, value, first):
        y, _, _, _ = coordinates()
        for k in range(nz):
            low = value[:, 2 * k * block : (2 * k + 1) * block]
            high = value[:, (2 * k + 1) * block : (2 * k + 2) * block]
            at = slice(first, first + value.shape[0]), slice(k * block, (k + 1) * block)
            out_mine[at] = jnp.where(y == 0, low, high)
            out_send[at] = jnp.where(y == 0, high, low)

    def first_kernel(
        near_ref, far_ref, enc_near_ref, enc_far_ref, embed_ref, vectors_ref,
        enc_ref, hidden_ref, normed_ref, mine_ref, send_ref,
    ):
        both_cores(enc_near_ref, enc_far_ref, enc_ref)
        for number, ref in enumerate((near_ref, far_ref)):
            first = number * half_rows
            hidden = dot(ref[:, :genes], enc_ref[...]) + embed_ref[first : first + half_rows, :]
            if number == 0:
                hidden_ref[...] = hidden
            normal, _ = normalise(hidden)
            normed = (normal * vectors_ref[1:2, :] + vectors_ref[2:3, :]).astype(bf16)
            normed_ref[first : first + half_rows, :] = normed
            by_y(mine_ref, send_ref, normed, first)

    square_bf16, half_bf16 = ((width, width), bf16), ((half_rows, width), bf16)
    half_f32 = ((half_rows, width), f32)
    columns_bf16 = ((rows, width // 2), bf16)
    w_enc, hidden0, normed1, normed1_mine, normed1_send = in_vmem(
        first_kernel, [square_bf16, half_f32, ((rows, width), bf16), columns_bf16, columns_bf16],
        near_cells, far_cells, enc_half, enc_far, embed, vectors, flops=4 * square,
    )

    def attend_kernel(normed_ref, *refs):
        pieces, refs = refs[: nz + 3], refs[nz + 3 :]
        column_ref, row_ref, w_ref, w_out_ref, qkv_ref, out_ref, own_ref, send_ref = refs
        y, _, z, x = coordinates()
        parts = [(0, k, pieces[k], 0) for k in range(nz)]
        parts += [(1, k, pieces[nz + min(k, 2)], max(k - 2, 0) * block) for k in range(nz)]
        for dy, k, ref, first in parts:
            there = (z - k) % nz
            for dx in range(2):
                row = (2 * there + (x ^ dx)) * block + (y ^ dy) * half
                put(w_ref, row, 0, ref[first + dx * half : first + (dx + 1) * half, :three])
            for j in range(4):
                row = there * half + (y ^ dy) * quarter
                part = ref[first + j * quarter : first + (j + 1) * quarter, three:]
                put(w_out_ref, row, j * slice_width, part)
        qkv_ref[...] = dot(normed_ref[...], w_ref[...]).astype(bf16)
        allowed = column_ref[...] == row_ref[...]
        for number in range(heads):
            queries, keys, values = (one_head(qkv_ref, i, heads, number, head) for i in range(3))
            probs = soft(queries, keys, allowed, head**-0.5)
            at = slice(number * head, (number + 1) * head)
            out_ref[:, at] = dot(probs.astype(bf16), values).astype(bf16)
        own_ref[...] = dot(out_ref[:half_rows, :], w_out_ref[...])
        send_ref[...] = dot(out_ref[half_rows:, :], w_out_ref[...]).astype(bf16)

    w_qkv, w_out, qkv, context, own, send = in_vmem(
        attend_kernel,
        [((width, three), bf16), ((slice_width, width), bf16), ((rows, three), bf16),
         ((rows, slice_width), bf16), half_f32, half_bf16],
        after(normed1, up_near[2]), *qkv_pieces, segment, segment_row,
        flops=4 * square + 4 * pairs * head, exps=pairs,
    )

    def add_kernel(own_ref, other_ref, out_ref):
        out_ref[...] = (own_ref[...].astype(f32) + other_ref[...].astype(f32)).astype(out_ref.dtype)

    def add(own, other, dtype=bf16):
        return in_vmem(add_kernel, [(own.shape, dtype)], own, other)

    def sum_x(mine_ref, other_ref):
        other = jnp.concatenate([other_ref[own_rows:, :], other_ref[:own_rows, :]], axis=0)
        return mine_ref[...].astype(f32) + other.astype(f32)

    mine = add(own, after(place.swap_core(send), up_near[3], up_far[2]))

    def second_kernel(hidden_ref, mine_ref, other_ref, vectors_ref, out_ref, normed_ref):
        hidden = hidden_ref[...] + sum_x(mine_ref, other_ref)
        out_ref[...] = hidden
        normal, _ = normalise(hidden)
        normed_ref[...] = (normal * vectors_ref[3:4, :] + vectors_ref[4:5, :]).astype(bf16)

    hidden1, normed2 = in_vmem(
        second_kernel, [half_f32, half_bf16],
        hidden0, mine, after(place.swap_x(mine), up_far[3]), vectors,
    )
    normed2_far = place.swap_core(normed2)

    def dec_rows_kernel(near_ref, far_ref, out_ref):
        for dx, ref in enumerate((near_ref, far_ref)):
            for k in range(nz):
                at, out = k * tall + half, (dx * nz + k) * quarter
                out_ref[out : out + quarter, :] = ref[at : at + quarter, :]

    dec_near = in_vmem(
        dec_rows_kernel, [((2 * nz * quarter, genes), bf16)], whole_near, after(whole_far, qkv)
    )

    def dec_half_kernel(near_ref, far_ref, out_ref):
        y, _, _, x = coordinates()
        for dy, ref in enumerate((near_ref, far_ref)):
            for dx in range(2):
                for k in range(nz):
                    at = (dx * nz + k) * quarter
                    row = (2 * k + (x ^ dx)) * half + (y ^ dy) * quarter
                    put(out_ref, row, 0, ref[at : at + quarter, :])

    dec_half = in_vmem(
        dec_half_kernel, [((width // 2, genes), bf16)],
        dec_near, after(place.swap_y(dec_near), mine),
    )
    dec_far = place.swap_core(dec_half)

    def decoder_kernel(near_ref, far_ref, dec_near_ref, dec_far_ref, dec_ref, grad_ref, low_ref, sums_ref):
        both_cores(dec_near_ref, dec_far_ref, dec_ref)
        grad = times_t(near_ref[:, genes : 2 * genes], dec_ref[...])
        grad_ref[...] = grad
        low_ref[:half_rows, :] = grad.astype(bf16)
        low_ref[half_rows:, :] = times_t(far_ref[:, genes : 2 * genes], dec_ref[...]).astype(bf16)
        sums_ref[...] = sum(
            jnp.sum(ref[:, genes : 2 * genes].astype(f32), axis=0, keepdims=True)
            for ref in (near_ref, far_ref)
        )

    w_dec, grad_h2, grad_down, bias_sums = in_vmem(
        decoder_kernel,
        [square_bf16, half_f32, ((rows, width), bf16), ((1, width), f32)],
        near_cells, far_cells, dec_half, dec_far, flops=4 * square,
    )

    def feed_kernel(normed_ref, normed_far_ref, grad_ref, *refs):
        pieces, refs = refs[: 2 * nz], refs[2 * nz :]
        active_ref, grad_up_ref, own_ref, send_ref, own2_ref, send2_ref, mine_ref, theirs_ref = refs[:8]
        w_up_ref, w_down_ref, normed_all, back, ahead = refs[8:]
        y, _, z, x = coordinates()
        for dy in range(2):
            for k in range(nz):
                ref = pieces[dy * nz + k]
                there = (z - k) % nz
                for dx in range(2):
                    for number in range(nz):
                        at = dx * up_half + number * lanes
                        column = (2 * number + (y ^ dy)) * lanes
                        put(w_up_ref, (2 * there + (x ^ dx)) * block, column, ref[:block, at : at + lanes])
                put(w_down_ref, (2 * there + (y ^ dy)) * many, 0, ref[block:, :])
        normed_all[:half_rows, :] = normed_ref[...]
        normed_all[half_rows:, :] = normed_far_ref[...]
        by_y(mine_ref, theirs_ref, normed_ref[...], 0)
        by_y(mine_ref, theirs_ref, normed_far_ref[...], half_rows)
        chunk = 2 * lanes
        for number in range(nz):
            at = slice(number * chunk, (number + 1) * chunk)
            active, slope = gelu_parts(dot(normed_all[...], w_up_ref[:, at]))
            active = active.astype(bf16)
            active_ref[:, at] = active
            grad_up = (times_t(grad_ref[...], w_down_ref[at, :]) * slope).astype(bf16)
            grad_up_ref[:, at] = grad_up
            part, part2 = times_t(grad_up, w_up_ref[:, at]), dot(active, w_down_ref[at, :])
            back[...] = part if number == 0 else back[...] + part
            ahead[...] = part2 if number == 0 else ahead[...] + part2
        for sums, one, two in ((back, own_ref, send_ref), (ahead, own2_ref, send2_ref)):
            one[...] = sums[:half_rows, :]
            two[...] = sums[half_rows:, :].astype(bf16)

    full_bf16, full_f32 = ((rows, width), bf16), ((rows, width), f32)
    active, grad_up, own, send, own2, send2, normed2_mine, normed2_send = in_vmem(
        feed_kernel,
        [full_bf16, full_bf16, half_f32, half_bf16, half_f32, half_bf16, columns_bf16, columns_bf16],
        normed2, normed2_far, grad_down, *up_near, *up_far,
        flops=16 * square, exps=rows * ff_slice,
        scratch=[square_bf16, square_bf16, full_bf16, full_f32, full_f32],
    )
    mine = add(own, place.swap_core(send))

    def down_halve_kernel(value_ref, *refs):
        _, _, z, _ = coordinates()
        for number in range(2):
            for ref, low in ((refs[2 * number], z % 2), (refs[2 * number + 1], 1 - z % 2)):
                for high in range(2):
                    part = rows_at(value_ref, ((2 * high + low) * 2 + number) * many, many)
                    ref[high * many : (high + 1) * many, :] = part

    def sum_halve_kernel(*refs):
        parts, (out_ref, send_ref, all_ref) = refs[:-3], refs[-3:]
        at = 0
        for ref in parts[1:]:
            rows_here = slice(at, at + ref.shape[0])
            all_ref[rows_here, :] = parts[0][rows_here, :].astype(f32) + ref[...].astype(f32)
            at += ref.shape[0]
        _, _, z, _ = coordinates()
        count = out_ref.shape[0] // 2
        for high in range(2):
            at = slice(high * count, (high + 1) * count)
            out_ref[at, :] = rows_at(all_ref, (2 * high + z % 2) * count, count).astype(bf16)
            send_ref[at, :] = rows_at(all_ref, (2 * high + 1 - z % 2) * count, count).astype(bf16)

    def sum_halve(own, *others):
        shape = ((own.shape[0] // 2, own.shape[1]), bf16)
        return in_vmem(
            sum_halve_kernel, [shape, shape], own, *others, scratch=[(own.shape, f32)]
        )

    def add_split_kernel(own_ref, other_ref, out_ref, send_ref):
        _, _, z, _ = coordinates()
        count = out_ref.shape[0]
        for ref, part in ((out_ref, z // 2), (send_ref, 1 - z // 2)):
            own, other = (rows_at(r, part * count, count).astype(f32) for r in (own_ref, other_ref))
            ref[...] = (own + other).astype(bf16)

    def add_halve(own, other):
        shape = ((own.shape[0] // 2, own.shape[1]), bf16)
        return in_vmem(add_split_kernel, [shape, shape], own, other)

    down_one = in_vmem(
        down_halve_kernel, [((2 * many, width), bf16)] * 4, inner(active, grad_down).astype(bf16)
    )
    down_one = [down_one[:2], down_one[2:]]
    down_other = place.swap_z(down_one[0][1], 1)
    up_mine = inner(after(normed2_mine, mine), grad_up).astype(bf16)
    up_send = inner(after(normed2_send, mine), grad_up).astype(bf16)
    low_rows = nz * block // 2
    up_other_low = place.swap_y(up_send[:low_rows])
    ahead = add(own2, after(place.swap_core(send2), mine))
    other = after(place.swap_x(mine), up_mine, up_send, ahead, up_other_low, down_other)
    up_other_high = place.swap_y(after(up_send[low_rows:], other))
    down_two = [add_halve(down_one[0][0], after(down_other, other))]
    down_two_other = place.swap_z(down_two[0][1], 2)
    down_other = place.swap_z(after(down_one[1][1], other), 1)

    def back_kernel(hidden_ref, mine_ref, other_ref, grad_ref, vectors_ref, out_ref, low_ref, row):
        inside, gain_sums, shift_sums = normalise_back(
            hidden_ref[...], sum_x(mine_ref, other_ref), vectors_ref[row : row + 1, :]
        )
        grad = grad_ref[...] + inside
        if out_ref is not None:
            out_ref[...] = grad
        low_ref[:half_rows, :] = grad.astype(bf16)
        low_ref[half_rows:, :] = jnp.zeros((16, width), bf16)
        low_ref[half_rows : half_rows + 1, :] = gain_sums.astype(bf16)
        low_ref[half_rows + 1 : half_rows + 2, :] = shift_sums.astype(bf16)

    def second_back_kernel(*refs):
        back_kernel(*refs, 3)

    def first_back_kernel(*refs):
        back_kernel(*refs[:5], None, refs[5], 1)

    message = ((half_rows + 16, width), bf16)
    grad_h1, near_two = in_vmem(
        second_back_kernel, [half_f32, message], hidden1, mine, other, grad_h2, vectors
    )
    far_two = place.swap_core(near_two)
    ahead_other = place.swap_x(after(ahead, other))

    def attend_back_kernel(
        near_ref, far_ref, w_out_ref, qkv_ref, column_ref, row_ref, w_ref,
        out_ref, own_ref, send_ref, all_ref, grad_ref,
    ):
        all_ref[:half_rows, :] = near_ref[:half_rows, :]
        all_ref[half_rows:, :] = far_ref[:half_rows, :]
        grad_ref[...] = times_t(all_ref[...], w_out_ref[...]).astype(bf16)
        allowed = column_ref[...] == row_ref[...]
        scaling = head**-0.5
        for number in range(heads):
            queries, keys, values = (one_head(qkv_ref, i, heads, number, head) for i in range(3))
            grad = one_head(grad_ref, 0, heads, number, head)
            probs = soft(queries, keys, allowed, scaling)
            weighted = probs * times_t(grad, values)
            delta = jnp.sum(weighted, axis=-1, keepdims=True)
            dscore = (weighted - probs * delta).astype(bf16)
            parts = (
                dot(dscore, keys) * scaling,
                inner(dscore, queries) * scaling,
                inner(probs.astype(bf16), grad),
            )
            for i, part in enumerate(parts):
                at = (i * heads + number) * head
                out_ref[:, at : at + head] = part.astype(bf16)
        own_ref[...] = times_t(out_ref[:half_rows, :], w_ref[...])
        send_ref[...] = times_t(out_ref[half_rows:, :], w_ref[...]).astype(bf16)

    grad_qkv, own, send, grad_attn = in_vmem(
        attend_back_kernel, [((rows, three), bf16), half_f32, half_bf16, full_bf16],
        near_two, far_two, w_out, qkv, segment, segment_row, w_qkv,
        flops=4 * square + 10 * pairs * head, exps=pairs,
        scratch=[((rows, slice_width), bf16)],
    )
    qkv_send = inner(normed1_send, grad_qkv).astype(bf16)
    qkv_other = place.swap_y(qkv_send)
    up_other_high, down_other, down_two_other, ahead_other = after(
        (up_other_high, down_other, down_two_other, ahead_other), grad_qkv
    )
    mine = add(
        own, after(place.swap_core(send), qkv_send, up_other_high, down_other, down_two_other, ahead_other)
    )
    up_one = sum_halve(up_mine, up_other_low, after(up_other_high, mine))
    down_two.append(add_halve(down_one[1][0], after(down_other, mine)))
    down_sum = [add(down_two[0][0], after(down_two_other, mine))]
    other = place.swap_x(mine)
    down_two_other = place.swap_z(down_two[1][1], 2)
    up_one_other = place.swap_z(up_one[1], 1)

    qkv_mine = inner(normed1_mine, grad_qkv).astype(bf16)
    grad_w_out = inner(context, grad_attn).astype(bf16)

    other = after(other, qkv_mine, down_two_other)
    qkv_one = sum_halve(qkv_mine, qkv_other)
    qkv_one_other = place.swap_z(qkv_one[1], 1)
    up_two = add_halve(up_one[0], after(up_one_other, other))
    up_two_other = place.swap_z(up_two[1], 2)
    near_one = in_vmem(first_back_kernel, [message], hidden0, mine, other, grad_h1, vectors)
    far_one = place.swap_core(near_one)

    def hidden_kernel(hidden_ref, mine_ref, other_ref, low_ref, own_ref, send_ref):
        _, core, _, x = coordinates()
        hidden = (hidden_ref[...] + sum_x(mine_ref, other_ref)).astype(bf16)
        low_ref[...] = hidden[:own_rows, :]
        for k in range(nz):
            group = hidden[:, 2 * k * block : (2 * k + 2) * block]
            at = slice(k * half, (k + 1) * half)
            own_ref[:, at] = own_part(group, core, x, half)
            send_ref[:, at] = own_part(group, 1 - core, x, half)

    part_bf16 = ((half_rows, slice_width), bf16)
    hidden2, hidden2_own, hidden2_send = in_vmem(
        hidden_kernel, [((own_rows, width), bf16), part_bf16, part_bf16],
        hidden1, ahead, after(ahead_other, near_one),
    )
    hidden2_far = place.swap_core(hidden2_send)

    def few_rows_kernel(own_ref, far_ref, near_cells_ref, far_cells_ref, out_grad_ref, mine_ref, send_ref):
        y, _, _, _ = coordinates()
        columns = slice(genes, 2 * genes)
        grad = inner(own_ref[...], near_cells_ref[:, columns])
        grad = (grad + inner(far_ref[...], far_cells_ref[:, columns])).astype(bf16)
        mine_ref[...] = jnp.where(y == 0, out_grad_ref[...], grad)
        send_ref[...] = jnp.where(y == 0, grad, out_grad_ref[...])

    few_shape = ((slice_width, genes), bf16)
    few_mine, few_send = in_vmem(
        few_rows_kernel, [few_shape, few_shape],
        hidden2_own, hidden2_far, near_cells, far_cells, grad_w_out, flops=square,
    )
    few_other = place.swap_y(few_send)
    logits = (dot(hidden2, w_dec) + b_dec_row).astype(bf16)
    one, two = logits[:cells], logits[cells:]

    input_grad = times_t(near_one[:own_rows], w_enc).astype(bf16)

    tall_last = 2 * half + 16

    def last_kernel(
        near_ref, far_ref, one_ref, one_far_ref, two_ref, two_far_ref, bias_ref, few_ref, few_other_ref, *refs
    ):
        own_ref, send_ref, slice_ref, grad_ref, sums_ref = refs
        _, core, z, x = coordinates()
        for number, ref in enumerate((near_ref, far_ref)):
            for k in range(nz):
                group = ref[:, 2 * k * block : (2 * k + 2) * block]
                slice_ref[
                    number * half_rows : (number + 1) * half_rows, k * half : (k + 1) * half
                ] = own_part(group, core, x, half)
        grad_ref[...] = inner(slice_ref[:half_rows, :], one_ref[:half_rows, :]) + inner(
            slice_ref[half_rows:, :], one_far_ref[:half_rows, :]
        )
        sums_ref[...] = jnp.zeros((8, width), f32)
        sums_ref[0:1, :] = bias_ref[...]
        at = slice(half_rows, half_rows + 2)
        sums_ref[1:3, :] = one_ref[at, :].astype(f32) + one_far_ref[at, :].astype(f32)
        sums_ref[3:5, :] = two_ref[at, :].astype(f32) + two_far_ref[at, :].astype(f32)
        for ref, low in ((own_ref, z % 2), (send_ref, 1 - z % 2)):
            ref[...] = jnp.zeros(ref.shape, bf16)
            for high in range(2):
                there, first = 2 * high + low, high * tall_last
                ref[first : first + half, :] = rows_at(grad_ref, there * half, half).astype(bf16)
                column = pl.multiple_of((2 * there + x) * block, block)
                part = sums_ref[:, pl.ds(column, block)].astype(bf16)
                ref[first + half : first + half + 8, :block] = part
                few = [rows_at(r, there * half, half).astype(f32) for r in (few_ref, few_other_ref)]
                ref[first + half + 16 : first + tall_last, :] = (few[0] + few[1]).astype(bf16)

    last_one = in_vmem(
        last_kernel, [((2 * tall_last, width), bf16)] * 2,
        near_cells, far_cells, near_one, after(far_one, qkv_one_other, up_two_other),
        near_two, far_two, bias_sums, few_mine, few_other, flops=square,
        scratch=[((rows, slice_width), bf16), ((slice_width, width), f32), ((8, width), f32)],
    )
    last_one_other = place.swap_z(last_one[1], 1)
    qkv_two = add_halve(qkv_one[0], after(qkv_one_other, last_one[1]))
    qkv_two_other = place.swap_z(qkv_two[1], 2)

    def feed_sum_kernel(down_ref, one_ref, one_other_ref, two_ref, two_other_ref, out_ref):
        out_ref[:many, :] = down_ref[...]
        for row, ref, other_ref in ((many, one_ref, one_other_ref), (2 * many, two_ref, two_other_ref)):
            total = ref[...].astype(f32) + other_ref[...].astype(f32)
            out_ref[row : row + ref.shape[0], :] = total.astype(bf16)

    feed_sum = in_vmem(
        feed_sum_kernel, [((2 * many + block, width), bf16)],
        down_sum[0], down_two[1][0], down_two_other, up_two[0], after(up_two_other, last_one[1]),
    )
    feed_other = place.swap_y(feed_sum)

    def by_x_kernel(own_ref, other_ref, mine_ref, send_ref):
        y, _, _, x = coordinates()
        at = slice(0, mine_ref.shape[0]), slice(0, mine_ref.shape[1])
        mine_ref[...] = jnp.where(y == x, own_ref[at], other_ref[at])
        send_ref[...] = jnp.where(y == x, other_ref[at], own_ref[at])

    def by_x(own, other, width):
        return in_vmem(by_x_kernel, [((block, width), bf16)] * 2, own, other)

    last_two = add_halve(last_one[0], after(last_one_other, feed_other, qkv_two_other))
    last_two_other = place.swap_z(last_two[1], 2)
    qkv_sum = add(
        qkv_two[0], after(qkv_two_other, last_two[1])
    )

    def feed_split_kernel(own_ref, other_ref, down_ref, mine_ref, send_ref):
        y, _, _, x = coordinates()
        total = own_ref[: 2 * many, :].astype(f32) + other_ref[: 2 * many, :].astype(f32)
        down_ref[...] = total.astype(bf16)
        own, other = own_ref[2 * many :, :], other_ref[2 * many :, :]
        mine_ref[...] = jnp.where(y == x, own, other)
        send_ref[...] = jnp.where(y == x, other, own)

    block_bf16 = ((block, width), bf16)
    down_sum, up_mine, up_send = in_vmem(
        feed_split_kernel, [((2 * many, width), bf16), block_bf16, block_bf16],
        feed_sum, after(feed_other, last_two[1]),
    )
    qkv_other = place.swap_y(qkv_sum)
    up_there = place.swap_x(up_send)
    down_far = place.swap_core(down_sum)
    def halves_kernel(near_ref, far_ref, out_ref):
        _, core, _, _ = coordinates()
        count = near_ref.shape[0]
        for dc, ref in enumerate((near_ref, far_ref)):
            put(out_ref, (core ^ dc) * count, 0, ref[...])

    def halves(near, far):
        return in_vmem(
            halves_kernel, [((2 * near.shape[0], near.shape[1]), f32)], near, far
        )


    def up_out_kernel(near_ref, far_ref, out_ref):
        _, core, _, x = coordinates()
        for dc, ref in enumerate((near_ref, far_ref)):
            for dx in range(2):
                for k in range(nz):
                    part = ref[dx * block : (dx + 1) * block, 2 * k * lanes : 2 * (k + 1) * lanes]
                    put(out_ref, 0, ((2 * k + (x ^ dx)) * 2 + (core ^ dc)) * 2 * lanes, part)

    qkv_other, last_two_other, one, two, up_there, down_far = lax.optimization_barrier(
        (qkv_other, last_two_other, one, two, up_there, down_far)
    )
    up_both = jnp.concatenate([up_mine, up_there], axis=0)
    out_down = halves(down_sum, down_far)
    out_up = in_vmem(
        up_out_kernel, [((block, ff), f32)], up_both, place.swap_core(up_both)
    )
    last = add(last_two[0], last_two_other)
    last_other = place.swap_y(last)

    def last_add_kernel(one_ref, other_ref, out_ref, sums_ref):
        y, _, _, _ = coordinates()
        total = one_ref[: half + 16, :].astype(f32) + other_ref[: half + 16, :].astype(f32)
        out_ref[:half, :] = total[:half, :].astype(bf16)
        sums_ref[...] = total[half : half + 8, :block]
        own, other = one_ref[half + 16 :, :], other_ref[half + 16 :, :]
        out_ref[half : 2 * half, :] = jnp.where(y == 0, own, other)
        out_ref[2 * half :, :] = jnp.where(y == 0, other, own)

    last, sums = in_vmem(
        last_add_kernel, [((3 * half, width), bf16), ((8, block), f32)], last, last_other
    )

    def last_out_kernel(near_ref, far_ref, *out_refs):
        _, core, _, _ = coordinates()
        for dc, ref in enumerate((near_ref, far_ref)):
            for part, out_ref in enumerate(out_refs):
                put(out_ref, (core ^ dc) * half, 0, ref[part * half : (part + 1) * half, :])

    out_enc, out_out, out_dec = in_vmem(
        last_out_kernel, [((block, width), f32)] * 3, last, place.swap_core(last)
    )

    qkv_mine, qkv_send = by_x(qkv_sum, qkv_other, three)
    qkv_there = place.swap_x(qkv_send)
    qkv_both = jnp.concatenate([qkv_mine, qkv_there], axis=0)
    pair = place.regroup(
        *(
            jnp.concatenate(
                [part, after(input_grad[i * cells : (i + 1) * cells], qkv_other)], axis=1
            )
            for i, part in enumerate((one, two))
        )
    )
    pair = jnp.stack(place.by_parity(pair))
    logits, input_grad = pair[:, :, :genes], pair[:, :, genes:]

    def qkv_out_kernel(near_ref, far_ref, out_ref):
        _, core, _, x = coordinates()
        for dx in range(2):
            for number in range(3 * nz):
                at = slice(dx * block, (dx + 1) * block), slice(number * head, (number + 1) * head)
                near_part, far_part = near_ref[at].astype(f32), far_ref[at].astype(f32)
                low = jnp.where(core == 0, near_part, far_part)
                high = jnp.where(core == 0, far_part, near_part)
                put(
                    out_ref, 0, number * 4 * head + (x ^ dx) * 2 * head,
                    jnp.concatenate([low, high], axis=1),
                )

    out_qkv = in_vmem(
        qkv_out_kernel, [((block, 3 * width), f32)], qkv_both, place.swap_core(qkv_both)
    )
    return (
        logits, input_grad, out_enc, out_qkv, out_out, out_up, out_down, out_dec,
        sums[0], sums[1], sums[2], sums[3], sums[4],
    )


IN_SPECS = (
    ("dp", "blk", None), (None, "dp", "blk"), ("dp", "blk"), ("dp", "blk", None),
    *[("blk", None)] * 6, *[("blk",)] * 5,
)
OUT_SPECS = (("dp", "blk", None), ("dp", "blk", None), *[("blk", None)] * 6, *[("blk",)] * 5)


def solution(mesh):
    groups, blocks = mesh.shape["dp"], mesh.shape["blk"]

    def run(*args):
        seqs = args[0].shape[0] // groups
        if groups == 4 and blocks == 4 * seqs and seqs == 2 and HEADS == 4 * (blocks // 2):
            sizes = (groups // 2, 2, blocks // 2, 2)
            fine = Mesh(mesh.devices.reshape(sizes), AXES)
            names = {"dp": ("y", "core"), "blk": ("z", "x"), None: None}
            plan = functools.partial(grouped_plan, sizes)
        else:
            fine, names, plan = mesh, {"dp": "dp", "blk": "blk", None: None}, spread_plan
        specs = lambda entries: tuple(P(*[names[axis] for axis in entry]) for entry in entries)
        return jax.shard_map(
            plan, mesh=fine, in_specs=specs(IN_SPECS), out_specs=specs(OUT_SPECS), check_vma=False
        )(*args)

    return run
```

```python
import functools
import math

import jax
import jax.numpy as jnp
from jax import lax
from jax.experimental import pallas as pl
from jax.experimental.pallas import tpu as pltpu
from jax.sharding import Mesh
from jax.sharding import PartitionSpec as P

HEADS = 16


NEGATIVE = -1e30
EPSILON = 1e-05


def layer_norm(inputs, gain_vec, shift_vec):
    centre = inputs - jnp.mean(inputs, axis=-1, keepdims=True)
    spread = jnp.mean(centre * centre, axis=-1, keepdims=True)
    return centre * lax.rsqrt(spread + EPSILON) * gain_vec + shift_vec


def sinusoids(coords, width):
    quarter = width // 4
    frequency = jnp.exp(jnp.arange(quarter, dtype=jnp.float32) * (-math.log(10000.0) / quarter))
    first_angle = coords[0].astype(jnp.float32)[..., None] * frequency
    second_angle = coords[1].astype(jnp.float32)[..., None] * frequency
    return jnp.concatenate(
        [jnp.sin(first_angle), jnp.cos(first_angle), jnp.sin(second_angle), jnp.cos(second_angle)],
        axis=-1,
    )


def inner(left, right):
    return lax.dot_general(
        left, right, (((0,), (0,)), ((), ())), preferred_element_type=jnp.float32
    )


def times_t(left, right):
    return lax.dot_general(
        left, right, (((1,), (1,)), ((), ())), preferred_element_type=jnp.float32
    )


def spread_plan(
    counts,
    coords,
    segment_ids,
    logit_grad,
    enc_weight,
    qkv_weight,
    out_weight,
    up_weight,
    down_weight,
    dec_weight,
    dec_bias,
    norm1_gain,
    norm1_shift,
    norm2_gain,
    norm2_shift,
):
    gathered = (
        lax.all_gather(enc_weight, "blk", axis=0, tiled=True),
        lax.all_gather(qkv_weight, "blk", axis=0, tiled=True),
        lax.all_gather(out_weight, "blk", axis=0, tiled=True),
        lax.all_gather(up_weight, "blk", axis=0, tiled=True),
        lax.all_gather(down_weight, "blk", axis=0, tiled=True),
        lax.all_gather(dec_weight, "blk", axis=0, tiled=True),
        lax.all_gather(dec_bias, "blk", axis=0, tiled=True),
        lax.all_gather(norm1_gain, "blk", axis=0, tiled=True),
        lax.all_gather(norm1_shift, "blk", axis=0, tiled=True),
        lax.all_gather(norm2_gain, "blk", axis=0, tiled=True),
        lax.all_gather(norm2_shift, "blk", axis=0, tiled=True),
    )
    w_enc, w_qkv, w_out, w_up, w_down, w_dec, b_dec, gain_one, shift_one, gain_two, shift_two = (
        gathered
    )
    seg_all = lax.all_gather(segment_ids, "blk", axis=1, tiled=True)
    seq_count, cell_count, gene_count = counts.shape
    width = w_enc.shape[1]
    head_count = HEADS
    head_size = width // head_count
    scaling = head_size ** (-0.5)
    row_count = seq_count * cell_count
    express = (
        jnp.log1p(counts.astype(jnp.float32)).astype(jnp.bfloat16).reshape(row_count, gene_count)
    )
    embed = sinusoids(coords, width).reshape(row_count, width)
    hidden0 = jnp.dot(express, w_enc, preferred_element_type=jnp.float32) + embed
    gain_one32 = gain_one.astype(jnp.float32)
    shift_one32 = shift_one.astype(jnp.float32)
    gain_two32 = gain_two.astype(jnp.float32)
    shift_two32 = shift_two.astype(jnp.float32)
    normed1 = layer_norm(hidden0, gain_one32, shift_one32).astype(jnp.bfloat16)
    qkv = jnp.dot(normed1, w_qkv, preferred_element_type=jnp.float32).astype(jnp.bfloat16)
    queries = qkv[:, :width].reshape(seq_count, cell_count, head_count, head_size)
    key_rows = qkv[:, width : 2 * width].reshape(seq_count, cell_count, head_count, head_size)
    values = qkv[:, 2 * width :].reshape(seq_count, cell_count, head_count, head_size)

    def masked_scores(query_part, key_part, seg_query, seg_key):
        scores = (
            jnp.einsum("sqhe,skhe->shqk", query_part, key_part, preferred_element_type=jnp.float32)
            * scaling
        )
        return jnp.where(seg_query[:, None, :, None] == seg_key[:, None, None, :], scores, NEGATIVE)

    start_max = jnp.full((seq_count, head_count, cell_count), NEGATIVE, jnp.float32)
    piece = (
        lax.all_gather(key_rows, "blk", axis=1, tiled=True),
        lax.all_gather(values, "blk", axis=1, tiled=True),
    )
    seg_part = seg_all
    incoming = (piece[0], piece[1], seg_part)
    running_max = start_max
    key_part, value_part, context_seg_part = incoming
    query_part = queries
    scores = masked_scores(query_part, key_part, segment_ids, context_seg_part)
    newest = jnp.maximum(running_max, jnp.max(scores, axis=-1))
    expo = jnp.exp(scores - newest[..., None])
    running_sum = jnp.sum(expo, axis=-1)
    update = jnp.einsum(
        "shqk,skhe->sqhe", expo.astype(jnp.bfloat16), value_part, preferred_element_type=jnp.float32
    )
    weighted = update
    running_max, running_sum, weighted = (newest, running_sum, weighted)
    context32 = weighted / jnp.transpose(running_sum, (0, 2, 1))[..., None]
    logsum = jnp.transpose(running_max + jnp.log(running_sum), (0, 2, 1))
    context = context32.astype(jnp.bfloat16).reshape(row_count, width)
    hidden1 = hidden0 + jnp.dot(context, w_out, preferred_element_type=jnp.float32)
    normed2 = layer_norm(hidden1, gain_two32, shift_two32).astype(jnp.bfloat16)
    up_value = jnp.dot(normed2, w_up, preferred_element_type=jnp.float32)
    active = jax.nn.gelu(up_value).astype(jnp.bfloat16)
    hidden2 = hidden1 + jnp.dot(active, w_down, preferred_element_type=jnp.float32)
    hidden2_low = hidden2.astype(jnp.bfloat16)
    logits = (
        jnp.dot(hidden2_low, w_dec, preferred_element_type=jnp.float32) + b_dec.astype(jnp.float32)
    ).astype(jnp.bfloat16)
    cotangent = logit_grad.reshape(row_count, gene_count)
    grad_dec = inner(hidden2_low, cotangent)
    grad_bias = jnp.sum(cotangent.astype(jnp.float32), axis=0)
    grad_h2 = times_t(cotangent, w_dec)
    grad_down = grad_h2.astype(jnp.bfloat16)
    grad_w_down = inner(active, grad_down)
    grad_active = times_t(grad_down, w_down)
    gelu_pull = jax.vjp(jax.nn.gelu, up_value)[1]
    grad_up = gelu_pull(grad_active)[0].astype(jnp.bfloat16)
    grad_w_up = inner(normed2, grad_up)
    grad_normed2 = times_t(grad_up, w_up)
    norm_pull_two = jax.vjp(layer_norm, hidden1, gain_two32, shift_two32)[1]
    part_two, grad_gain_two, grad_shift_two = norm_pull_two(grad_normed2)
    grad_h1 = grad_h2 + part_two
    grad_attn = grad_h1.astype(jnp.bfloat16)
    grad_w_out = inner(context, grad_attn)
    grad_context = (
        times_t(grad_attn, w_out)
        .astype(jnp.bfloat16)
        .reshape(seq_count, cell_count, head_count, head_size)
    )
    delta = jnp.sum(grad_context.astype(jnp.float32) * context32, axis=-1)
    logsum_all, delta_all = (
        lax.all_gather(logsum, "blk", axis=1, tiled=True),
        lax.all_gather(delta, "blk", axis=1, tiled=True),
    )
    seg_part = seg_all
    query_seg_part = seg_part
    query_part = queries
    gradout_part = grad_context
    logsum_part = logsum
    delta_part = delta
    scores = masked_scores(query_part, key_part, segment_ids, query_seg_part)
    probs = jnp.exp(scores - jnp.transpose(logsum_part, (0, 2, 1))[..., None])
    dprob = jnp.einsum(
        "sqhe,skhe->shqk", gradout_part, value_part, preferred_element_type=jnp.float32
    )
    dscore = (probs * (dprob - jnp.transpose(delta_part, (0, 2, 1))[..., None])).astype(
        jnp.bfloat16
    )
    grad_queries = (
        jnp.einsum("shqk,skhe->sqhe", dscore, key_part, preferred_element_type=jnp.float32)
        * scaling
    )
    piece = (
        lax.all_gather(queries, "blk", axis=1, tiled=True),
        lax.all_gather(grad_context, "blk", axis=1, tiled=True),
    )
    seg_part = seg_all
    logsum_part = logsum_all
    delta_part = delta_all
    incoming = (piece[0], piece[1], logsum_part, delta_part, seg_part)
    query_part, gradout_part, key_logsum_part, key_delta_part, key_seg_part = incoming
    key_part = key_rows
    scores = masked_scores(query_part, key_part, key_seg_part, segment_ids)
    probs = jnp.exp(scores - jnp.transpose(key_logsum_part, (0, 2, 1))[..., None])
    grad_values = jnp.einsum(
        "shqk,sqhe->skhe",
        probs.astype(jnp.bfloat16),
        gradout_part,
        preferred_element_type=jnp.float32,
    )
    dprob = jnp.einsum("sqhe,skhe->shqk", gradout_part, values, preferred_element_type=jnp.float32)
    dscore = (probs * (dprob - jnp.transpose(key_delta_part, (0, 2, 1))[..., None])).astype(
        jnp.bfloat16
    )
    grad_keys = (
        jnp.einsum("shqk,sqhe->skhe", dscore, query_part, preferred_element_type=jnp.float32)
        * scaling
    )
    grad_keys, grad_values = (grad_keys, grad_values)
    grad_qkv = jnp.concatenate(
        [
            grad_queries.reshape(row_count, width),
            grad_keys.reshape(row_count, width),
            grad_values.reshape(row_count, width),
        ],
        axis=1,
    ).astype(jnp.bfloat16)
    grad_w_qkv = inner(normed1, grad_qkv)
    grad_normed1 = times_t(grad_qkv, w_qkv)
    norm_pull_one = jax.vjp(layer_norm, hidden0, gain_one32, shift_one32)[1]
    part_one, grad_gain_one, grad_shift_one = norm_pull_one(grad_normed1)
    grad_h0 = (grad_h1 + part_one).astype(jnp.bfloat16)
    input_grad = (
        times_t(grad_h0, w_enc).astype(jnp.bfloat16).reshape(seq_count, cell_count, gene_count)
    )
    enc_share = lax.psum_scatter(inner(express, grad_h0), "blk", scatter_dimension=0, tiled=True)
    shares = (
        lax.psum_scatter(grad_w_qkv, "blk", scatter_dimension=0, tiled=True),
        lax.psum_scatter(grad_w_out, "blk", scatter_dimension=0, tiled=True),
        lax.psum_scatter(grad_w_up, "blk", scatter_dimension=0, tiled=True),
        lax.psum_scatter(grad_w_down, "blk", scatter_dimension=0, tiled=True),
        lax.psum_scatter(grad_dec, "blk", scatter_dimension=0, tiled=True),
        lax.psum_scatter(grad_bias, "blk", scatter_dimension=0, tiled=True),
        lax.psum_scatter(grad_gain_one, "blk", scatter_dimension=0, tiled=True),
        lax.psum_scatter(grad_shift_one, "blk", scatter_dimension=0, tiled=True),
        lax.psum_scatter(grad_gain_two, "blk", scatter_dimension=0, tiled=True),
        lax.psum_scatter(grad_shift_two, "blk", scatter_dimension=0, tiled=True),
    )
    summed = (
        lax.psum(enc_share.astype(jnp.bfloat16), "dp").astype(jnp.float32),
        lax.psum(shares[0].astype(jnp.bfloat16), "dp").astype(jnp.float32),
        lax.psum(shares[1].astype(jnp.bfloat16), "dp").astype(jnp.float32),
        lax.psum(shares[2].astype(jnp.bfloat16), "dp").astype(jnp.float32),
        lax.psum(shares[3].astype(jnp.bfloat16), "dp").astype(jnp.float32),
        lax.psum(shares[4].astype(jnp.bfloat16), "dp").astype(jnp.float32),
        lax.psum(shares[5].astype(jnp.bfloat16), "dp").astype(jnp.float32),
        lax.psum(shares[6].astype(jnp.bfloat16), "dp").astype(jnp.float32),
        lax.psum(shares[7].astype(jnp.bfloat16), "dp").astype(jnp.float32),
        lax.psum(shares[8].astype(jnp.bfloat16), "dp").astype(jnp.float32),
        lax.psum(shares[9].astype(jnp.bfloat16), "dp").astype(jnp.float32),
    )
    return (
        logits.reshape(seq_count, cell_count, gene_count),
        input_grad,
        summed[0],
        summed[1],
        summed[2],
        summed[3],
        summed[4],
        summed[5],
        summed[6],
        summed[7],
        summed[8],
        summed[9],
        summed[10],
    )


AXES = ("y", "core", "z", "x")
SPLIT = 64


class Place:
    def __init__(self, sizes):
        self.sizes = sizes
        self.y, self.core, self.z, self.x = (lax.axis_index(name) for name in AXES)

    def send(self, value, move):
        ny, nc, nz, nx = self.sizes

        def flat(place):
            y, c, z, x = place
            return ((y * nc + c) * nz + z) * nx + x

        everywhere = [
            (y, c, z, x) for y in range(ny) for c in range(nc) for z in range(nz) for x in range(nx)
        ]
        return lax.ppermute(value, AXES, [(flat(p), flat(move(*p))) for p in everywhere])

    def swap_core(self, value):
        return self.send(value, lambda y, c, z, x: (y, 1 - c, z, x))

    def swap_x(self, value):
        return self.send(value, lambda y, c, z, x: (y, c, z, 1 - x))

    def swap_y(self, value):
        return self.send(value, lambda y, c, z, x: (1 - y, c, z, x))

    def shift_z(self, value, step):
        nz = self.sizes[2]
        return self.send(value, lambda y, c, z, x: (y, c, (z + step) % nz, x))

    def swap_z(self, value, distance):
        return self.send(value, lambda y, c, z, x: (y, c, z ^ distance, x))

    def exchange_z(self, value):
        return lax.all_to_all(value, "z", split_axis=0, concat_axis=0, tiled=True)

    def regroup(self, first, second):
        return (
            self.send(first, lambda y, c, z, x: (y, z // 2, 2 * c + z % 2, x)),
            self.send(second, lambda y, c, z, x: (y, z // 2, 2 * c + 1 - z % 2, x)),
        )

    def by_parity(self, pair):
        even = self.z % 2 == 0
        return jnp.where(even, pair[0], pair[1]), jnp.where(even, pair[1], pair[0])


def after(value, *earlier):
    return lax.optimization_barrier((value, *earlier))[0]


def coordinates():
    return tuple(lax.axis_index(name) for name in AXES)


def put(target, row, column, part):
    if not isinstance(row, int):
        row = pl.multiple_of(row, 16)
    if not isinstance(column, int):
        column = pl.multiple_of(column, 128)
    target[pl.ds(row, part.shape[0]), pl.ds(column, part.shape[1])] = part.astype(target.dtype)


def rows_at(source, row, count):
    return source[pl.ds(pl.multiple_of(row, 16), count), :]


def own_part(group, core, x, head):
    pair = jnp.where(x == 0, group[:, : 2 * head], group[:, 2 * head :])
    return jnp.where(core == 0, pair[:, :head], pair[:, head:])


def dot(left, right):
    return jnp.dot(left, right, preferred_element_type=jnp.float32)


def soft(queries, keys, allowed, scaling):
    scores = times_t(queries, keys) * scaling
    scores = jnp.where(allowed, scores, NEGATIVE)
    expo = jnp.exp(scores - jnp.max(scores, axis=-1, keepdims=True))
    return expo / jnp.sum(expo, axis=-1, keepdims=True)


def one_head(ref, part, heads, number, size):
    at = (part * heads + number) * size
    return ref[:, at : at + size]


def in_vmem(kernel, outs, *operands, flops=0, exps=0, scratch=()):
    whole = pl.BlockSpec(memory_space=pltpu.VMEM)
    shapes = [jax.ShapeDtypeStruct(shape, dtype) for shape, dtype in outs]
    held = sum(math.prod(v.shape) * v.dtype.itemsize for v in (*operands, *shapes))
    kept = sum(math.prod(shape) * jnp.dtype(dtype).itemsize for shape, dtype in scratch)
    results = pl.pallas_call(
        kernel,
        out_shape=shapes,
        in_specs=[whole] * len(operands),
        out_specs=[whole] * len(shapes),
        scratch_shapes=[pltpu.VMEM(shape, dtype) for shape, dtype in scratch],
        compiler_params=pltpu.CompilerParams(
            vmem_limit_bytes=(held // 2 if flops else held) + kept + (8 if flops else 4) * 1024 * 1024
        ),
        cost_estimate=pl.CostEstimate(flops=0, bytes_accessed=1024, transcendentals=0),
    )(*operands)
    return results if len(shapes) > 1 else results[0]


def sinusoids_of_whole(coords, width):
    quarter = width // 4
    frequency = jnp.exp(jnp.arange(quarter, dtype=jnp.float32) * (-math.log(10000.0) / quarter))
    number = jnp.arange(32, dtype=jnp.float32)[:, None]
    far, near = 32.0 * number * frequency, number * frequency
    far = jnp.concatenate([jnp.sin(far), jnp.cos(far)], axis=1)
    near = jnp.concatenate([jnp.sin(near), jnp.cos(near)], axis=1)
    parts = []
    for coord in coords:
        whole = coord.astype(jnp.int32)
        pick_far = (whole // 32 == jnp.arange(32)[None, :]).astype(jnp.float32)
        pick_near = (whole % 32 == jnp.arange(32)[None, :]).astype(jnp.float32)
        at_far = jnp.dot(pick_far, far, precision=lax.Precision.HIGHEST)
        at_near = jnp.dot(pick_near, near, precision=lax.Precision.HIGHEST)
        sin_far, cos_far = at_far[:, :quarter], at_far[:, quarter:]
        sin_near, cos_near = at_near[:, :quarter], at_near[:, quarter:]
        parts.append(sin_far * cos_near + cos_far * sin_near)
        parts.append(cos_far * cos_near - sin_far * sin_near)
    return jnp.concatenate(parts, axis=1)


def normalise(inputs):
    centre = inputs - jnp.mean(inputs, axis=-1, keepdims=True)
    factor = lax.rsqrt(jnp.mean(centre * centre, axis=-1, keepdims=True) + EPSILON)
    return centre * factor, factor


def normalise_back(inputs, grad, gain):
    normal, factor = normalise(inputs)
    scaled = grad * gain
    inside = (
        scaled
        - jnp.mean(scaled, axis=-1, keepdims=True)
        - normal * jnp.mean(scaled * normal, axis=-1, keepdims=True)
    )
    return (
        factor * inside,
        jnp.sum(grad * normal, axis=0, keepdims=True),
        jnp.sum(grad, axis=0, keepdims=True),
    )


def gelu_parts(value):
    root = math.sqrt(2.0 / math.pi)
    square = value * value
    bent = jnp.tanh(root * value * (1.0 + 0.044715 * square))
    slope = 0.5 * (1.0 + bent) + 0.5 * value * (1.0 - bent * bent) * root * (1.0 + 0.134145 * square)
    return 0.5 * value * (1.0 + bent), slope


def grouped_plan(
    sizes,
    counts,
    coords,
    segment_ids,
    logit_grad,
    enc_weight,
    qkv_weight,
    out_weight,
    up_weight,
    down_weight,
    dec_weight,
    dec_bias,
    norm1_gain,
    norm1_shift,
    norm2_gain,
    norm2_shift,
):
    place = Place(sizes)
    nz = sizes[2]
    seqs, cells, genes = counts.shape
    width = enc_weight.shape[1]
    block = enc_weight.shape[0]
    head = width // HEADS
    heads = HEADS // 4
    slice_width = width // 4
    own_rows = seqs * cells
    rows = 4 * own_rows
    ff = up_weight.shape[1]
    ff_slice = ff // 4
    bf16, f32 = jnp.bfloat16, jnp.float32

    half, quarter = block // 2, block // 4
    three = 3 * slice_width
    lanes = ff // (8 * nz)
    up_half = nz * lanes
    many = down_weight.shape[0] // 4
    half_rows = rows // 2
    pairs = heads * rows * rows
    square = 2 * rows * width * width // 4

    vectors = jnp.stack([dec_bias, norm1_gain, norm1_shift, norm2_gain, norm2_shift])
    tall = half + quarter + 16

    def whole_kernel(enc_ref, dec_ref, vectors_ref, out_ref):
        y, core, _, _ = coordinates()
        for k in range(nz):
            at = k * tall
            put(out_ref, at, 0, rows_at(enc_ref, core * half, half))
            put(out_ref, at + half, 0, rows_at(dec_ref, core * half + y * quarter, quarter))
            out_ref[at + half + quarter : at + tall, :] = jnp.zeros((16, width), bf16)
            out_ref[at + half + quarter : at + half + quarter + 5, :block] = vectors_ref[...]

    whole_own = in_vmem(
        whole_kernel, [((nz * tall, width), bf16)], enc_weight, dec_weight, vectors
    )
    whole_near = place.exchange_z(whole_own)

    express = jnp.log1p(counts.astype(f32)).astype(bf16)
    numbers = jnp.stack([coords[0], coords[1], segment_ids], axis=-1)
    beside = jnp.concatenate([numbers // SPLIT, numbers % SPLIT], axis=-1).astype(bf16)
    beside = jnp.pad(beside, ((0, 0), (0, 0), (0, 122)))
    pair = place.by_parity(
        jnp.concatenate([express, logit_grad, after(beside, whole_own)], axis=-1)
    )
    own_cells = place.regroup(*pair)
    def up_columns(up_ref, out_ref, first, x):
        y, core, _, _ = coordinates()
        for number in range(nz):
            at = ((2 * number + x) * 2 + core) * 2 + y
            out_ref[first : first + block, number * lanes : (number + 1) * lanes] = up_ref[
                :, pl.ds(pl.multiple_of(at * lanes, lanes), lanes)
            ]

    def qkv_columns(qkv_ref, out_ref, row, core, x, first, count):
        for at in range(3 * nz):
            columns = slice(at * 4 * head, (at + 1) * 4 * head)
            part = own_part(
                qkv_ref[pl.ds(pl.multiple_of(first, 16), count), columns], core, x, head
            )
            out_ref[row : row + count, at * head : (at + 1) * head] = part

    def theirs_kernel(qkv_ref, up_ref, out_ref):
        _, core, _, x = coordinates()
        qkv_columns(qkv_ref, out_ref, 0, core, 1 - x, 0, block)
        up_columns(up_ref, out_ref, block, 1 - x)
        out_ref[block:, up_half:] = jnp.zeros((block, three - up_half), bf16)

    theirs = in_vmem(
        theirs_kernel, [((2 * block, three), bf16)], after(qkv_weight, *pair), up_weight
    )
    theirs = place.swap_x(theirs)

    def qkv_kernel(qkv_ref, theirs_ref, out_weight_ref, own_ref, other_ref):
        y, core, _, x = coordinates()
        for out_ref, there in ((own_ref, y), (other_ref, 1 - y)):
            qkv_columns(qkv_ref, out_ref, 0, core, x, there * half, half)
            out_ref[half:, :three] = rows_at(theirs_ref, there * half, half)
            part = rows_at(out_weight_ref, core * half + there * quarter, quarter)
            for j in range(4):
                out_ref[j * quarter : (j + 1) * quarter, three:] = part[
                    :, j * slice_width : (j + 1) * slice_width
                ]

    qkv_own, qkv_own_far = in_vmem(
        qkv_kernel, [((block, width), bf16)] * 2, qkv_weight, theirs, out_weight
    )
    qkv_own = after(qkv_own, whole_near)

    def up_kernel(up_ref, theirs_ref, down_ref, out_ref):
        y, core, _, x = coordinates()
        up_columns(up_ref, out_ref, 0, x)
        out_ref[:block, up_half:] = theirs_ref[block:, :up_half]
        out_ref[block:, :] = rows_at(down_ref, (2 * core + y) * many, many)

    up_own = in_vmem(
        up_kernel, [((block + many, width), bf16)], up_weight, theirs, down_weight
    )
    up_near, up_far = [up_own], [place.swap_y(up_own)]
    for k in range(1, nz):
        up_near.append(place.shift_z(after(up_near[-1], whole_near), 1))
        if k < nz - 1:
            up_far.append(place.swap_y(up_near[-1]))
    up_far.append(place.shift_z(up_far[-1], 1))
    near = [qkv_own, place.shift_z(qkv_own, 1)]
    near += [place.shift_z(after(qkv_own, up_near[1]), k) for k in range(2, nz)]

    def two_kernel(one_ref, two_ref, out_ref):
        out_ref[:block, :] = one_ref[...]
        out_ref[block:, :] = two_ref[...]

    far_one = place.swap_y(near[1])
    far_two = place.swap_y(in_vmem(two_kernel, [((2 * block, width), bf16)], *near[2:]))
    qkv_pieces = (*near, qkv_own_far, far_one, far_two)

    whole_far = place.swap_x(whole_near)

    near_cells = jnp.concatenate(after(own_cells, near[1]), axis=0)
    near_cells = jnp.concatenate(
        [near_cells, after(
                place.swap_x(near_cells), up_far[0], *near[1:], up_near[1], whole_far,
                up_far[1], far_one,
            )], axis=0
    )
    far_cells = place.swap_core(near_cells)
    beside = jnp.concatenate([near_cells[:, 2 * genes :], far_cells[:, 2 * genes :]], axis=0).astype(f32)
    beside = beside[:, :3] * SPLIT + beside[:, 3:6]
    segment = beside[:, 2:3]
    segment_row = segment.reshape(1, rows)
    embed = sinusoids_of_whole((beside[:, 0:1], beside[:, 1:2]), width)


    def enc_half_kernel(near_ref, far_ref, out_ref, vectors_ref):
        _, _, _, x = coordinates()
        for dx, ref in enumerate((near_ref, far_ref)):
            for k in range(nz):
                at = k * tall
                put(out_ref, (2 * k + (x ^ dx)) * half, 0, ref[at : at + half, :])
                part = ref[at + half + quarter : at + tall, :block]
                put(vectors_ref, 0, (2 * k + (x ^ dx)) * block, part)

    enc_half, vectors = in_vmem(
        enc_half_kernel, [((genes // 2, width), bf16), ((16, width), f32)], whole_near, whole_far
    )
    enc_far = place.swap_core(enc_half)

    b_dec_row = vectors[0:1]

    def both_cores(near_ref, far_ref, out_ref):
        _, core, _, _ = coordinates()
        for dc, ref in enumerate((near_ref, far_ref)):
            for k in range(2 * nz):
                put(out_ref, k * block + (core ^ dc) * half, 0, ref[k * half : (k + 1) * half, :])

    def by_y(out_mine, out_send, value, first):
        y, _, _, _ = coordinates()
        for k in range(nz):
            low = value[:, 2 * k * block : (2 * k + 1) * block]
            high = value[:, (2 * k + 1) * block : (2 * k + 2) * block]
            at = slice(first, first + value.shape[0]), slice(k * block, (k + 1) * block)
            out_mine[at] = jnp.where(y == 0, low, high)
            out_send[at] = jnp.where(y == 0, high, low)

    def first_kernel(
        near_ref, far_ref, enc_near_ref, enc_far_ref, embed_ref, vectors_ref,
        enc_ref, hidden_ref, normed_ref, mine_ref, send_ref,
    ):
        both_cores(enc_near_ref, enc_far_ref, enc_ref)
        for number, ref in enumerate((near_ref, far_ref)):
            first = number * half_rows
            hidden = dot(ref[:, :genes], enc_ref[...]) + embed_ref[first : first + half_rows, :]
            if number == 0:
                hidden_ref[...] = hidden
            normal, _ = normalise(hidden)
            normed = (normal * vectors_ref[1:2, :] + vectors_ref[2:3, :]).astype(bf16)
            normed_ref[first : first + half_rows, :] = normed
            by_y(mine_ref, send_ref, normed, first)

    square_bf16, half_bf16 = ((width, width), bf16), ((half_rows, width), bf16)
    half_f32 = ((half_rows, width), f32)
    columns_bf16 = ((rows, width // 2), bf16)
    w_enc, hidden0, normed1, normed1_mine, normed1_send = in_vmem(
        first_kernel, [square_bf16, half_f32, ((rows, width), bf16), columns_bf16, columns_bf16],
        near_cells, far_cells, enc_half, enc_far, embed, vectors, flops=4 * square,
    )

    def attend_kernel(normed_ref, *refs):
        pieces, refs = refs[: nz + 3], refs[nz + 3 :]
        column_ref, row_ref, w_ref, w_out_ref, qkv_ref, out_ref, own_ref, send_ref = refs
        y, _, z, x = coordinates()
        parts = [(0, k, pieces[k], 0) for k in range(nz)]
        parts += [(1, k, pieces[nz + min(k, 2)], max(k - 2, 0) * block) for k in range(nz)]
        for dy, k, ref, first in parts:
            there = (z - k) % nz
            for dx in range(2):
                row = (2 * there + (x ^ dx)) * block + (y ^ dy) * half
                put(w_ref, row, 0, ref[first + dx * half : first + (dx + 1) * half, :three])
            for j in range(4):
                row = there * half + (y ^ dy) * quarter
                part = ref[first + j * quarter : first + (j + 1) * quarter, three:]
                put(w_out_ref, row, j * slice_width, part)
        qkv_ref[...] = dot(normed_ref[...], w_ref[...]).astype(bf16)
        allowed = column_ref[...] == row_ref[...]
        for number in range(heads):
            queries, keys, values = (one_head(qkv_ref, i, heads, number, head) for i in range(3))
            probs = soft(queries, keys, allowed, head**-0.5)
            at = slice(number * head, (number + 1) * head)
            out_ref[:, at] = dot(probs.astype(bf16), values).astype(bf16)
        own_ref[...] = dot(out_ref[:half_rows, :], w_out_ref[...])
        send_ref[...] = dot(out_ref[half_rows:, :], w_out_ref[...]).astype(bf16)

    w_qkv, w_out, qkv, context, own, send = in_vmem(
        attend_kernel,
        [((width, three), bf16), ((slice_width, width), bf16), ((rows, three), bf16),
         ((rows, slice_width), bf16), half_f32, half_bf16],
        after(normed1, up_near[2]), *qkv_pieces, segment, segment_row,
        flops=4 * square + 4 * pairs * head, exps=pairs,
    )

    def add_kernel(own_ref, other_ref, out_ref):
        out_ref[...] = (own_ref[...].astype(f32) + other_ref[...].astype(f32)).astype(out_ref.dtype)

    def add(own, other, dtype=bf16):
        return in_vmem(add_kernel, [(own.shape, dtype)], own, other)

    def sum_x(mine_ref, other_ref):
        other = jnp.concatenate([other_ref[own_rows:, :], other_ref[:own_rows, :]], axis=0)
        return mine_ref[...].astype(f32) + other.astype(f32)

    mine = add(own, after(place.swap_core(send), up_near[3], up_far[2]))

    def second_kernel(hidden_ref, mine_ref, other_ref, vectors_ref, out_ref, normed_ref):
        hidden = hidden_ref[...] + sum_x(mine_ref, other_ref)
        out_ref[...] = hidden
        normal, _ = normalise(hidden)
        normed_ref[...] = (normal * vectors_ref[3:4, :] + vectors_ref[4:5, :]).astype(bf16)

    hidden1, normed2 = in_vmem(
        second_kernel, [half_f32, half_bf16],
        hidden0, mine, after(place.swap_x(mine), up_far[3]), vectors,
    )
    normed2_far = place.swap_core(normed2)

    def dec_rows_kernel(near_ref, far_ref, out_ref):
        for dx, ref in enumerate((near_ref, far_ref)):
            for k in range(nz):
                at, out = k * tall + half, (dx * nz + k) * quarter
                out_ref[out : out + quarter, :] = ref[at : at + quarter, :]

    dec_near = in_vmem(
        dec_rows_kernel, [((2 * nz * quarter, genes), bf16)], whole_near, after(whole_far, qkv)
    )

    def dec_half_kernel(near_ref, far_ref, out_ref):
        y, _, _, x = coordinates()
        for dy, ref in enumerate((near_ref, far_ref)):
            for dx in range(2):
                for k in range(nz):
                    at = (dx * nz + k) * quarter
                    row = (2 * k + (x ^ dx)) * half + (y ^ dy) * quarter
                    put(out_ref, row, 0, ref[at : at + quarter, :])

    dec_half = in_vmem(
        dec_half_kernel, [((width // 2, genes), bf16)],
        dec_near, after(place.swap_y(dec_near), mine),
    )
    dec_far = place.swap_core(dec_half)

    def decoder_kernel(near_ref, far_ref, dec_near_ref, dec_far_ref, dec_ref, grad_ref, low_ref, sums_ref):
        both_cores(dec_near_ref, dec_far_ref, dec_ref)
        grad = times_t(near_ref[:, genes : 2 * genes], dec_ref[...])
        grad_ref[...] = grad
        low_ref[:half_rows, :] = grad.astype(bf16)
        low_ref[half_rows:, :] = times_t(far_ref[:, genes : 2 * genes], dec_ref[...]).astype(bf16)
        sums_ref[...] = sum(
            jnp.sum(ref[:, genes : 2 * genes].astype(f32), axis=0, keepdims=True)
            for ref in (near_ref, far_ref)
        )

    w_dec, grad_h2, grad_down, bias_sums = in_vmem(
        decoder_kernel,
        [square_bf16, half_f32, ((rows, width), bf16), ((1, width), f32)],
        near_cells, far_cells, dec_half, dec_far, flops=4 * square,
    )

    def feed_kernel(normed_ref, normed_far_ref, grad_ref, *refs):
        pieces, refs = refs[: 2 * nz], refs[2 * nz :]
        active_ref, grad_up_ref, own_ref, send_ref, own2_ref, send2_ref, mine_ref, theirs_ref = refs[:8]
        w_up_ref, w_down_ref, normed_all, back, ahead = refs[8:]
        y, _, z, x = coordinates()
        for dy in range(2):
            for k in range(nz):
                ref = pieces[dy * nz + k]
                there = (z - k) % nz
                for dx in range(2):
                    for number in range(nz):
                        at = dx * up_half + number * lanes
                        column = (2 * number + (y ^ dy)) * lanes
                        put(w_up_ref, (2 * there + (x ^ dx)) * block, column, ref[:block, at : at + lanes])
                put(w_down_ref, (2 * there + (y ^ dy)) * many, 0, ref[block:, :])
        normed_all[:half_rows, :] = normed_ref[...]
        normed_all[half_rows:, :] = normed_far_ref[...]
        by_y(mine_ref, theirs_ref, normed_ref[...], 0)
        by_y(mine_ref, theirs_ref, normed_far_ref[...], half_rows)
        chunk = 2 * lanes
        for number in range(nz):
            at = slice(number * chunk, (number + 1) * chunk)
            active, slope = gelu_parts(dot(normed_all[...], w_up_ref[:, at]))
            active = active.astype(bf16)
            active_ref[:, at] = active
            grad_up = (times_t(grad_ref[...], w_down_ref[at, :]) * slope).astype(bf16)
            grad_up_ref[:, at] = grad_up
            part, part2 = times_t(grad_up, w_up_ref[:, at]), dot(active, w_down_ref[at, :])
            back[...] = part if number == 0 else back[...] + part
            ahead[...] = part2 if number == 0 else ahead[...] + part2
        for sums, one, two in ((back, own_ref, send_ref), (ahead, own2_ref, send2_ref)):
            one[...] = sums[:half_rows, :]
            two[...] = sums[half_rows:, :].astype(bf16)

    full_bf16, full_f32 = ((rows, width), bf16), ((rows, width), f32)
    active, grad_up, own, send, own2, send2, normed2_mine, normed2_send = in_vmem(
        feed_kernel,
        [full_bf16, full_bf16, half_f32, half_bf16, half_f32, half_bf16, columns_bf16, columns_bf16],
        normed2, normed2_far, grad_down, *up_near, *up_far,
        flops=16 * square, exps=rows * ff_slice,
        scratch=[square_bf16, square_bf16, full_bf16, full_f32, full_f32],
    )
    mine = add(own, place.swap_core(send))

    def down_halve_kernel(value_ref, *refs):
        _, _, z, _ = coordinates()
        for number in range(2):
            for ref, low in ((refs[2 * number], z % 2), (refs[2 * number + 1], 1 - z % 2)):
                for high in range(2):
                    part = rows_at(value_ref, ((2 * high + low) * 2 + number) * many, many)
                    ref[high * many : (high + 1) * many, :] = part

    def sum_halve_kernel(*refs):
        parts, (out_ref, send_ref, all_ref) = refs[:-3], refs[-3:]
        at = 0
        for ref in parts[1:]:
            rows_here = slice(at, at + ref.shape[0])
            all_ref[rows_here, :] = parts[0][rows_here, :].astype(f32) + ref[...].astype(f32)
            at += ref.shape[0]
        _, _, z, _ = coordinates()
        count = out_ref.shape[0] // 2
        for high in range(2):
            at = slice(high * count, (high + 1) * count)
            out_ref[at, :] = rows_at(all_ref, (2 * high + z % 2) * count, count).astype(bf16)
            send_ref[at, :] = rows_at(all_ref, (2 * high + 1 - z % 2) * count, count).astype(bf16)

    def sum_halve(own, *others):
        shape = ((own.shape[0] // 2, own.shape[1]), bf16)
        return in_vmem(
            sum_halve_kernel, [shape, shape], own, *others, scratch=[(own.shape, f32)]
        )

    def add_split_kernel(own_ref, other_ref, out_ref, send_ref):
        _, _, z, _ = coordinates()
        count = out_ref.shape[0]
        for ref, part in ((out_ref, z // 2), (send_ref, 1 - z // 2)):
            own, other = (rows_at(r, part * count, count).astype(f32) for r in (own_ref, other_ref))
            ref[...] = (own + other).astype(bf16)

    def add_halve(own, other):
        shape = ((own.shape[0] // 2, own.shape[1]), bf16)
        return in_vmem(add_split_kernel, [shape, shape], own, other)

    down_one = in_vmem(
        down_halve_kernel, [((2 * many, width), bf16)] * 4, inner(active, grad_down).astype(bf16)
    )
    down_one = [down_one[:2], down_one[2:]]
    down_other = place.swap_z(down_one[0][1], 1)
    up_mine = inner(after(normed2_mine, mine), grad_up).astype(bf16)
    up_send = inner(after(normed2_send, mine), grad_up).astype(bf16)
    low_rows = nz * block // 2
    up_other_low = place.swap_y(up_send[:low_rows])
    ahead = add(own2, after(place.swap_core(send2), mine))
    other = after(place.swap_x(mine), up_mine, up_send, ahead, up_other_low, down_other)
    up_other_high = place.swap_y(after(up_send[low_rows:], other))
    down_two = [add_halve(down_one[0][0], after(down_other, other))]
    down_two_other = place.swap_z(down_two[0][1], 2)
    down_other = place.swap_z(after(down_one[1][1], other), 1)

    def back_kernel(hidden_ref, mine_ref, other_ref, grad_ref, vectors_ref, out_ref, low_ref, row):
        inside, gain_sums, shift_sums = normalise_back(
            hidden_ref[...], sum_x(mine_ref, other_ref), vectors_ref[row : row + 1, :]
        )
        grad = grad_ref[...] + inside
        if out_ref is not None:
            out_ref[...] = grad
        low_ref[:half_rows, :] = grad.astype(bf16)
        low_ref[half_rows:, :] = jnp.zeros((16, width), bf16)
        low_ref[half_rows : half_rows + 1, :] = gain_sums.astype(bf16)
        low_ref[half_rows + 1 : half_rows + 2, :] = shift_sums.astype(bf16)

    def second_back_kernel(*refs):
        back_kernel(*refs, 3)

    def first_back_kernel(*refs):
        back_kernel(*refs[:5], None, refs[5], 1)

    message = ((half_rows + 16, width), bf16)
    grad_h1, near_two = in_vmem(
        second_back_kernel, [half_f32, message], hidden1, mine, other, grad_h2, vectors
    )
    far_two = place.swap_core(near_two)
    ahead_other = place.swap_x(after(ahead, other))

    def attend_back_kernel(
        near_ref, far_ref, w_out_ref, qkv_ref, column_ref, row_ref, w_ref,
        out_ref, own_ref, send_ref, all_ref, grad_ref,
    ):
        all_ref[:half_rows, :] = near_ref[:half_rows, :]
        all_ref[half_rows:, :] = far_ref[:half_rows, :]
        grad_ref[...] = times_t(all_ref[...], w_out_ref[...]).astype(bf16)
        allowed = column_ref[...] == row_ref[...]
        scaling = head**-0.5
        for number in range(heads):
            queries, keys, values = (one_head(qkv_ref, i, heads, number, head) for i in range(3))
            grad = one_head(grad_ref, 0, heads, number, head)
            probs = soft(queries, keys, allowed, scaling)
            weighted = probs * times_t(grad, values)
            delta = jnp.sum(weighted, axis=-1, keepdims=True)
            dscore = (weighted - probs * delta).astype(bf16)
            parts = (
                dot(dscore, keys) * scaling,
                inner(dscore, queries) * scaling,
                inner(probs.astype(bf16), grad),
            )
            for i, part in enumerate(parts):
                at = (i * heads + number) * head
                out_ref[:, at : at + head] = part.astype(bf16)
        own_ref[...] = times_t(out_ref[:half_rows, :], w_ref[...])
        send_ref[...] = times_t(out_ref[half_rows:, :], w_ref[...]).astype(bf16)

    grad_qkv, own, send, grad_attn = in_vmem(
        attend_back_kernel, [((rows, three), bf16), half_f32, half_bf16, full_bf16],
        near_two, far_two, w_out, qkv, segment, segment_row, w_qkv,
        flops=4 * square + 10 * pairs * head, exps=pairs,
        scratch=[((rows, slice_width), bf16)],
    )
    qkv_send = inner(normed1_send, grad_qkv).astype(bf16)
    qkv_other = place.swap_y(qkv_send)
    up_other_high, down_other, down_two_other, ahead_other = after(
        (up_other_high, down_other, down_two_other, ahead_other), grad_qkv
    )
    mine = add(
        own, after(place.swap_core(send), qkv_send, up_other_high, down_other, down_two_other, ahead_other)
    )
    up_one = sum_halve(up_mine, up_other_low, after(up_other_high, mine))
    down_two.append(add_halve(down_one[1][0], after(down_other, mine)))
    down_sum = [add(down_two[0][0], after(down_two_other, mine))]
    other = place.swap_x(mine)
    down_two_other = place.swap_z(down_two[1][1], 2)
    up_one_other = place.swap_z(up_one[1], 1)

    qkv_mine = inner(normed1_mine, grad_qkv).astype(bf16)
    grad_w_out = inner(context, grad_attn).astype(bf16)

    other = after(other, qkv_mine, down_two_other)
    qkv_one = sum_halve(qkv_mine, qkv_other)
    qkv_one_other = place.swap_z(qkv_one[1], 1)
    up_two = add_halve(up_one[0], after(up_one_other, other))
    up_two_other = place.swap_z(up_two[1], 2)
    near_one = in_vmem(first_back_kernel, [message], hidden0, mine, other, grad_h1, vectors)
    far_one = place.swap_core(near_one)

    def hidden_kernel(hidden_ref, mine_ref, other_ref, low_ref, own_ref, send_ref):
        _, core, _, x = coordinates()
        hidden = (hidden_ref[...] + sum_x(mine_ref, other_ref)).astype(bf16)
        low_ref[...] = hidden[:own_rows, :]
        for k in range(nz):
            group = hidden[:, 2 * k * block : (2 * k + 2) * block]
            at = slice(k * half, (k + 1) * half)
            own_ref[:, at] = own_part(group, core, x, half)
            send_ref[:, at] = own_part(group, 1 - core, x, half)

    part_bf16 = ((half_rows, slice_width), bf16)
    hidden2, hidden2_own, hidden2_send = in_vmem(
        hidden_kernel, [((own_rows, width), bf16), part_bf16, part_bf16],
        hidden1, ahead, after(ahead_other, near_one),
    )
    hidden2_far = place.swap_core(hidden2_send)

    def few_rows_kernel(own_ref, far_ref, near_cells_ref, far_cells_ref, out_grad_ref, mine_ref, send_ref):
        y, _, _, _ = coordinates()
        columns = slice(genes, 2 * genes)
        grad = inner(own_ref[...], near_cells_ref[:, columns])
        grad = (grad + inner(far_ref[...], far_cells_ref[:, columns])).astype(bf16)
        mine_ref[...] = jnp.where(y == 0, out_grad_ref[...], grad)
        send_ref[...] = jnp.where(y == 0, grad, out_grad_ref[...])

    few_shape = ((slice_width, genes), bf16)
    few_mine, few_send = in_vmem(
        few_rows_kernel, [few_shape, few_shape],
        hidden2_own, hidden2_far, near_cells, far_cells, grad_w_out, flops=square,
    )
    few_other = place.swap_y(few_send)
    logits = (dot(hidden2, w_dec) + b_dec_row).astype(bf16)
    one, two = logits[:cells], logits[cells:]

    input_grad = times_t(near_one[:own_rows], w_enc).astype(bf16)

    tall_last = 2 * half + 16

    def last_kernel(
        near_ref, far_ref, one_ref, one_far_ref, two_ref, two_far_ref, bias_ref, few_ref, few_other_ref, *refs
    ):
        own_ref, send_ref, slice_ref, grad_ref, sums_ref = refs
        _, core, z, x = coordinates()
        for number, ref in enumerate((near_ref, far_ref)):
            for k in range(nz):
                group = ref[:, 2 * k * block : (2 * k + 2) * block]
                slice_ref[
                    number * half_rows : (number + 1) * half_rows, k * half : (k + 1) * half
                ] = own_part(group, core, x, half)
        grad_ref[...] = inner(slice_ref[:half_rows, :], one_ref[:half_rows, :]) + inner(
            slice_ref[half_rows:, :], one_far_ref[:half_rows, :]
        )
        sums_ref[...] = jnp.zeros((8, width), f32)
        sums_ref[0:1, :] = bias_ref[...]
        at = slice(half_rows, half_rows + 2)
        sums_ref[1:3, :] = one_ref[at, :].astype(f32) + one_far_ref[at, :].astype(f32)
        sums_ref[3:5, :] = two_ref[at, :].astype(f32) + two_far_ref[at, :].astype(f32)
        for ref, low in ((own_ref, z % 2), (send_ref, 1 - z % 2)):
            ref[...] = jnp.zeros(ref.shape, bf16)
            for high in range(2):
                there, first = 2 * high + low, high * tall_last
                ref[first : first + half, :] = rows_at(grad_ref, there * half, half).astype(bf16)
                column = pl.multiple_of((2 * there + x) * block, block)
                part = sums_ref[:, pl.ds(column, block)].astype(bf16)
                ref[first + half : first + half + 8, :block] = part
                few = [rows_at(r, there * half, half).astype(f32) for r in (few_ref, few_other_ref)]
                ref[first + half + 16 : first + tall_last, :] = (few[0] + few[1]).astype(bf16)

    last_one = in_vmem(
        last_kernel, [((2 * tall_last, width), bf16)] * 2,
        near_cells, far_cells, near_one, after(far_one, qkv_one_other, up_two_other),
        near_two, far_two, bias_sums, few_mine, few_other, flops=square,
        scratch=[((rows, slice_width), bf16), ((slice_width, width), f32), ((8, width), f32)],
    )
    last_one_other = place.swap_z(last_one[1], 1)
    qkv_two = add_halve(qkv_one[0], after(qkv_one_other, last_one[1]))
    qkv_two_other = place.swap_z(qkv_two[1], 2)

    def feed_sum_kernel(down_ref, one_ref, one_other_ref, two_ref, two_other_ref, out_ref):
        out_ref[:many, :] = down_ref[...]
        for row, ref, other_ref in ((many, one_ref, one_other_ref), (2 * many, two_ref, two_other_ref)):
            total = ref[...].astype(f32) + other_ref[...].astype(f32)
            out_ref[row : row + ref.shape[0], :] = total.astype(bf16)

    feed_sum = in_vmem(
        feed_sum_kernel, [((2 * many + block, width), bf16)],
        down_sum[0], down_two[1][0], down_two_other, up_two[0], after(up_two_other, last_one[1]),
    )
    feed_other = place.swap_y(feed_sum)

    def by_x_kernel(own_ref, other_ref, mine_ref, send_ref):
        y, _, _, x = coordinates()
        at = slice(0, mine_ref.shape[0]), slice(0, mine_ref.shape[1])
        mine_ref[...] = jnp.where(y == x, own_ref[at], other_ref[at])
        send_ref[...] = jnp.where(y == x, other_ref[at], own_ref[at])

    def by_x(own, other, width):
        return in_vmem(by_x_kernel, [((block, width), bf16)] * 2, own, other)

    last_two = add_halve(last_one[0], after(last_one_other, feed_other, qkv_two_other))
    last_two_other = place.swap_z(last_two[1], 2)
    qkv_sum = add(
        qkv_two[0], after(qkv_two_other, last_two[1])
    )

    def feed_split_kernel(own_ref, other_ref, down_ref, mine_ref, send_ref):
        y, _, _, x = coordinates()
        total = own_ref[: 2 * many, :].astype(f32) + other_ref[: 2 * many, :].astype(f32)
        down_ref[...] = total.astype(bf16)
        own, other = own_ref[2 * many :, :], other_ref[2 * many :, :]
        mine_ref[...] = jnp.where(y == x, own, other)
        send_ref[...] = jnp.where(y == x, other, own)

    block_bf16 = ((block, width), bf16)
    down_sum, up_mine, up_send = in_vmem(
        feed_split_kernel, [((2 * many, width), bf16), block_bf16, block_bf16],
        feed_sum, after(feed_other, last_two[1]),
    )
    qkv_other = place.swap_y(qkv_sum)
    up_there = place.swap_x(up_send)
    down_far = place.swap_core(down_sum)
    def halves_kernel(near_ref, far_ref, out_ref):
        _, core, _, _ = coordinates()
        count = near_ref.shape[0]
        for dc, ref in enumerate((near_ref, far_ref)):
            put(out_ref, (core ^ dc) * count, 0, ref[...])

    def halves(near, far):
        return in_vmem(
            halves_kernel, [((2 * near.shape[0], near.shape[1]), f32)], near, far
        )


    def up_out_kernel(near_ref, far_ref, out_ref):
        _, core, _, x = coordinates()
        for dc, ref in enumerate((near_ref, far_ref)):
            for dx in range(2):
                for k in range(nz):
                    part = ref[dx * block : (dx + 1) * block, 2 * k * lanes : 2 * (k + 1) * lanes]
                    put(out_ref, 0, ((2 * k + (x ^ dx)) * 2 + (core ^ dc)) * 2 * lanes, part)

    qkv_other, last_two_other, one, two, up_there, down_far = lax.optimization_barrier(
        (qkv_other, last_two_other, one, two, up_there, down_far)
    )
    up_both = jnp.concatenate([up_mine, up_there], axis=0)
    out_down = halves(down_sum, down_far)
    out_up = in_vmem(
        up_out_kernel, [((block, ff), f32)], up_both, place.swap_core(up_both)
    )
    last = add(last_two[0], last_two_other)
    last_other = place.swap_y(last)

    def last_add_kernel(one_ref, other_ref, out_ref, sums_ref):
        y, _, _, _ = coordinates()
        total = one_ref[: half + 16, :].astype(f32) + other_ref[: half + 16, :].astype(f32)
        out_ref[:half, :] = total[:half, :].astype(bf16)
        sums_ref[...] = total[half : half + 8, :block]
        own, other = one_ref[half + 16 :, :], other_ref[half + 16 :, :]
        out_ref[half : 2 * half, :] = jnp.where(y == 0, own, other)
        out_ref[2 * half :, :] = jnp.where(y == 0, other, own)

    last, sums = in_vmem(
        last_add_kernel, [((3 * half, width), bf16), ((8, block), f32)], last, last_other
    )

    def last_out_kernel(near_ref, far_ref, *out_refs):
        _, core, _, _ = coordinates()
        for dc, ref in enumerate((near_ref, far_ref)):
            for part, out_ref in enumerate(out_refs):
                put(out_ref, (core ^ dc) * half, 0, ref[part * half : (part + 1) * half, :])

    out_enc, out_out, out_dec = in_vmem(
        last_out_kernel, [((block, width), f32)] * 3, last, place.swap_core(last)
    )

    qkv_mine, qkv_send = by_x(qkv_sum, qkv_other, three)
    qkv_there = place.swap_x(qkv_send)
    qkv_both = jnp.concatenate([qkv_mine, qkv_there], axis=0)
    pair = place.regroup(
        *(
            jnp.concatenate(
                [part, after(input_grad[i * cells : (i + 1) * cells], qkv_other)], axis=1
            )
            for i, part in enumerate((one, two))
        )
    )

    def results_kernel(one_ref, two_ref, logits_ref, grad_ref):
        _, _, z, _ = coordinates()
        one, two = one_ref[...], two_ref[...]
        for number, part in enumerate(
            (jnp.where(z % 2 == 0, one, two), jnp.where(z % 2 == 0, two, one))
        ):
            at = slice(number * cells, (number + 1) * cells)
            logits_ref[at, :], grad_ref[at, :] = part[:, :genes], part[:, genes:]

    results = in_vmem(results_kernel, [((own_rows, genes), bf16)] * 2, *pair)
    logits, input_grad = (result.reshape(seqs, cells, genes) for result in results)

    def qkv_out_kernel(near_ref, far_ref, out_ref):
        _, core, _, x = coordinates()
        for dx in range(2):
            for number in range(3 * nz):
                at = slice(dx * block, (dx + 1) * block), slice(number * head, (number + 1) * head)
                near_part, far_part = near_ref[at].astype(f32), far_ref[at].astype(f32)
                low = jnp.where(core == 0, near_part, far_part)
                high = jnp.where(core == 0, far_part, near_part)
                put(
                    out_ref, 0, number * 4 * head + (x ^ dx) * 2 * head,
                    jnp.concatenate([low, high], axis=1),
                )

    out_qkv = in_vmem(
        qkv_out_kernel, [((block, 3 * width), f32)], qkv_both, place.swap_core(qkv_both)
    )
    return (
        logits, input_grad, out_enc, out_qkv, out_out, out_up, out_down, out_dec,
        sums[0], sums[1], sums[2], sums[3], sums[4],
    )


IN_SPECS = (
    ("dp", "blk", None), (None, "dp", "blk"), ("dp", "blk"), ("dp", "blk", None),
    *[("blk", None)] * 6, *[("blk",)] * 5,
)
OUT_SPECS = (("dp", "blk", None), ("dp", "blk", None), *[("blk", None)] * 6, *[("blk",)] * 5)


def solution(mesh):
    groups, blocks = mesh.shape["dp"], mesh.shape["blk"]

    def run(*args):
        seqs = args[0].shape[0] // groups
        if groups == 4 and blocks == 4 * seqs and seqs == 2 and HEADS == 4 * (blocks // 2):
            sizes = (groups // 2, 2, blocks // 2, 2)
            fine = Mesh(mesh.devices.reshape(sizes), AXES)
            names = {"dp": ("y", "core"), "blk": ("z", "x"), None: None}
            plan = functools.partial(grouped_plan, sizes)
        else:
            fine, names, plan = mesh, {"dp": "dp", "blk": "blk", None: None}, spread_plan
        specs = lambda entries: tuple(P(*[names[axis] for axis in entry]) for entry in entries)
        return jax.shard_map(
            plan, mesh=fine, in_specs=specs(IN_SPECS), out_specs=specs(OUT_SPECS), check_vma=False
        )(*args)

    return run
```
